256 devices in a mesh: gx: 8 (over x, core), gy: 32 (over y, z).
Axes of the slice: x: 4, y: 4, z: 8, core: 2. Of those that a mesh axis runs over, the one named last changes fastest.
Arguments:
- air_now: float32 [128, 1024, 512], P('gx', 'gy'), may hold values from -6 to 6
- air_prev: float32 [128, 1024, 512], P('gx', 'gy'), may hold values from -6 to 6
- membrane_now: float32 [128, 1024], P('gx', 'gy'), may hold values from -5.3 to 5.3
- membrane_prev: float32 [128, 1024], P('gx', 'gy'), may hold values from -5.3 to 5.3
- inv_mass: float32 [128, 1024], P('gx', 'gy'), may hold values from 0.5 to 2
- air_row: int32 [1024], replicated, may hold values from 720 to 975, as said below
Outputs:
- air_next: float32 [128, 1024, 512], P('gx', 'gy')
- air_last: float32 [128, 1024, 512], P('gx', 'gy')
- membrane_next: float32 [128, 1024], P('gx', 'gy')
- membrane_last: float32 [128, 1024], P('gx', 'gy')
The draws below stay inside these ranges and needn't reach their ends.
Inputs may be any that keep to these rules, and one draw needn't show every extreme that they name: `air_row`: nondecreasing over the membrane's columns and rising by 0 or 1 from one column to the next, so every air y row from 720 to 975 lies under some column.
All inputs are finite; a program needn't handle non-finite values.
Results may differ from the reference program's by a relative error of at most 0.0003.
Values sent between devices are 32-bit elements; how exact they have to be, the bound alone decides.
No kernel may reach another device: no remote copies, remote signals or barrier semaphores. Data moves between devices by JAX's collectives and lax.ppermute only.
A program may use at most 128 MiB of HBM per device.

```python
import math
import jax
import jax.numpy as jnp

NZ = 512
STEPS = 4
NX = 128
NY = 1024
MX = 128
MY = 1024
FOOT = 256
Y_START = 720


def membrane_scale(tilt):
    row_ratio = jnp.arange(MX, dtype=jnp.float32) / MX
    col_ratio = jnp.arange(MY, dtype=jnp.float32) / MY
    rising = 0.5 * (row_ratio[:, None] + col_ratio[None, :])
    return 0.15 * jnp.power(10.0, rising) * jnp.power(2.0, tilt * col_ratio[None, :])


def membrane_noise(key):
    noise = jax.random.truncated_normal(key, -3.0, 3.0, (MX, MY), jnp.float32)
    return noise * membrane_scale(0.0)


def draw_membrane_now(key, part):
    key = jax.random.fold_in(key, 11)
    return membrane_noise(key)


def draw_membrane_prev(key, part):
    key = jax.random.fold_in(key, 23)
    return membrane_noise(key)


def draw_air_row(key, part):
    key = jax.random.fold_in(key, 7)
    strata = jnp.arange(FOOT, dtype=jnp.int32)
    bounds = 1 + strata * (MY - 1) // (FOOT - 1)
    starts = bounds[:-1]
    spans = bounds[1:] - bounds[:-1]
    offsets = jax.random.randint(key, (FOOT - 1,), 0, spans)
    marker = jnp.zeros((MY,), jnp.int32).at[starts + offsets].set(1)
    return (Y_START + jnp.cumsum(marker)).astype(jnp.int32)


def shard_levels(key, extent, split, least, top_value):
    def one(axis_at, parts):
        heights = jax.random.uniform(jax.random.fold_in(jax.random.fold_in(key, 6), axis_at), (parts,), jnp.float32, least / len(split), top_value / len(split))
        return jnp.repeat(jnp.exp(heights), extent[axis_at] // parts).reshape((-1,) + (1,) * (len(extent) - axis_at - 1))

    level = one(*split[0])
    for cut in split[1:]:
        level = level * one(*cut)
    return level


def gaussian(own_key, dims, width, bound, split=(), kind=jnp.bfloat16):
    loudness = shard_levels(own_key, dims, split, -0.22, 0.18) if split else 1.0
    values = jax.random.normal(own_key, dims, jnp.float32) * width * loudness
    return jnp.minimum(jnp.maximum(values, -bound), bound).astype(kind)


def setup_inputs(seed: int = 0) -> dict:
    streams_of = jax.random.split(jax.random.key(seed), 7)
    return {
        "air_now": gaussian(streams_of[0], (NX, NY, NZ), 1.0, 6.0, ((0, 8), (1, 32)), jnp.float32),
        "air_prev": gaussian(streams_of[1], (NX, NY, NZ), 1.0, 6.0, ((0, 8), (1, 32)), jnp.float32),
        "membrane_now": draw_membrane_now(jax.random.fold_in(streams_of[6], 71), 0),
        "membrane_prev": draw_membrane_prev(jax.random.fold_in(streams_of[6], 71), 0),
        "inv_mass": jnp.clip(jnp.exp(math.log(2.0) - 1.3862944 * jax.random.uniform(streams_of[4], (MX, MY), jnp.float32) ** shard_levels(streams_of[4], (MX, MY), ((0, 8), (1, 32)), -0.2, 0.2)), 0.5, 2.0),
        "air_row": draw_air_row(jax.random.fold_in(streams_of[6], 71), 0),
    }


courant_square = 0.32
membrane_speed = 0.08
berger_gain = 0.4
force_gain = 0.1
source_gain = 0.5


def plane_laplacian(field):
    padded = jnp.pad(field, 1)
    return padded[2:, 1:-1] + padded[:-2, 1:-1] + padded[1:-1, 2:] + padded[1:-1, :-2] - 4.0 * field


def air_laplacian(field):
    padded = jnp.pad(field, 1)
    beside = padded[2:, 1:-1, 1:-1] + padded[:-2, 1:-1, 1:-1]
    beside = beside + padded[1:-1, 2:, 1:-1] + padded[1:-1, :-2, 1:-1]
    beside = beside + padded[1:-1, 1:-1, 2:] + padded[1:-1, 1:-1, :-2]
    return beside - 6.0 * field


def reference(air_now, air_prev, membrane_now, membrane_prev, inv_mass, air_row):
    middle = NZ // 2
    pressure, pressure_old = air_now, air_prev
    shape_now, shape_old = membrane_now, membrane_prev
    for moment in range(STEPS):
        curvature = plane_laplacian(shape_now)
        energy = -jnp.sum(shape_now * curvature)
        tension = 1.0 + berger_gain * energy / (MX * MY)
        forcing = pressure[:, air_row, middle - 1] - pressure[:, air_row, middle]
        acceleration = inv_mass * (membrane_speed * tension * curvature + force_gain * forcing)
        shape_next = 2.0 * shape_now - shape_old + acceleration
        source = jax.ops.segment_sum(acceleration.T, air_row, num_segments=NY).T
        air_step = 2.0 * pressure - pressure_old + courant_square * air_laplacian(pressure)
        air_step = air_step.at[:, :, middle].add(source_gain * source)
        air_step = air_step.at[:, :, middle - 1].add(-source_gain * source)
        pressure_old, pressure = pressure, air_step
        shape_old, shape_now = shape_now, shape_next
    return pressure, pressure_old, shape_now, shape_old
```

```python
import functools

import jax
import jax.numpy as jnp
from jax import lax
from jax.experimental import pallas as pl
from jax.experimental.pallas import tpu as pltpu
from jax.sharding import PartitionSpec as P

COURANT = 0.32
SPEED = 0.08
BERGER = 0.4
FORCE = 0.1
SOURCE = 0.5

GX, GY = 8, 32
BX, BY, NZ = 16, 32, 512
MID = NZ // 2
COLS = GY * BY
NODES = GX * BX * COLS
HALO = 4
XE = BX + 2 * HALO
YE = BY + 16
WINDOW = 384
ROW0 = COLS - WINDOW
FIRST, LAST = 22, 30
PACK = 160
FOLD = 40

VMEM = pltpu.VMEM
WHOLE = pl.BlockSpec(memory_space=pltpu.VMEM)
ANY = pl.BlockSpec(memory_space=pl.ANY)
PARAMS = pltpu.CompilerParams(vmem_limit_bytes=40 * 1024 * 1024)


def f32(*shape):
    return jax.ShapeDtypeStruct(shape, jnp.float32)


def lanes(shape):
    return lax.broadcasted_iota(jnp.int32, shape, len(shape) - 1)


def sublanes(shape):
    return lax.broadcasted_iota(jnp.int32, shape, len(shape) - 2)


def pack_x_kernel(p, q, u, w, m, low, high, sems):
    copies = [
        pltpu.make_async_copy(p.at[0:4], low.at[0:4], sems.at[0]),
        pltpu.make_async_copy(q.at[0:3], low.at[4:7], sems.at[1]),
        pltpu.make_async_copy(p.at[12:16], high.at[0:4], sems.at[2]),
        pltpu.make_async_copy(q.at[13:16], high.at[4:7], sems.at[3]),
    ]
    for copy in copies:
        copy.start()
    for out, at in ((low, 0), (high, 12)):
        for i, field in enumerate((u, w, m)):
            out[7, 8 * i : 8 * i + 4, 0:BY] = field[at : at + 4, :]
    for copy in copies:
        copy.wait()


def pack_y_kernel(p, q, xlow, xhigh, low, high):
    tall = lax.axis_index("gx")
    lower = sublanes((8, NZ)) < 4

    def row(r, pt, qt, keep):
        a = jnp.where(lower, pt[0:8], pltpu.roll(qt[0:8], 4, 0))
        b = jnp.where(lower, pltpu.roll(qt[24:32], 4, 0), pt[24:32])
        if keep is not None:
            a = jnp.where(keep, a, 0.0)
            b = jnp.where(keep, b, 0.0)
        low[r] = a
        high[r] = b

    for r in range(BX):
        row(r + 4, p.at[r], q.at[r], None)
    keep_low = jnp.broadcast_to(tall, (8, NZ)) > 0
    keep_high = jnp.broadcast_to(tall, (8, NZ)) < GX - 1
    for i in range(4):
        row(i, xlow.at[i], xlow.at[4 + max(i - 1, 0)], keep_low)
        row(20 + i, xhigh.at[i], xhigh.at[4 + min(i, 2)], keep_high)


def air_kernel(p, q, xlow, xhigh, ylow, yhigh, u, w, m, out_next, out_last, block, a, b, jumps, rows, sems):
    tall = lax.axis_index("gx")
    wide = lax.axis_index("gy")
    copies = [
        pltpu.make_async_copy(p, a.at[4:20, 8:40], sems.at[0]),
        pltpu.make_async_copy(q, b.at[4:20, 8:40], sems.at[1]),
    ]
    for copy in copies:
        copy.start()
    first, last = tall == 0, tall == GX - 1
    bottom, top = wide == 0, wide == GY - 1

    def keep(shape, edge):
        return jnp.broadcast_to(edge.astype(jnp.int32), shape) == 0

    inner_low, inner_high = keep((BY, NZ), first), keep((BY, NZ), last)
    for i in range(4):
        a[i, 8:40] = jnp.where(inner_low, xlow[i], 0.0)
        a[20 + i, 8:40] = jnp.where(inner_high, xhigh[i], 0.0)
    b[0, 8:40] = jnp.zeros((BY, NZ), jnp.float32)
    b[23, 8:40] = jnp.zeros((BY, NZ), jnp.float32)
    for i in range(3):
        b[1 + i, 8:40] = jnp.where(inner_low, xlow[4 + i], 0.0)
        b[20 + i, 8:40] = jnp.where(inner_high, xhigh[4 + i], 0.0)
    tile_low, tile_high = keep((8, NZ), bottom), keep((8, NZ), top)
    for r in range(XE):
        lo = jnp.where(tile_low, ylow[r], 0.0)
        hi = jnp.where(tile_high, yhigh[r], 0.0)
        a[r, 0:8] = lo
        a[r, 40:48] = hi
        b[r, 0:8] = pltpu.roll(lo, 4, 0)
        b[r, 40:48] = pltpu.roll(hi, 4, 0)

    own = (u, w, m)
    narrow = keep((4, BY), first), keep((4, BY), last)
    for i in range(3):
        at = XE * i
        rows[at : at + 4, 0:BY] = jnp.where(narrow[0], xlow[7, 8 * i : 8 * i + 4, 0:BY], 0.0)
        rows[at + 4 : at + 20, 0:BY] = own[i][...]
        rows[at + 20 : at + 24, 0:BY] = jnp.where(narrow[1], xhigh[7, 8 * i : 8 * i + 4, 0:BY], 0.0)
    for copy in copies:
        copy.wait()

    lane = lanes((YE, NZ))
    at_low, at_high = lane == 0, lane == NZ - 1
    slot = lanes((BY, 128))
    start = jnp.where(first, 4, 0)
    stop = jnp.where(last, 20, 24)

    def stepped(now, old, r):
        c = now[r]
        z = jnp.where(at_low, 0.0, pltpu.roll(c, 1, 1)) + jnp.where(at_high, 0.0, pltpu.roll(c, NZ - 1, 1))
        y = pltpu.roll(c, 1, 0) + pltpu.roll(c, YE - 1, 0)
        x = now[r - 1] + now[r + 1]
        return (2.0 - 6.0 * COURANT) * c - old[r] + COURANT * (x + y + z)

    def jump(now, r, at, total):
        below = pltpu.roll(now[r, 8:40, MID - 128 : MID], at + 1, 1)
        above = pltpu.roll(now[r, 8:40, MID : MID + 128], at, 1)
        return jnp.where(slot == at, below - above, total)

    total = jnp.zeros((BY, 128), jnp.float32)
    for t in range(4):
        now, old = (a, b) if t % 2 == 0 else (b, a)
        shift = 24 * t if t < 3 else 68
        total = lax.fori_loop(t + 1, XE - 1 - t, lambda r, s: jump(now, r, r + shift, s), total)
        if t < 3:

            def advance(r, carry):
                new = stepped(now, old, r)
                old[r, 8:40] = new[8:40]
                old[r, 0:8] = jnp.where(tile_low, new[0:8], 0.0)
                old[r, 40:48] = jnp.where(tile_high, new[40:48], 0.0)
                return carry

            lax.fori_loop(jnp.maximum(t + 1, start), jnp.minimum(XE - 1 - t, stop), advance, 0)
        else:

            def finish(r, carry):
                out_next[r - 4] = stepped(now, old, r)[8:40]
                out_last[r - 4] = now[r, 8:40]
                return carry

            lax.fori_loop(4, 20, finish, 0)

    jumps[0:BY, :] = total
    jumps[BY:128, :] = jnp.zeros((128 - BY, 128), jnp.float32)
    rows[72:160, :] = jnp.transpose(jumps[...])[0:88]
    quarter = lanes((FOLD, 128)) // 32
    folded = rows[0:FOLD, :]
    for g in range(1, 4):
        folded = jnp.where(quarter == g, pltpu.roll(rows[FOLD * g : FOLD * (g + 1), :], 32 * g, 1), folded)
    folded = pltpu.roll(folded, 32 * lax.rem(wide, 4), 1)
    for i in range(GY):
        block[i] = folded


def split(x):
    high = x.astype(jnp.bfloat16)
    low = (x - high.astype(jnp.float32)).astype(jnp.bfloat16)
    return jnp.concatenate([high, low], axis=0)


def to_columns(x, chooser):
    n = x.shape[0]
    both = lax.dot_general(split(x), chooser, (((1,), (0,)), ((), ())), preferred_element_type=jnp.float32)
    return both[0:n] + both[n : 2 * n]


def to_rows(x, chooser):
    n = x.shape[0]
    both = lax.dot_general(split(x), chooser, (((1,), (1,)), ((), ())), preferred_element_type=jnp.float32)
    return both[0:n] + both[n : 2 * n]


def chooser_of(air_row):
    rows = lax.broadcasted_iota(jnp.int32, (WINDOW, COLS), 0) + ROW0
    return jnp.where(rows == air_row[...], 1.0, 0.0).astype(jnp.bfloat16)


def beside(field):
    n = field.shape[1]
    lane = lanes(field.shape)
    left = jnp.where(lane == 0, 0.0, pltpu.roll(field, 1, 1))
    right = jnp.where(lane == n - 1, 0.0, pltpu.roll(field, n - 1, 1))
    return left + right + pltpu.roll(field, 1, 0) + pltpu.roll(field, field.shape[0] - 1, 0)


def curve(field):
    return beside(field) - 4.0 * field


def inside(shape):
    tall = lax.axis_index("gx")
    row = sublanes(shape)
    low = jnp.where(tall == 0, 4, 0)
    high = jnp.where(tall == GX - 1, 20, 24)
    return (row >= low) & (row < high)


def membrane_kernel(blocks, air_row, sums, start, mono1, mono2, force2, force3, source0, source1, parts):
    quarter = lanes((FOLD, 128)) // 32
    for g in range(4):
        for t in range(8):
            if g == 3 and t < 5:
                continue
            merged = blocks[4 * t + (-g) % 4]
            for s in range(1, 4):
                merged = jnp.where(quarter == s, blocks[4 * t + (s - g) % 4], merged)
            parts[FOLD * g : FOLD * (g + 1), 128 * t : 128 * (t + 1)] = pltpu.roll(merged, (128 - 32 * g) % 128, 1)
    chooser = chooser_of(air_row)
    u0, w0, m0 = parts[0:24, :], parts[24:48, :], parts[48:72, :]
    start[0:24] = u0
    start[24:48] = m0
    free = to_columns(parts[72:160, ROW0:], chooser)
    force3[0:8] = jnp.zeros((8, COLS), jnp.float32)
    force3[8:24] = free[72:88]
    drive, stiff = FORCE * m0, SPEED * m0
    within = inside((XE, WINDOW))
    row = sublanes((XE, COLS))
    mine = (row >= HALO) & (row < HALO + BX)
    totals = []

    def gram(fields, curves):
        for i in range(len(fields)):
            for j in range(i, len(fields)):
                product = fields[i] * curves[j]
                part = product[:, 0:128]
                for k in range(1, COLS // 128):
                    part = part + product[:, 128 * k : 128 * (k + 1)]
                totals.append(jnp.sum(part, axis=0, keepdims=True))

    def masked(curves):
        return [jnp.where(mine, -c, 0.0) for c in curves]

    c0 = curve(u0)
    gram([u0], masked([c0]))
    a0 = [drive * free[0:24], stiff * c0]
    u1 = [2.0 * u0 - w0 + a0[0], a0[1]]
    mono1[0:24] = u1[0]
    mono1[24:48] = u1[1]
    c1 = [curve(x) for x in u1]
    gram(u1, masked(c1))
    s0 = to_rows(jnp.concatenate(a0, axis=0), chooser)
    source0[...] = s0
    f1 = to_columns(-s0, chooser)
    a1 = [drive * (free[24:48] + f1[0:24]), drive * f1[24:48], stiff * c1[0], stiff * c1[1]]
    u2 = [2.0 * u1[0] - u0 + a1[0], 2.0 * u1[1] + a1[1], a1[2], a1[3]]
    for i in range(4):
        mono2[24 * i : 24 * (i + 1)] = u2[i]
    c2 = [curve(x) for x in u2]
    gram(u2, masked(c2))
    s1 = to_rows(jnp.concatenate(a1, axis=0), chooser)
    source1[...] = s1
    jump2 = []
    for i in range(4):
        half = SOURCE * s1[24 * i : 24 * (i + 1)]
        if i < 2:
            g1 = SOURCE * s0[24 * i : 24 * (i + 1)]
            half = half + (2.0 - 7.0 * COURANT) * g1 + COURANT * jnp.where(within, beside(g1), 0.0)
        jump2.append(-2.0 * half)
    f2 = to_columns(jnp.concatenate(jump2, axis=0), chooser)
    f2 = [f2[24 * i : 24 * (i + 1)] for i in range(4)]
    f2[0] = f2[0] + free[48:72]
    for i in range(4):
        force2[24 * i : 24 * (i + 1)] = f2[i]
    u3 = [2.0 * u2[i] + drive * f2[i] for i in range(4)] + [stiff * c for c in c2]
    u3[0] = u3[0] - u1[0]
    u3[1] = u3[1] - u1[1]
    gram(u3, masked([curve(x) for x in u3]))

    count = len(totals)
    stack = jnp.concatenate(totals + [jnp.zeros((56 - count, 128), jnp.float32)], axis=0)
    column = jnp.sum(stack, axis=1, keepdims=True)
    diagonal = jnp.where(sublanes((56, 128)) == lanes((56, 128)), column, 0.0)
    sums[...] = jnp.sum(diagonal, axis=0, keepdims=True)


def quadratic(sums, at, monos):
    total = 0.0
    for i in range(len(monos)):
        for j in range(i, len(monos)):
            term = monos[i] * (sums[0, at] * monos[j])
            total = total + (term if i == j else 2.0 * term)
            at += 1
    return total


def finish_kernel(
    sums, air_row, start, mono1, mono2, force2, force3, source0, source1, next_in, last_in,
    out_next, out_last, out_u, out_w, plane_next, plane_last, fields, wide_rows, turned, sems,
):
    wide = lax.axis_index("gy")
    reached = (wide >= FIRST) & (wide <= LAST)
    loads = [
        pltpu.make_async_copy(next_in.at[:, :, MID - 128 : MID + 128], plane_next, sems.at[0]),
        pltpu.make_async_copy(last_in.at[:, :, MID - 128 : MID + 128], plane_last, sems.at[1]),
    ]

    @pl.when(reached)
    def _():
        for copy in loads:
            copy.start()

    def tension(energy):
        return 1.0 + BERGER * energy / NODES

    t0 = tension(sums[0, 0])
    t1 = tension(quadratic(sums, 1, [1.0, t0]))
    four = [1.0, t0, t1, t0 * t1]
    t2 = tension(quadratic(sums, 4, four))
    t3 = tension(quadratic(sums, 14, four + [t2 * x for x in four]))

    def mixed(ref, factors):
        total = ref[0:24]
        for i in range(1, len(factors)):
            total = total + factors[i] * ref[24 * i : 24 * (i + 1)]
        return total

    chooser = chooser_of(air_row)
    m0 = start[24:48]
    drive, stiff = FORCE * m0, SPEED * m0
    u1 = mixed(mono1, four[:2])
    u2 = mixed(mono2, four)
    a2 = stiff * (t2 * curve(u2)) + drive * mixed(force2, four)
    u3 = 2.0 * u2 - u1 + a2
    s0 = mixed(source0, four[:2])
    s1 = mixed(source1, four)
    s2 = to_rows(a2, chooser)
    within = inside((XE, WINDOW))

    def spread(x):
        return jnp.where(within, beside(x), 0.0)

    g1 = SOURCE * s0
    g2 = [SOURCE * s1 + (2.0 - 7.0 * COURANT) * g1 + COURANT * spread(g1), COURANT * g1]
    g3 = [
        SOURCE * s2 + (2.0 - 7.0 * COURANT) * g2[0] - g1 + COURANT * (spread(g2[0]) + g2[1]),
        (2.0 - 6.0 * COURANT) * g2[1] + COURANT * (spread(g2[1]) + g2[0]),
        COURANT * g2[1],
    ]
    f3 = to_columns(-2.0 * g3[0], chooser)
    shifted = pltpu.roll(force3[...], XE - 4, 0)
    a3 = stiff * (t3 * curve(u3)) + drive * (f3 + shifted)
    u4 = 2.0 * u3 - u2 + a3

    tile = pl.ds(pl.multiple_of(128 * (wide // 4), 128), 128)
    back = lax.rem(128 - 32 * lax.rem(wide, 4), 128)
    fields[0:24] = u4
    fields[24:48] = u3
    out_u[...] = pltpu.roll(fields[4:20, tile], back, 1)[:, 0:BY]
    out_w[...] = pltpu.roll(fields[28:44, tile], back, 1)[:, 0:BY]

    @pl.when(reached)
    def _():
        s3 = to_rows(a3, chooser)
        g4 = [
            SOURCE * s3 + (2.0 - 7.0 * COURANT) * g3[0] - g2[0] + COURANT * (spread(g3[0]) + g3[1]),
            (2.0 - 6.0 * COURANT) * g3[1] - g2[1] + COURANT * (spread(g3[1]) + g3[0] + g3[2]),
            (2.0 - 6.0 * COURANT) * g3[2] + COURANT * (spread(g3[2]) + g3[1]),
            COURANT * g3[2],
        ]
        tile = pl.ds(pl.multiple_of(128 * (wide // 4 - ROW0 // 128), 128), 128)
        for copy in loads:
            copy.wait()
        for gains, plane in ((g4, plane_next), (g3 + [None], plane_last)):
            for k in range(4):
                if gains[k] is None:
                    turned[pl.ds(k, BX, stride=8), :] = jnp.zeros((BX, 128), jnp.float32)
                    turned[pl.ds(7 - k, BX, stride=8), :] = jnp.zeros((BX, 128), jnp.float32)
                    continue
                wide_rows[...] = gains[k]
                part = pltpu.roll(wide_rows[4:20, tile], back, 1)
                turned[pl.ds(k, BX, stride=8), :] = part
                turned[pl.ds(7 - k, BX, stride=8), :] = -part
            across = jnp.transpose(turned[...])[0:BY]
            lane = lanes((BY, 128))
            for x in range(BX):
                above = jnp.where(lane < 4, pltpu.roll(across, (128 - 8 * x) % 128, 1), 0.0)
                below = jnp.where(lane >= 124, pltpu.roll(across, (120 - 8 * x) % 128, 1), 0.0)
                plane[x, :, 0:128] = plane[x, :, 0:128] + below
                plane[x, :, 128:256] = plane[x, :, 128:256] + above
        stores = [
            pltpu.make_async_copy(plane_next, out_next.at[:, :, MID - 128 : MID + 128], sems.at[2]),
            pltpu.make_async_copy(plane_last, out_last.at[:, :, MID - 128 : MID + 128], sems.at[3]),
        ]
        for copy in stores:
            copy.start()
        for copy in stores:
            copy.wait()


def ring(count, by):
    return [(i, (i + by) % count) for i in range(count)]


def per_device(air_now, air_prev, membrane_now, membrane_prev, inv_mass, air_row):
    sem = pltpu.SemaphoreType.DMA((4,))
    halo_x = f32(8, BY, NZ)
    halo_y = f32(XE, 8, NZ)
    to_low, to_high = pl.pallas_call(
        pack_x_kernel,
        out_shape=(halo_x, halo_x),
        in_specs=[ANY, ANY, WHOLE, WHOLE, WHOLE],
        out_specs=(WHOLE, WHOLE),
        scratch_shapes=[sem],
        compiler_params=PARAMS,
        name="pack_x",
    )(air_now, air_prev, membrane_now, membrane_prev, inv_mass)
    xlow = lax.ppermute(to_high, "gx", ring(GX, 1))
    xhigh = lax.ppermute(to_low, "gx", ring(GX, -1))
    to_low, to_high = pl.pallas_call(
        pack_y_kernel,
        out_shape=(halo_y, halo_y),
        in_specs=[WHOLE] * 4,
        out_specs=(WHOLE, WHOLE),
        compiler_params=PARAMS,
        name="pack_y",
    )(air_now, air_prev, xlow, xhigh)
    ylow = lax.ppermute(to_high, "gy", ring(GY, 1))
    yhigh = lax.ppermute(to_low, "gy", ring(GY, -1))
    air = f32(BX, BY, NZ)
    next_free, last_free, block = pl.pallas_call(
        air_kernel,
        out_shape=(air, air, f32(GY, FOLD, 128)),
        in_specs=[ANY, ANY] + [WHOLE] * 7,
        out_specs=(WHOLE, WHOLE, WHOLE),
        scratch_shapes=[
            VMEM((XE, YE, NZ), jnp.float32),
            VMEM((XE, YE, NZ), jnp.float32),
            VMEM((128, 128), jnp.float32),
            VMEM((PACK, 128), jnp.float32),
            sem,
        ],
        compiler_params=PARAMS,
        name="air_free",
    )(air_now, air_prev, xlow, xhigh, ylow, yhigh, membrane_now, membrane_prev, inv_mass)
    blocks = lax.all_to_all(block, "gy", 0, 0)
    listed = air_row.reshape(1, COLS)
    sums, *saved = pl.pallas_call(
        membrane_kernel,
        out_shape=(
            f32(1, 128), f32(48, COLS), f32(48, COLS), f32(96, COLS), f32(96, COLS), f32(24, COLS),
            f32(48, WINDOW), f32(96, WINDOW),
        ),
        in_specs=[WHOLE] * 2,
        out_specs=(WHOLE,) * 8,
        scratch_shapes=[VMEM((PACK, COLS), jnp.float32)],
        compiler_params=PARAMS,
        name="membrane",
    )(blocks, listed)
    sums = lax.psum(sums, "gx")
    return pl.pallas_call(
        finish_kernel,
        out_shape=(air, air, f32(BX, BY), f32(BX, BY)),
        in_specs=[pl.BlockSpec(memory_space=pltpu.SMEM)] + [WHOLE] * 8 + [ANY, ANY],
        out_specs=(ANY, ANY, WHOLE, WHOLE),
        scratch_shapes=[
            VMEM((BX, BY, 256), jnp.float32),
            VMEM((BX, BY, 256), jnp.float32),
            VMEM((48, COLS), jnp.float32),
            VMEM((XE, WINDOW), jnp.float32),
            VMEM((128, 128), jnp.float32),
            sem,
        ],
        input_output_aliases={9: 0, 10: 1},
        compiler_params=PARAMS,
        name="finish",
    )(sums, listed, *saved, next_free, last_free)


def solution(mesh):
    in_specs = (
        P("gx", "gy", None),
        P("gx", "gy", None),
        P("gx", "gy"),
        P("gx", "gy"),
        P("gx", "gy"),
        P(),
    )
    out_specs = (P("gx", "gy", None), P("gx", "gy", None), P("gx", "gy"), P("gx", "gy"))
    return jax.shard_map(
        per_device, mesh=mesh, in_specs=in_specs, out_specs=out_specs, check_vma=False
    )
```

```python
import functools

import jax
import jax.numpy as jnp
from jax import lax
from jax.experimental import pallas as pl
from jax.experimental.pallas import tpu as pltpu
from jax.sharding import PartitionSpec as P

COURANT = 0.32
SPEED = 0.08
BERGER = 0.4
FORCE = 0.1
SOURCE = 0.5

GX, GY = 8, 32
BX, BY, NZ = 16, 32, 512
MID = NZ // 2
COLS = GY * BY
NODES = GX * BX * COLS
HALO = 4
XE = BX + 2 * HALO
YE = BY + 16
WINDOW = 384
ROW0 = COLS - WINDOW
FIRST, LAST = 22, 30
PACK = 160
FOLD = 40

VMEM = pltpu.VMEM
WHOLE = pl.BlockSpec(memory_space=pltpu.VMEM)
ANY = pl.BlockSpec(memory_space=pl.ANY)
HBM = pl.BlockSpec(memory_space=pltpu.HBM)


def granted(mib):
    return pltpu.CompilerParams(vmem_limit_bytes=mib * 1024 * 1024)


def f32(*shape):
    return jax.ShapeDtypeStruct(shape, jnp.float32)


def lanes(shape):
    return lax.broadcasted_iota(jnp.int32, shape, len(shape) - 1)


def sublanes(shape):
    return lax.broadcasted_iota(jnp.int32, shape, len(shape) - 2)


def fold(rows, wide):
    quarter = lanes((FOLD, 128)) // 32
    folded = rows[0:FOLD, :]
    for g in range(1, 4):
        folded = jnp.where(quarter == g, pltpu.roll(rows[FOLD * g : FOLD * (g + 1), :], 32 * g, 1), folded)
    return pltpu.roll(folded, 32 * lax.rem(wide, 4), 1)


def pack_kernel(
    p, q, u, w, m, xlow, xhigh, ylow, yhigh, block,
    edges, sides, tips, copied, planes, members, turned, rows, sems,
):
    wide = lax.axis_index("gy")

    def started(pairs, at):
        copies = [pltpu.make_async_copy(x, y, sems.at[at + i]) for i, (x, y) in enumerate(pairs)]
        for copy in copies:
            copy.start()
        return copies

    mids = started([(x.at[:, :, MID - 128 : MID + 128], planes.at[i]) for i, x in enumerate((p, q))], 0)
    own = started([(x, members.at[i]) for i, x in enumerate((u, w, m))], 2)
    ins = started([(x.at[:, at : at + 8], edges.at[i]) for i, (x, at) in enumerate(((p, 0), (q, 0), (p, 24), (q, 24)))], 5)
    ends = started(
        [
            (p.at[0:4], tips.at[0, 0:4]),
            (q.at[0:3], tips.at[0, 4:7]),
            (p.at[12:16], tips.at[1, 0:4]),
            (q.at[13:16], tips.at[1, 4:7]),
        ],
        9,
    )
    lane = lanes((BY, 128))
    for i in range(2):
        mids[i].wait()
        total = jnp.zeros((BY, 128), jnp.float32)
        for x in range(BX):
            above = pltpu.roll(planes[i, x, :, 128:256], 8 * x, 1)
            below = pltpu.roll(planes[i, x, :, 0:128], (8 * x + 8) % 128, 1)
            total = jnp.where((lane >= 8 * x) & (lane < 8 * x + 4), above, total)
            total = jnp.where((lane >= 8 * x + 4) & (lane < 8 * x + 8), below, total)
        turned[i, 0:BY, :] = total
        turned[i, BY:128, :] = jnp.zeros((128 - BY, 128), jnp.float32)
        turned[i] = jnp.transpose(turned[i])
        for k in range(4 - i):
            at = 48 + 64 * i + 16 * k
            rows[at : at + 16, :] = turned[i, pl.ds(7 - k, BX, stride=8), :] - turned[i, pl.ds(k, BX, stride=8), :]
    for i in range(3):
        own[i].wait()
        rows[16 * i : 16 * i + 16, 0:BY] = members[i]
    folded = fold(rows, wide)
    for i in range(GY):
        copied[i] = folded
    sent = started([(copied, block)], 13)
    lower = sublanes((8, NZ)) < 4
    for copy in ins:
        copy.wait()
    for r in range(BX):
        sides[0, r] = jnp.where(lower, edges[0, r], pltpu.roll(edges[1, r], 4, 0))
        sides[1, r] = jnp.where(lower, pltpu.roll(edges[3, r], 4, 0), edges[2, r])
    sent += started([(sides.at[0], ylow), (sides.at[1], yhigh)], 14)
    for copy in ends:
        copy.wait()
    sent += started([(tips.at[0], xlow), (tips.at[1], xhigh)], 16)
    for copy in sent:
        copy.wait()


def corner_kernel(xlow, xhigh, corner_low, corner_high):
    lower = sublanes((8, NZ)) < 4
    for i in range(4):
        for at, halo, j in ((i, xlow, 4 + max(i - 1, 0)), (4 + i, xhigh, 4 + min(i, 2))):
            corner_low[at] = jnp.where(lower, halo[i, 0:8], pltpu.roll(halo[j, 0:8], 4, 0))
            corner_high[at] = jnp.where(lower, pltpu.roll(halo[j, 24:32], 4, 0), halo[i, 24:32])


def unfold_kernel(blocks, members, jumps, to_low, to_high):
    quarter = lanes((FOLD, 128)) // 32
    for g in range(4):
        for t in range(8):
            if g >= 2 and t < 5:
                continue
            merged = blocks[4 * t + (-g) % 4]
            for s in range(1, 4):
                merged = jnp.where(quarter == s, blocks[4 * t + (s - g) % 4], merged)
            merged = pltpu.roll(merged, (128 - 32 * g) % 128, 1)
            column = slice(128 * t, 128 * (t + 1))
            narrow = slice(128 * (t - 5), 128 * (t - 4))
            if g == 0:
                members[0:40, column] = merged
            elif g == 1:
                members[40:48, column] = merged[0:8]
                if t >= 5:
                    jumps[0:32, narrow] = merged[8:40]
            else:
                jumps[40 * g - 48 : 40 * g - 8, narrow] = merged
    for out, at in ((to_low, 0), (to_high, 12)):
        for i in range(3):
            out[4 * i : 4 * i + 4, :] = members[16 * i + at : 16 * i + at + 4, :]
        for k in range(4):
            out[12 + 4 * k : 16 + 4 * k, 0:WINDOW] = jumps[16 * k + at : 16 * k + at + 4, :]
        for k in range(3):
            out[12 + 4 * k : 16 + 4 * k, 512 : 512 + WINDOW] = jumps[64 + 16 * k + at : 68 + 16 * k + at, :]


def edge_free(shape, edge):
    return jnp.broadcast_to(edge.astype(jnp.int32), shape) == 0


def air_kernel(p, q, xlow, xhigh, ylow, yhigh, clow, chigh, out_next, out_last, a, b, sems):
    tall = lax.axis_index("gx")
    wide = lax.axis_index("gy")
    first, last = tall == 0, tall == GX - 1
    bottom, top = wide == 0, wide == GY - 1
    layers = [slice(128 * k, 128 * (k + 1)) for k in range(4)]
    copies = []
    for k in range(4):
        copies.append(pltpu.make_async_copy(p.at[:, :, layers[k]], a.at[k, 4:20, 8:40], sems.at[k]))
        copies.append(pltpu.make_async_copy(q.at[:, :, layers[k]], b.at[k, 4:20, 8:40], sems.at[4 + k]))
    for copy in copies:
        copy.start()
    inner_low, inner_high = edge_free((BY, 128), first), edge_free((BY, 128), last)
    tile_low, tile_high = edge_free((8, 128), bottom), edge_free((8, 128), top)
    for k in range(4):
        for i in range(4):
            a[k, i, 8:40] = jnp.where(inner_low, xlow[i, :, layers[k]], 0.0)
            a[k, 20 + i, 8:40] = jnp.where(inner_high, xhigh[i, :, layers[k]], 0.0)
        for i in range(3):
            b[k, 1 + i, 8:40] = jnp.where(inner_low, xlow[4 + i, :, layers[k]], 0.0)
            b[k, 20 + i, 8:40] = jnp.where(inner_high, xhigh[4 + i, :, layers[k]], 0.0)
        for r in range(XE):
            if 4 <= r < 20:
                lo, hi = ylow[r - 4, :, layers[k]], yhigh[r - 4, :, layers[k]]
            else:
                i = r if r < 4 else r - 16
                free = (inner_low if r < 4 else inner_high)[0:8]
                lo = jnp.where(free, clow[i, :, layers[k]], 0.0)
                hi = jnp.where(free, chigh[i, :, layers[k]], 0.0)
            lo = jnp.where(tile_low, lo, 0.0)
            hi = jnp.where(tile_high, hi, 0.0)
            a[k, r, 0:8] = lo
            a[k, r, 40:48] = hi
            b[k, r, 0:8] = pltpu.roll(lo, 4, 0)
            b[k, r, 40:48] = pltpu.roll(hi, 4, 0)
    for copy in copies:
        copy.wait()

    lane = lanes((8, 128))

    def advance(now, old, r, tile):
        at = 8 * tile
        c = [now[k, r, at : at + 8] for k in range(4)]
        up = [pltpu.roll(x, 1, 1) for x in c]
        down = [pltpu.roll(x, 127, 1) for x in c]
        for k in range(4):
            left = jnp.where(lane == 0, up[k - 1] if k else 0.0, up[k])
            right = jnp.where(lane == 127, down[k + 1] if k < 3 else 0.0, down[k])
            if tile > 0:
                before = now[k, r, at - 1 : at + 7]
            else:
                before = pltpu.roll(c[k], 1, 0)
            if tile < 5:
                after = now[k, r, at + 1 : at + 9]
            else:
                after = pltpu.roll(c[k], 7, 0)
            ring = (left + right) + (before + after) + (now[k, r - 1, at : at + 8] + now[k, r + 1, at : at + 8])
            new = (2.0 - 6.0 * COURANT) * c[k] - old[k, r, at : at + 8] + COURANT * ring
            if tile == 0:
                new = jnp.where(tile_low, new, 0.0)
            if tile == 5:
                new = jnp.where(tile_high, new, 0.0)
            old[k, r, at : at + 8] = new

    def results(x, out, at):
        return [pltpu.make_async_copy(x.at[k, 4:20, 8:40], out.at[:, :, layers[k]], sems.at[at + k]) for k in range(4)]

    for t in range(4):
        now, old = (a, b) if t % 2 == 0 else (b, a)

        def row(r):
            for tile in range(6) if t < 3 else range(1, 5):
                advance(now, old, r, tile)

        if t < 3:

            @pl.when(jnp.logical_not(first))
            def _():
                for r in range(t + 1, 4):
                    row(r)

        def body(i, carry):
            for r in range(8):
                row(4 + 8 * i + r)
            return carry

        lax.fori_loop(0, 2, body, 0)
        if t < 3:

            @pl.when(jnp.logical_not(last))
            def _():
                for r in range(20, XE - 1 - t):
                    row(r)

        if t == 2:
            sent = results(b, out_last, 8)
            for copy in sent:
                copy.start()
    sent = sent + results(a, out_next, 12)
    for copy in sent[4:]:
        copy.start()
    for copy in sent:
        copy.wait()


def split(x):
    high = x.astype(jnp.bfloat16)
    low = (x - high.astype(jnp.float32)).astype(jnp.bfloat16)
    return jnp.concatenate([high, low], axis=0)


def to_columns(x, chooser):
    n = x.shape[0]
    both = lax.dot_general(split(x), chooser, (((1,), (0,)), ((), ())), preferred_element_type=jnp.float32)
    return both[0:n] + both[n : 2 * n]


def to_rows(x, chooser):
    n = x.shape[0]
    both = lax.dot_general(split(x), chooser, (((1,), (1,)), ((), ())), preferred_element_type=jnp.float32)
    return both[0:n] + both[n : 2 * n]


def chooser_of(air_row):
    rows = lax.broadcasted_iota(jnp.int32, (WINDOW, COLS), 0) + ROW0
    return jnp.where(rows == air_row[...], 1.0, 0.0).astype(jnp.bfloat16)


def beside(field):
    n = field.shape[1]
    lane = lanes(field.shape)
    left = jnp.where(lane == 0, 0.0, pltpu.roll(field, 1, 1))
    right = jnp.where(lane == n - 1, 0.0, pltpu.roll(field, n - 1, 1))
    return left + right + pltpu.roll(field, 1, 0) + pltpu.roll(field, field.shape[0] - 1, 0)


def curve(field):
    return beside(field) - 4.0 * field


def inside(shape):
    tall = lax.axis_index("gx")
    row = sublanes(shape)
    low = jnp.where(tall == 0, 4, 0)
    high = jnp.where(tall == GX - 1, 20, 24)
    return (row >= low) & (row < high)


def membrane_kernel(
    members, jumps, hlow, hhigh, air_row, sums, start, mono1, mono2, force2, force3, source0, source1, parts, slab, listed, sems
):
    tall = lax.axis_index("gx")
    loaded = pltpu.make_async_copy(air_row, listed, sems.at[0])
    loaded.start()
    for i in range(3):
        at = XE * i
        parts[at : at + 4] = jnp.where(edge_free((4, COLS), tall == 0), hlow[4 * i : 4 * i + 4, :], 0.0)
        parts[at + 4 : at + 20] = members[16 * i : 16 * i + 16]
        parts[at + 20 : at + 24] = jnp.where(edge_free((4, COLS), tall == GX - 1), hhigh[4 * i : 4 * i + 4, :], 0.0)
    for i in range(7):
        at, row = XE * i, 12 + 4 * (i % 4)
        narrow = slice(512 * (i // 4), 512 * (i // 4) + WINDOW)
        slab[at : at + 4] = jnp.where(edge_free((4, WINDOW), tall == 0), hlow[row : row + 4, narrow], 0.0)
        slab[at + 4 : at + 20] = jumps[16 * i : 16 * i + 16]
        slab[at + 20 : at + 24] = jnp.where(edge_free((4, WINDOW), tall == GX - 1), hhigh[row : row + 4, narrow], 0.0)
    within = inside((XE, WINDOW))

    def spread(x):
        return jnp.where(within, beside(x), 0.0)

    older = [slab[96 + XE * k : 96 + XE * (k + 1)] for k in range(3)] + [None]
    newer = [slab[XE * k : XE * (k + 1)] for k in range(4)]
    free = [newer[0]]
    for t in range(3):
        step = []
        for k in range(3 - t):
            own = 2.0 - (7.0 if k == 0 else 6.0) * COURANT
            ring = spread(newer[k]) + newer[k + 1]
            if k:
                ring = ring + newer[k - 1]
            step.append(own * newer[k] - older[k] + COURANT * ring)
        older, newer = newer, step
        free.append(newer[0])
    loaded.wait()
    chooser = chooser_of(listed)
    u0, w0, m0 = parts[0:24], parts[24:48], parts[48:72]
    start[0:24] = u0
    start[24:48] = m0
    free = to_columns(jnp.concatenate(free, axis=0), chooser)
    force3[...] = free[72:96]
    drive, stiff = FORCE * m0, SPEED * m0
    row = sublanes((XE, COLS))
    mine = (row >= HALO) & (row < HALO + BX)
    totals = []

    def gram(fields, curves):
        for i in range(len(fields)):
            for j in range(i, len(fields)):
                product = fields[i] * curves[j]
                part = product[:, 0:128]
                for k in range(1, COLS // 128):
                    part = part + product[:, 128 * k : 128 * (k + 1)]
                totals.append(jnp.sum(part, axis=0, keepdims=True))

    def masked(curves):
        return [jnp.where(mine, -c, 0.0) for c in curves]

    c0 = curve(u0)
    gram([u0], masked([c0]))
    a0 = [drive * free[0:24], stiff * c0]
    u1 = [2.0 * u0 - w0 + a0[0], a0[1]]
    mono1[0:24] = u1[0]
    mono1[24:48] = u1[1]
    c1 = [curve(x) for x in u1]
    gram(u1, masked(c1))
    s0 = to_rows(jnp.concatenate(a0, axis=0), chooser)
    source0[...] = s0
    f1 = to_columns(-s0, chooser)
    a1 = [drive * (free[24:48] + f1[0:24]), drive * f1[24:48], stiff * c1[0], stiff * c1[1]]
    u2 = [2.0 * u1[0] - u0 + a1[0], 2.0 * u1[1] + a1[1], a1[2], a1[3]]
    for i in range(4):
        mono2[24 * i : 24 * (i + 1)] = u2[i]
    c2 = [curve(x) for x in u2]
    gram(u2, masked(c2))
    s1 = to_rows(jnp.concatenate(a1, axis=0), chooser)
    source1[...] = s1
    jump2 = []
    for i in range(4):
        half = SOURCE * s1[24 * i : 24 * (i + 1)]
        if i < 2:
            g1 = SOURCE * s0[24 * i : 24 * (i + 1)]
            half = half + (2.0 - 7.0 * COURANT) * g1 + COURANT * spread(g1)
        jump2.append(-2.0 * half)
    f2 = to_columns(jnp.concatenate(jump2, axis=0), chooser)
    f2 = [f2[24 * i : 24 * (i + 1)] for i in range(4)]
    f2[0] = f2[0] + free[48:72]
    for i in range(4):
        force2[24 * i : 24 * (i + 1)] = f2[i]
    u3 = [2.0 * u2[i] + drive * f2[i] for i in range(4)] + [stiff * c for c in c2]
    u3[0] = u3[0] - u1[0]
    u3[1] = u3[1] - u1[1]
    gram(u3, masked([curve(x) for x in u3]))

    count = len(totals)
    stack = jnp.concatenate(totals + [jnp.zeros((56 - count, 128), jnp.float32)], axis=0)
    column = jnp.sum(stack, axis=1, keepdims=True)
    diagonal = jnp.where(sublanes((56, 128)) == lanes((56, 128)), column, 0.0)
    sums[...] = jnp.sum(diagonal, axis=0, keepdims=True)


def quadratic(sums, at, monos):
    total = 0.0
    for i in range(len(monos)):
        for j in range(i, len(monos)):
            term = monos[i] * (sums(at) * monos[j])
            total = total + (term if i == j else 2.0 * term)
            at += 1
    return total


def finish_kernel(
    share0, share1, share2, share3, air_row, start, mono1, mono2, force2, force3, source0, source1, next_in, last_in,
    out_next, out_last, out_u, out_w, plane_next, plane_last, fields, wide_rows, turned, listed, sems,
):
    wide = lax.axis_index("gy")
    reached = (wide >= FIRST) & (wide <= LAST)
    loaded = pltpu.make_async_copy(air_row, listed, sems.at[4])
    loaded.start()
    loads = [
        pltpu.make_async_copy(next_in.at[:, :, MID - 128 : MID + 128], plane_next, sems.at[0]),
        pltpu.make_async_copy(last_in.at[:, :, MID - 128 : MID + 128], plane_last, sems.at[1]),
    ]

    @pl.when(reached)
    def _():
        for copy in loads:
            copy.start()

    def tension(energy):
        return 1.0 + BERGER * energy / NODES

    def sums(at):
        return (share0[0, at] + share1[0, at]) + (share2[0, at] + share3[0, at])

    t0 = tension(sums(0))
    t1 = tension(quadratic(sums, 1, [1.0, t0]))
    four = [1.0, t0, t1, t0 * t1]
    t2 = tension(quadratic(sums, 4, four))
    t3 = tension(quadratic(sums, 14, four + [t2 * x for x in four]))

    def mixed(ref, factors):
        total = ref[0:24]
        for i in range(1, len(factors)):
            total = total + factors[i] * ref[24 * i : 24 * (i + 1)]
        return total

    loaded.wait()
    chooser = chooser_of(listed)
    m0 = start[24:48]
    drive, stiff = FORCE * m0, SPEED * m0
    u1 = mixed(mono1, four[:2])
    u2 = mixed(mono2, four)
    a2 = stiff * (t2 * curve(u2)) + drive * mixed(force2, four)
    u3 = 2.0 * u2 - u1 + a2
    s0 = mixed(source0, four[:2])
    s1 = mixed(source1, four)
    s2 = to_rows(a2, chooser)
    within = inside((XE, WINDOW))

    def spread(x):
        return jnp.where(within, beside(x), 0.0)

    g1 = SOURCE * s0
    g2 = [SOURCE * s1 + (2.0 - 7.0 * COURANT) * g1 + COURANT * spread(g1), COURANT * g1]
    g3 = [
        SOURCE * s2 + (2.0 - 7.0 * COURANT) * g2[0] - g1 + COURANT * (spread(g2[0]) + g2[1]),
        (2.0 - 6.0 * COURANT) * g2[1] + COURANT * (spread(g2[1]) + g2[0]),
        COURANT * g2[1],
    ]
    f3 = to_columns(-2.0 * g3[0], chooser)
    a3 = stiff * (t3 * curve(u3)) + drive * (f3 + force3[...])
    u4 = 2.0 * u3 - u2 + a3

    tile = pl.ds(pl.multiple_of(128 * (wide // 4), 128), 128)
    back = lax.rem(128 - 32 * lax.rem(wide, 4), 128)
    fields[0:24] = u4
    fields[24:48] = u3
    out_u[...] = pltpu.roll(fields[4:20, tile], back, 1)[:, 0:BY]
    out_w[...] = pltpu.roll(fields[28:44, tile], back, 1)[:, 0:BY]

    @pl.when(reached)
    def _():
        s3 = to_rows(a3, chooser)
        g4 = [
            SOURCE * s3 + (2.0 - 7.0 * COURANT) * g3[0] - g2[0] + COURANT * (spread(g3[0]) + g3[1]),
            (2.0 - 6.0 * COURANT) * g3[1] - g2[1] + COURANT * (spread(g3[1]) + g3[0] + g3[2]),
            (2.0 - 6.0 * COURANT) * g3[2] + COURANT * (spread(g3[2]) + g3[1]),
            COURANT * g3[2],
        ]
        tile = pl.ds(pl.multiple_of(128 * (wide // 4 - ROW0 // 128), 128), 128)
        for copy in loads:
            copy.wait()
        for gains, plane in ((g4, plane_next), (g3 + [None], plane_last)):
            for k in range(4):
                if gains[k] is None:
                    turned[pl.ds(k, BX, stride=8), :] = jnp.zeros((BX, 128), jnp.float32)
                    turned[pl.ds(7 - k, BX, stride=8), :] = jnp.zeros((BX, 128), jnp.float32)
                    continue
                wide_rows[...] = gains[k]
                part = pltpu.roll(wide_rows[4:20, tile], back, 1)
                turned[pl.ds(k, BX, stride=8), :] = part
                turned[pl.ds(7 - k, BX, stride=8), :] = -part
            across = jnp.transpose(turned[...])[0:BY]
            lane = lanes((BY, 128))
            for x in range(BX):
                above = jnp.where(lane < 4, pltpu.roll(across, (128 - 8 * x) % 128, 1), 0.0)
                below = jnp.where(lane >= 124, pltpu.roll(across, (120 - 8 * x) % 128, 1), 0.0)
                plane[x, :, 0:128] = plane[x, :, 0:128] + below
                plane[x, :, 128:256] = plane[x, :, 128:256] + above
        stores = [
            pltpu.make_async_copy(plane_next, out_next.at[:, :, MID - 128 : MID + 128], sems.at[2]),
            pltpu.make_async_copy(plane_last, out_last.at[:, :, MID - 128 : MID + 128], sems.at[3]),
        ]
        for copy in stores:
            copy.start()
        for copy in stores:
            copy.wait()


def ring(count, by):
    return [(i, (i + by) % count) for i in range(count)]


def across(count, by):
    return [(i, (i + 2 * by) % count if by else i ^ 1) for i in range(count)]


def per_device(air_now, air_prev, membrane_now, membrane_prev, inv_mass, air_row):
    def sems(n):
        return pltpu.SemaphoreType.DMA((n,))

    halo_x, halo_y, corner, stripe = f32(7, BY, NZ), f32(BX, 8, NZ), f32(8, 8, NZ), f32(28, COLS)
    *sends, block = pl.pallas_call(
        pack_kernel,
        out_shape=(halo_x, halo_x, halo_y, halo_y, f32(GY, FOLD, 128)),
        in_specs=[HBM] * 5,
        out_specs=(HBM,) * 5,
        scratch_shapes=[
            VMEM((4, BX, 8, NZ), jnp.float32),
            VMEM((2, BX, 8, NZ), jnp.float32),
            VMEM((2, 7, BY, NZ), jnp.float32),
            VMEM((GY, FOLD, 128), jnp.float32),
            VMEM((2, BX, BY, 256), jnp.float32),
            VMEM((3, BX, BY), jnp.float32),
            VMEM((2, 128, 128), jnp.float32),
            VMEM((PACK, 128), jnp.float32),
            sems(18),
        ],
        compiler_params=granted(63),
        name="pack",
    )(air_now, air_prev, membrane_now, membrane_prev, inv_mass)
    blocks = lax.all_to_all(block, "gy", 0, 0)
    to_xlow, to_xhigh, to_ylow, to_yhigh = sends
    xlow = lax.ppermute(to_xhigh, "gx", ring(GX, 1))
    xhigh = lax.ppermute(to_xlow, "gx", ring(GX, -1))
    ylow = lax.ppermute(to_yhigh, "gy", ring(GY, 1))
    yhigh = lax.ppermute(to_ylow, "gy", ring(GY, -1))
    to_clow, to_chigh = pl.pallas_call(
        corner_kernel,
        out_shape=(corner, corner),
        in_specs=[WHOLE] * 2,
        out_specs=(WHOLE,) * 2,
        compiler_params=granted(3),
        name="corners",
    )(xlow, xhigh)
    clow = lax.ppermute(to_chigh, "gy", ring(GY, 1))
    chigh = lax.ppermute(to_clow, "gy", ring(GY, -1))
    air = f32(BX, BY, NZ)
    brick = VMEM((4, XE, YE, 128), jnp.float32)
    next_free, last_free = pl.pallas_call(
        air_kernel,
        out_shape=(air, air),
        in_specs=[HBM, HBM] + [WHOLE] * 6,
        out_specs=(HBM, HBM),
        scratch_shapes=[brick, brick, sems(16)],
        compiler_params=granted(8),
        cost_estimate=pl.CostEstimate(flops=40_000_000, bytes_accessed=8_000_000, transcendentals=0),
        name="air_free",
    )(air_now, air_prev, xlow, xhigh, ylow, yhigh, clow, chigh)
    members, jumps, to_low, to_high = pl.pallas_call(
        unfold_kernel,
        out_shape=(f32(48, COLS), f32(112, WINDOW), stripe, stripe),
        in_specs=[WHOLE],
        out_specs=(WHOLE,) * 4,
        compiler_params=granted(3),
        name="unfold",
    )(blocks)
    hlow = lax.ppermute(to_high, "gx", ring(GX, 1))
    hhigh = lax.ppermute(to_low, "gx", ring(GX, -1))
    listed = air_row.reshape(1, COLS)
    sums, *saved = pl.pallas_call(
        membrane_kernel,
        out_shape=(
            f32(1, 128), f32(48, COLS), f32(48, COLS), f32(96, COLS), f32(96, COLS), f32(24, COLS),
            f32(48, WINDOW), f32(96, WINDOW),
        ),
        in_specs=[WHOLE] * 4 + [HBM],
        out_specs=(WHOLE,) * 8,
        scratch_shapes=[
            VMEM((3 * XE, COLS), jnp.float32),
            VMEM((7 * XE, WINDOW), jnp.float32),
            VMEM((1, COLS), jnp.int32),
            sems(1),
        ],
        compiler_params=granted(10),
        name="membrane",
    )(members, jumps, hlow, hhigh, listed)
    sums = sums + lax.ppermute(sums, "gx", across(GX, 0))
    shares = [sums] + [lax.ppermute(sums, "gx", across(GX, by)) for by in (1, 2, 3)]
    return pl.pallas_call(
        finish_kernel,
        out_shape=(air, air, f32(BX, BY), f32(BX, BY)),
        in_specs=[pl.BlockSpec(memory_space=pltpu.SMEM)] * 4 + [HBM] + [WHOLE] * 7 + [HBM, HBM],
        out_specs=(HBM, HBM, WHOLE, WHOLE),
        scratch_shapes=[
            VMEM((BX, BY, 256), jnp.float32),
            VMEM((BX, BY, 256), jnp.float32),
            VMEM((48, COLS), jnp.float32),
            VMEM((XE, WINDOW), jnp.float32),
            VMEM((128, 128), jnp.float32),
            VMEM((1, COLS), jnp.int32),
            sems(5),
        ],
        input_output_aliases={12: 0, 13: 1},
        compiler_params=granted(8),
        name="finish",
    )(*shares, listed, *saved, next_free, last_free)


def solution(mesh):
    in_specs = (
        P("gx", "gy", None),
        P("gx", "gy", None),
        P("gx", "gy"),
        P("gx", "gy"),
        P("gx", "gy"),
        P(),
    )
    out_specs = (P("gx", "gy", None), P("gx", "gy", None), P("gx", "gy"), P("gx", "gy"))
    return jax.shard_map(
        per_device, mesh=mesh, in_specs=in_specs, out_specs=out_specs, check_vma=False
    )
```

```python
import functools

import jax
import jax.numpy as jnp
from jax import lax
from jax.experimental import pallas as pl
from jax.experimental.pallas import tpu as pltpu
from jax.sharding import PartitionSpec as P

COURANT = 0.32
SPEED = 0.08
BERGER = 0.4
FORCE = 0.1
SOURCE = 0.5

GX, GY = 8, 32
BX, BY, NZ = 16, 32, 512
MID = NZ // 2
COLS = GY * BY
NODES = GX * BX * COLS
HALO = 4
XE = BX + 2 * HALO
YE = BY + 16
WINDOW = 384
ROW0 = COLS - WINDOW
FIRST, LAST = 22, 30
PACK = 160
FOLD = 40

VMEM = pltpu.VMEM
WHOLE = pl.BlockSpec(memory_space=pltpu.VMEM)
ANY = pl.BlockSpec(memory_space=pl.ANY)
HBM = pl.BlockSpec(memory_space=pltpu.HBM)


def granted(mib):
    return pltpu.CompilerParams(vmem_limit_bytes=mib * 1024 * 1024)


def f32(*shape):
    return jax.ShapeDtypeStruct(shape, jnp.float32)


def lanes(shape):
    return lax.broadcasted_iota(jnp.int32, shape, len(shape) - 1)


def sublanes(shape):
    return lax.broadcasted_iota(jnp.int32, shape, len(shape) - 2)


def fold(rows, wide):
    quarter = lanes((FOLD, 128)) // 32
    folded = rows[0:FOLD, :]
    for g in range(1, 4):
        folded = jnp.where(quarter == g, pltpu.roll(rows[FOLD * g : FOLD * (g + 1), :], 32 * g, 1), folded)
    return pltpu.roll(folded, 32 * lax.rem(wide, 4), 1)


def pack_kernel(
    p, q, u, w, m, xlow, xhigh, ylow, yhigh, block,
    edges, sides, tips, copied, planes, members, turned, rows, sems,
):
    wide = lax.axis_index("gy")

    def started(pairs, at):
        copies = [pltpu.make_async_copy(x, y, sems.at[at + i]) for i, (x, y) in enumerate(pairs)]
        for copy in copies:
            copy.start()
        return copies

    mids = started([(x.at[:, :, MID - 128 : MID + 128], planes.at[i]) for i, x in enumerate((p, q))], 0)
    own = started([(x, members.at[i]) for i, x in enumerate((u, w, m))], 2)
    ins = started([(x.at[:, at : at + 8], edges.at[i]) for i, (x, at) in enumerate(((p, 0), (q, 0), (p, 24), (q, 24)))], 5)
    ends = started(
        [
            (p.at[0:4], tips.at[0, 0:4]),
            (q.at[0:3], tips.at[0, 4:7]),
            (p.at[12:16], tips.at[1, 0:4]),
            (q.at[13:16], tips.at[1, 4:7]),
        ],
        9,
    )
    lane = lanes((BY, 128))
    for i in range(2):
        mids[i].wait()
        total = jnp.zeros((BY, 128), jnp.float32)
        for x in range(BX):
            above = pltpu.roll(planes[i, x, :, 128:256], 8 * x, 1)
            below = pltpu.roll(planes[i, x, :, 0:128], (8 * x + 8) % 128, 1)
            total = jnp.where((lane >= 8 * x) & (lane < 8 * x + 4), above, total)
            total = jnp.where((lane >= 8 * x + 4) & (lane < 8 * x + 8), below, total)
        turned[i, 0:BY, :] = total
        turned[i, BY:128, :] = jnp.zeros((128 - BY, 128), jnp.float32)
        turned[i] = jnp.transpose(turned[i])
        for k in range(4 - i):
            at = 48 + 64 * i + 16 * k
            rows[at : at + 16, :] = turned[i, pl.ds(7 - k, BX, stride=8), :] - turned[i, pl.ds(k, BX, stride=8), :]
    for i in range(3):
        own[i].wait()
        rows[16 * i : 16 * i + 16, 0:BY] = members[i]
    folded = fold(rows, wide)
    for i in range(GY):
        copied[i] = folded
    sent = started([(copied, block)], 13)
    lower = sublanes((8, NZ)) < 4
    for copy in ins:
        copy.wait()
    for r in range(BX):
        sides[0, r] = jnp.where(lower, edges[0, r], pltpu.roll(edges[1, r], 4, 0))
        sides[1, r] = jnp.where(lower, pltpu.roll(edges[3, r], 4, 0), edges[2, r])
    sent += started([(sides.at[0], ylow), (sides.at[1], yhigh)], 14)
    for copy in ends:
        copy.wait()
    sent += started([(tips.at[0], xlow), (tips.at[1], xhigh)], 16)
    for copy in sent:
        copy.wait()


def corner_kernel(xlow, xhigh, corner_low, corner_high):
    lower = sublanes((8, NZ)) < 4
    for i in range(4):
        for at, halo, j in ((i, xlow, 4 + max(i - 1, 0)), (4 + i, xhigh, 4 + min(i, 2))):
            corner_low[at] = jnp.where(lower, halo[i, 0:8], pltpu.roll(halo[j, 0:8], 4, 0))
            corner_high[at] = jnp.where(lower, pltpu.roll(halo[j, 24:32], 4, 0), halo[i, 24:32])


def unfold_kernel(blocks, after, members, jumps, to_low, to_high):
    quarter = lanes((FOLD, 128)) // 32
    for g in range(4):
        for t in range(8):
            if g >= 2 and t < 5:
                continue
            merged = blocks[4 * t + (-g) % 4]
            for s in range(1, 4):
                merged = jnp.where(quarter == s, blocks[4 * t + (s - g) % 4], merged)
            merged = pltpu.roll(merged, (128 - 32 * g) % 128, 1)
            column = slice(128 * t, 128 * (t + 1))
            narrow = slice(128 * (t - 5), 128 * (t - 4))
            if g == 0:
                members[0:40, column] = merged
            elif g == 1:
                members[40:48, column] = merged[0:8]
                if t >= 5:
                    jumps[0:32, narrow] = merged[8:40]
            else:
                jumps[40 * g - 48 : 40 * g - 8, narrow] = merged
    for out, at in ((to_low, 0), (to_high, 12)):
        for i in range(3):
            out[4 * i : 4 * i + 4, :] = members[16 * i + at : 16 * i + at + 4, :]
        for k in range(4):
            out[12 + 4 * k : 16 + 4 * k, 0:WINDOW] = jumps[16 * k + at : 16 * k + at + 4, :]
        for k in range(3):
            out[12 + 4 * k : 16 + 4 * k, 512 : 512 + WINDOW] = jumps[64 + 16 * k + at : 68 + 16 * k + at, :]


def edge_free(shape, edge):
    return jnp.broadcast_to(edge.astype(jnp.int32), shape) == 0


def air_kernel(p, q, xlow, xhigh, ylow, yhigh, clow, chigh, out_next, out_last, done, a, b, sems):
    tall = lax.axis_index("gx")
    wide = lax.axis_index("gy")
    first, last = tall == 0, tall == GX - 1
    bottom, top = wide == 0, wide == GY - 1
    layers = [slice(128 * k, 128 * (k + 1)) for k in range(4)]
    copies = []
    for k in range(4):
        copies.append(pltpu.make_async_copy(p.at[:, :, layers[k]], a.at[k, 4:20, 8:40], sems.at[k]))
        copies.append(pltpu.make_async_copy(q.at[:, :, layers[k]], b.at[k, 4:20, 8:40], sems.at[4 + k]))
    for copy in copies:
        copy.start()
    inner_low, inner_high = edge_free((BY, 128), first), edge_free((BY, 128), last)
    tile_low, tile_high = edge_free((8, 128), bottom), edge_free((8, 128), top)
    for k in range(4):
        for i in range(4):
            a[k, i, 8:40] = jnp.where(inner_low, xlow[i, :, layers[k]], 0.0)
            a[k, 20 + i, 8:40] = jnp.where(inner_high, xhigh[i, :, layers[k]], 0.0)
        for i in range(3):
            b[k, 1 + i, 8:40] = jnp.where(inner_low, xlow[4 + i, :, layers[k]], 0.0)
            b[k, 20 + i, 8:40] = jnp.where(inner_high, xhigh[4 + i, :, layers[k]], 0.0)
        for r in range(XE):
            if 4 <= r < 20:
                lo, hi = ylow[r - 4, :, layers[k]], yhigh[r - 4, :, layers[k]]
            else:
                i = r if r < 4 else r - 16
                free = (inner_low if r < 4 else inner_high)[0:8]
                lo = jnp.where(free, clow[i, :, layers[k]], 0.0)
                hi = jnp.where(free, chigh[i, :, layers[k]], 0.0)
            lo = jnp.where(tile_low, lo, 0.0)
            hi = jnp.where(tile_high, hi, 0.0)
            a[k, r, 0:8] = lo
            a[k, r, 40:48] = hi
            b[k, r, 0:8] = pltpu.roll(lo, 4, 0)
            b[k, r, 40:48] = pltpu.roll(hi, 4, 0)
    for copy in copies:
        copy.wait()

    lane = lanes((8, 128))

    def advance(now, old, r, tile):
        at = 8 * tile
        c = [now[k, r, at : at + 8] for k in range(4)]
        up = [pltpu.roll(x, 1, 1) for x in c]
        down = [pltpu.roll(x, 127, 1) for x in c]
        for k in range(4):
            left = jnp.where(lane == 0, up[k - 1] if k else 0.0, up[k])
            right = jnp.where(lane == 127, down[k + 1] if k < 3 else 0.0, down[k])
            if tile > 0:
                before = now[k, r, at - 1 : at + 7]
            else:
                before = pltpu.roll(c[k], 1, 0)
            if tile < 5:
                after = now[k, r, at + 1 : at + 9]
            else:
                after = pltpu.roll(c[k], 7, 0)
            ring = (left + right) + (before + after) + (now[k, r - 1, at : at + 8] + now[k, r + 1, at : at + 8])
            new = (2.0 - 6.0 * COURANT) * c[k] - old[k, r, at : at + 8] + COURANT * ring
            if tile == 0:
                new = jnp.where(tile_low, new, 0.0)
            if tile == 5:
                new = jnp.where(tile_high, new, 0.0)
            old[k, r, at : at + 8] = new

    def results(x, out, at):
        return [pltpu.make_async_copy(x.at[k, 4:20, 8:40], out.at[:, :, layers[k]], sems.at[at + k]) for k in range(4)]

    for t in range(4):
        now, old = (a, b) if t % 2 == 0 else (b, a)

        def row(r):
            for tile in range(6) if t < 3 else range(1, 5):
                advance(now, old, r, tile)

        if t < 3:

            @pl.when(jnp.logical_not(first))
            def _():
                for r in range(t + 1, 4):
                    row(r)

        def body(i, carry):
            for r in range(8):
                row(4 + 8 * i + r)
            return carry

        lax.fori_loop(0, 2, body, 0)
        if t < 3:

            @pl.when(jnp.logical_not(last))
            def _():
                for r in range(20, XE - 1 - t):
                    row(r)

        if t == 2:
            sent = results(b, out_last, 8)
            for copy in sent:
                copy.start()
    sent = sent + results(a, out_next, 12)
    for copy in sent[4:]:
        copy.start()
    done[...] = jnp.zeros((8, 128), jnp.float32)
    for copy in sent:
        copy.wait()


def split(x):
    high = x.astype(jnp.bfloat16)
    low = (x - high.astype(jnp.float32)).astype(jnp.bfloat16)
    return jnp.concatenate([high, low], axis=0)


def to_columns(x, chooser):
    n = x.shape[0]
    both = lax.dot_general(split(x), chooser, (((1,), (0,)), ((), ())), preferred_element_type=jnp.float32)
    return both[0:n] + both[n : 2 * n]


def to_rows(x, chooser):
    n = x.shape[0]
    both = lax.dot_general(split(x), chooser, (((1,), (1,)), ((), ())), preferred_element_type=jnp.float32)
    return both[0:n] + both[n : 2 * n]


def chooser_of(air_row):
    rows = lax.broadcasted_iota(jnp.int32, (WINDOW, COLS), 0) + ROW0
    return jnp.where(rows == air_row[...], 1.0, 0.0).astype(jnp.bfloat16)


def beside(field):
    n = field.shape[1]
    lane = lanes(field.shape)
    left = jnp.where(lane == 0, 0.0, pltpu.roll(field, 1, 1))
    right = jnp.where(lane == n - 1, 0.0, pltpu.roll(field, n - 1, 1))
    return left + right + pltpu.roll(field, 1, 0) + pltpu.roll(field, field.shape[0] - 1, 0)


def curve(field):
    return beside(field) - 4.0 * field


def inside(shape):
    tall = lax.axis_index("gx")
    row = sublanes(shape)
    low = jnp.where(tall == 0, 4, 0)
    high = jnp.where(tall == GX - 1, 20, 24)
    return (row >= low) & (row < high)


def membrane_kernel(
    members, jumps, hlow, hhigh, air_row, sums, start, mono1, mono2, force2, force3, source0, source1, parts, slab, listed, sems
):
    tall = lax.axis_index("gx")
    loaded = pltpu.make_async_copy(air_row, listed, sems.at[0])
    loaded.start()
    for i in range(3):
        at = XE * i
        parts[at : at + 4] = jnp.where(edge_free((4, COLS), tall == 0), hlow[4 * i : 4 * i + 4, :], 0.0)
        parts[at + 4 : at + 20] = members[16 * i : 16 * i + 16]
        parts[at + 20 : at + 24] = jnp.where(edge_free((4, COLS), tall == GX - 1), hhigh[4 * i : 4 * i + 4, :], 0.0)
    for i in range(7):
        at, row = XE * i, 12 + 4 * (i % 4)
        narrow = slice(512 * (i // 4), 512 * (i // 4) + WINDOW)
        slab[at : at + 4] = jnp.where(edge_free((4, WINDOW), tall == 0), hlow[row : row + 4, narrow], 0.0)
        slab[at + 4 : at + 20] = jumps[16 * i : 16 * i + 16]
        slab[at + 20 : at + 24] = jnp.where(edge_free((4, WINDOW), tall == GX - 1), hhigh[row : row + 4, narrow], 0.0)
    within = inside((XE, WINDOW))

    def spread(x):
        return jnp.where(within, beside(x), 0.0)

    older = [slab[96 + XE * k : 96 + XE * (k + 1)] for k in range(3)] + [None]
    newer = [slab[XE * k : XE * (k + 1)] for k in range(4)]
    free = [newer[0]]
    for t in range(3):
        step = []
        for k in range(3 - t):
            own = 2.0 - (7.0 if k == 0 else 6.0) * COURANT
            ring = spread(newer[k]) + newer[k + 1]
            if k:
                ring = ring + newer[k - 1]
            step.append(own * newer[k] - older[k] + COURANT * ring)
        older, newer = newer, step
        free.append(newer[0])
    loaded.wait()
    chooser = chooser_of(listed)
    u0, w0, m0 = parts[0:24], parts[24:48], parts[48:72]
    start[0:24] = u0
    start[24:48] = m0
    free = to_columns(jnp.concatenate(free, axis=0), chooser)
    force3[...] = free[72:96]
    drive, stiff = FORCE * m0, SPEED * m0
    row = sublanes((XE, COLS))
    mine = (row >= HALO) & (row < HALO + BX)
    totals = []

    def gram(fields, curves):
        for i in range(len(fields)):
            for j in range(i, len(fields)):
                product = fields[i] * curves[j]
                part = product[:, 0:128]
                for k in range(1, COLS // 128):
                    part = part + product[:, 128 * k : 128 * (k + 1)]
                totals.append(jnp.sum(part, axis=0, keepdims=True))

    def masked(curves):
        return [jnp.where(mine, -c, 0.0) for c in curves]

    c0 = curve(u0)
    gram([u0], masked([c0]))
    a0 = [drive * free[0:24], stiff * c0]
    u1 = [2.0 * u0 - w0 + a0[0], a0[1]]
    mono1[0:24] = u1[0]
    mono1[24:48] = u1[1]
    c1 = [curve(x) for x in u1]
    gram(u1, masked(c1))
    s0 = to_rows(jnp.concatenate(a0, axis=0), chooser)
    source0[...] = s0
    f1 = to_columns(-s0, chooser)
    a1 = [drive * (free[24:48] + f1[0:24]), drive * f1[24:48], stiff * c1[0], stiff * c1[1]]
    u2 = [2.0 * u1[0] - u0 + a1[0], 2.0 * u1[1] + a1[1], a1[2], a1[3]]
    for i in range(4):
        mono2[24 * i : 24 * (i + 1)] = u2[i]
    c2 = [curve(x) for x in u2]
    gram(u2, masked(c2))
    s1 = to_rows(jnp.concatenate(a1, axis=0), chooser)
    source1[...] = s1
    jump2 = []
    for i in range(4):
        half = SOURCE * s1[24 * i : 24 * (i + 1)]
        if i < 2:
            g1 = SOURCE * s0[24 * i : 24 * (i + 1)]
            half = half + (2.0 - 7.0 * COURANT) * g1 + COURANT * spread(g1)
        jump2.append(-2.0 * half)
    f2 = to_columns(jnp.concatenate(jump2, axis=0), chooser)
    f2 = [f2[24 * i : 24 * (i + 1)] for i in range(4)]
    f2[0] = f2[0] + free[48:72]
    for i in range(4):
        force2[24 * i : 24 * (i + 1)] = f2[i]
    u3 = [2.0 * u2[i] + drive * f2[i] for i in range(4)] + [stiff * c for c in c2]
    u3[0] = u3[0] - u1[0]
    u3[1] = u3[1] - u1[1]
    gram(u3, masked([curve(x) for x in u3]))

    count = len(totals)
    stack = jnp.concatenate(totals + [jnp.zeros((56 - count, 128), jnp.float32)], axis=0)
    column = jnp.sum(stack, axis=1, keepdims=True)
    diagonal = jnp.where(sublanes((56, 128)) == lanes((56, 128)), column, 0.0)
    sums[...] = jnp.sum(diagonal, axis=0, keepdims=True)


def quadratic(sums, at, monos):
    total = 0.0
    for i in range(len(monos)):
        for j in range(i, len(monos)):
            term = monos[i] * (sums(at) * monos[j])
            total = total + (term if i == j else 2.0 * term)
            at += 1
    return total


def finish_kernel(
    share0, share1, share2, share3, air_row, start, mono1, mono2, force2, force3, source0, source1, next_in, last_in,
    out_next, out_last, out_u, out_w, plane_next, plane_last, fields, wide_rows, turned, listed, sems,
):
    wide = lax.axis_index("gy")
    reached = (wide >= FIRST) & (wide <= LAST)
    loaded = pltpu.make_async_copy(air_row, listed, sems.at[4])
    loaded.start()
    loads = [
        pltpu.make_async_copy(next_in.at[:, :, MID - 128 : MID + 128], plane_next, sems.at[0]),
        pltpu.make_async_copy(last_in.at[:, :, MID - 128 : MID + 128], plane_last, sems.at[1]),
    ]

    @pl.when(reached)
    def _():
        for copy in loads:
            copy.start()

    def tension(energy):
        return 1.0 + BERGER * energy / NODES

    def sums(at):
        return (share0[0, at] + share1[0, at]) + (share2[0, at] + share3[0, at])

    t0 = tension(sums(0))
    t1 = tension(quadratic(sums, 1, [1.0, t0]))
    four = [1.0, t0, t1, t0 * t1]
    t2 = tension(quadratic(sums, 4, four))
    t3 = tension(quadratic(sums, 14, four + [t2 * x for x in four]))

    def mixed(ref, factors):
        total = ref[0:24]
        for i in range(1, len(factors)):
            total = total + factors[i] * ref[24 * i : 24 * (i + 1)]
        return total

    loaded.wait()
    chooser = chooser_of(listed)
    m0 = start[24:48]
    drive, stiff = FORCE * m0, SPEED * m0
    u1 = mixed(mono1, four[:2])
    u2 = mixed(mono2, four)
    a2 = stiff * (t2 * curve(u2)) + drive * mixed(force2, four)
    u3 = 2.0 * u2 - u1 + a2
    s0 = mixed(source0, four[:2])
    s1 = mixed(source1, four)
    s2 = to_rows(a2, chooser)
    within = inside((XE, WINDOW))

    def spread(x):
        return jnp.where(within, beside(x), 0.0)

    g1 = SOURCE * s0
    g2 = [SOURCE * s1 + (2.0 - 7.0 * COURANT) * g1 + COURANT * spread(g1), COURANT * g1]
    g3 = [
        SOURCE * s2 + (2.0 - 7.0 * COURANT) * g2[0] - g1 + COURANT * (spread(g2[0]) + g2[1]),
        (2.0 - 6.0 * COURANT) * g2[1] + COURANT * (spread(g2[1]) + g2[0]),
        COURANT * g2[1],
    ]
    f3 = to_columns(-2.0 * g3[0], chooser)
    a3 = stiff * (t3 * curve(u3)) + drive * (f3 + force3[...])
    u4 = 2.0 * u3 - u2 + a3

    tile = pl.ds(pl.multiple_of(128 * (wide // 4), 128), 128)
    back = lax.rem(128 - 32 * lax.rem(wide, 4), 128)
    fields[0:24] = u4
    fields[24:48] = u3
    out_u[...] = pltpu.roll(fields[4:20, tile], back, 1)[:, 0:BY]
    out_w[...] = pltpu.roll(fields[28:44, tile], back, 1)[:, 0:BY]

    @pl.when(reached)
    def _():
        s3 = to_rows(a3, chooser)
        g4 = [
            SOURCE * s3 + (2.0 - 7.0 * COURANT) * g3[0] - g2[0] + COURANT * (spread(g3[0]) + g3[1]),
            (2.0 - 6.0 * COURANT) * g3[1] - g2[1] + COURANT * (spread(g3[1]) + g3[0] + g3[2]),
            (2.0 - 6.0 * COURANT) * g3[2] + COURANT * (spread(g3[2]) + g3[1]),
            COURANT * g3[2],
        ]
        tile = pl.ds(pl.multiple_of(128 * (wide // 4 - ROW0 // 128), 128), 128)
        for copy in loads:
            copy.wait()
        for gains, plane in ((g4, plane_next), (g3 + [None], plane_last)):
            for k in range(4):
                if gains[k] is None:
                    turned[pl.ds(k, BX, stride=8), :] = jnp.zeros((BX, 128), jnp.float32)
                    turned[pl.ds(7 - k, BX, stride=8), :] = jnp.zeros((BX, 128), jnp.float32)
                    continue
                wide_rows[...] = gains[k]
                part = pltpu.roll(wide_rows[4:20, tile], back, 1)
                turned[pl.ds(k, BX, stride=8), :] = part
                turned[pl.ds(7 - k, BX, stride=8), :] = -part
            across = jnp.transpose(turned[...])[0:BY]
            lane = lanes((BY, 128))
            for x in range(BX):
                above = jnp.where(lane < 4, pltpu.roll(across, (128 - 8 * x) % 128, 1), 0.0)
                below = jnp.where(lane >= 124, pltpu.roll(across, (120 - 8 * x) % 128, 1), 0.0)
                plane[x, :, 0:128] = plane[x, :, 0:128] + below
                plane[x, :, 128:256] = plane[x, :, 128:256] + above
        stores = [
            pltpu.make_async_copy(plane_next, out_next.at[:, :, MID - 128 : MID + 128], sems.at[2]),
            pltpu.make_async_copy(plane_last, out_last.at[:, :, MID - 128 : MID + 128], sems.at[3]),
        ]
        for copy in stores:
            copy.start()
        for copy in stores:
            copy.wait()


def ring(count, by):
    return [(i, (i + by) % count) for i in range(count)]


def across(count, by):
    return [(i, (i + 2 * by) % count if by else i ^ 1) for i in range(count)]


def per_device(air_now, air_prev, membrane_now, membrane_prev, inv_mass, air_row):
    def sems(n):
        return pltpu.SemaphoreType.DMA((n,))

    halo_x, halo_y, corner, stripe = f32(7, BY, NZ), f32(BX, 8, NZ), f32(8, 8, NZ), f32(28, COLS)
    *sends, block = pl.pallas_call(
        pack_kernel,
        out_shape=(halo_x, halo_x, halo_y, halo_y, f32(GY, FOLD, 128)),
        in_specs=[HBM] * 5,
        out_specs=(HBM,) * 5,
        scratch_shapes=[
            VMEM((4, BX, 8, NZ), jnp.float32),
            VMEM((2, BX, 8, NZ), jnp.float32),
            VMEM((2, 7, BY, NZ), jnp.float32),
            VMEM((GY, FOLD, 128), jnp.float32),
            VMEM((2, BX, BY, 256), jnp.float32),
            VMEM((3, BX, BY), jnp.float32),
            VMEM((2, 128, 128), jnp.float32),
            VMEM((PACK, 128), jnp.float32),
            sems(18),
        ],
        compiler_params=granted(63),
        name="pack",
    )(air_now, air_prev, membrane_now, membrane_prev, inv_mass)
    blocks = lax.all_to_all(block, "gy", 0, 0)
    to_xlow, to_xhigh, to_ylow, to_yhigh = sends
    xlow = lax.ppermute(to_xhigh, "gx", ring(GX, 1))
    xhigh = lax.ppermute(to_xlow, "gx", ring(GX, -1))
    ylow = lax.ppermute(to_yhigh, "gy", ring(GY, 1))
    yhigh = lax.ppermute(to_ylow, "gy", ring(GY, -1))
    to_clow, to_chigh = pl.pallas_call(
        corner_kernel,
        out_shape=(corner, corner),
        in_specs=[WHOLE] * 2,
        out_specs=(WHOLE,) * 2,
        compiler_params=granted(3),
        name="corners",
    )(xlow, xhigh)
    clow = lax.ppermute(to_chigh, "gy", ring(GY, 1))
    chigh = lax.ppermute(to_clow, "gy", ring(GY, -1))
    air = f32(BX, BY, NZ)
    brick = VMEM((4, XE, YE, 128), jnp.float32)
    next_free, last_free, done = pl.pallas_call(
        air_kernel,
        out_shape=(air, air, f32(8, 128)),
        in_specs=[HBM, HBM] + [WHOLE] * 6,
        out_specs=(HBM, HBM, WHOLE),
        scratch_shapes=[brick, brick, sems(16)],
        compiler_params=granted(8),
        cost_estimate=pl.CostEstimate(flops=40_000_000, bytes_accessed=8_000_000, transcendentals=0),
        name="air_free",
    )(air_now, air_prev, xlow, xhigh, ylow, yhigh, clow, chigh)
    members, jumps, to_low, to_high = pl.pallas_call(
        unfold_kernel,
        out_shape=(f32(48, COLS), f32(112, WINDOW), stripe, stripe),
        in_specs=[WHOLE, ANY],
        out_specs=(WHOLE,) * 4,
        compiler_params=granted(3),
        name="unfold",
    )(blocks, done)
    hlow = lax.ppermute(to_high, "gx", ring(GX, 1))
    hhigh = lax.ppermute(to_low, "gx", ring(GX, -1))
    listed = air_row.reshape(1, COLS)
    sums, *saved = pl.pallas_call(
        membrane_kernel,
        out_shape=(
            f32(1, 128), f32(48, COLS), f32(48, COLS), f32(96, COLS), f32(96, COLS), f32(24, COLS),
            f32(48, WINDOW), f32(96, WINDOW),
        ),
        in_specs=[WHOLE] * 4 + [HBM],
        out_specs=(WHOLE,) * 8,
        scratch_shapes=[
            VMEM((3 * XE, COLS), jnp.float32),
            VMEM((7 * XE, WINDOW), jnp.float32),
            VMEM((1, COLS), jnp.int32),
            sems(1),
        ],
        compiler_params=granted(10),
        name="membrane",
    )(members, jumps, hlow, hhigh, listed)
    sums = sums + lax.ppermute(sums, "gx", across(GX, 0))
    shares = [sums] + [lax.ppermute(sums, "gx", across(GX, by)) for by in (1, 2, 3)]
    return pl.pallas_call(
        finish_kernel,
        out_shape=(air, air, f32(BX, BY), f32(BX, BY)),
        in_specs=[pl.BlockSpec(memory_space=pltpu.SMEM)] * 4 + [HBM] + [WHOLE] * 7 + [HBM, HBM],
        out_specs=(HBM, HBM, WHOLE, WHOLE),
        scratch_shapes=[
            VMEM((BX, BY, 256), jnp.float32),
            VMEM((BX, BY, 256), jnp.float32),
            VMEM((48, COLS), jnp.float32),
            VMEM((XE, WINDOW), jnp.float32),
            VMEM((128, 128), jnp.float32),
            VMEM((1, COLS), jnp.int32),
            sems(5),
        ],
        input_output_aliases={12: 0, 13: 1},
        compiler_params=granted(8),
        name="finish",
    )(*shares, listed, *saved, next_free, last_free)


def solution(mesh):
    in_specs = (
        P("gx", "gy", None),
        P("gx", "gy", None),
        P("gx", "gy"),
        P("gx", "gy"),
        P("gx", "gy"),
        P(),
    )
    out_specs = (P("gx", "gy", None), P("gx", "gy", None), P("gx", "gy"), P("gx", "gy"))
    return jax.shard_map(
        per_device, mesh=mesh, in_specs=in_specs, out_specs=out_specs, check_vma=False
    )
```

```python
import functools

import jax
import jax.numpy as jnp
from jax import lax
from jax.experimental import pallas as pl
from jax.experimental.pallas import tpu as pltpu
from jax.sharding import PartitionSpec as P

COURANT = 0.32
SPEED = 0.08
BERGER = 0.4
FORCE = 0.1
SOURCE = 0.5

GX, GY = 8, 32
BX, BY, NZ = 16, 32, 512
MID = NZ // 2
COLS = GY * BY
NODES = GX * BX * COLS
HALO = 4
XE = BX + 2 * HALO
YE = BY + 16
WINDOW = 384
ROW0 = COLS - WINDOW
FIRST, LAST = 22, 30
PACK = 160
FOLD = 40

VMEM = pltpu.VMEM
WHOLE = pl.BlockSpec(memory_space=pltpu.VMEM)
ANY = pl.BlockSpec(memory_space=pl.ANY)
HBM = pl.BlockSpec(memory_space=pltpu.HBM)


def granted(mib):
    return pltpu.CompilerParams(vmem_limit_bytes=mib * 1024 * 1024)


def f32(*shape):
    return jax.ShapeDtypeStruct(shape, jnp.float32)


def lanes(shape):
    return lax.broadcasted_iota(jnp.int32, shape, len(shape) - 1)


def sublanes(shape):
    return lax.broadcasted_iota(jnp.int32, shape, len(shape) - 2)


def fold(rows, wide):
    quarter = lanes((FOLD, 128)) // 32
    folded = rows[0:FOLD, :]
    for g in range(1, 4):
        folded = jnp.where(quarter == g, pltpu.roll(rows[FOLD * g : FOLD * (g + 1), :], 32 * g, 1), folded)
    return pltpu.roll(folded, 32 * lax.rem(wide, 4), 1)


def pack_kernel(
    p, q, u, w, m, xlow, xhigh, block,
    tips, copied, planes, members, turned, rows, sems,
):
    wide = lax.axis_index("gy")

    def started(pairs, at):
        copies = [pltpu.make_async_copy(x, y, sems.at[at + i]) for i, (x, y) in enumerate(pairs)]
        for copy in copies:
            copy.start()
        return copies

    mids = started([(x.at[:, :, MID - 128 : MID + 128], planes.at[i]) for i, x in enumerate((p, q))], 0)
    own = started([(x, members.at[i]) for i, x in enumerate((u, w, m))], 2)
    ends = started(
        [
            (p.at[0:4], tips.at[0, 0:4]),
            (q.at[0:3], tips.at[0, 4:7]),
            (p.at[12:16], tips.at[1, 0:4]),
            (q.at[13:16], tips.at[1, 4:7]),
        ],
        5,
    )
    lane = lanes((BY, 128))
    for i in range(2):
        mids[i].wait()
        total = jnp.zeros((BY, 128), jnp.float32)
        for x in range(BX):
            above = pltpu.roll(planes[i, x, :, 128:256], 8 * x, 1)
            below = pltpu.roll(planes[i, x, :, 0:128], (8 * x + 8) % 128, 1)
            total = jnp.where((lane >= 8 * x) & (lane < 8 * x + 4), above, total)
            total = jnp.where((lane >= 8 * x + 4) & (lane < 8 * x + 8), below, total)
        turned[i, 0:BY, :] = total
        turned[i, BY:128, :] = jnp.zeros((128 - BY, 128), jnp.float32)
        turned[i] = jnp.transpose(turned[i])
        for k in range(4 - i):
            at = 48 + 64 * i + 16 * k
            rows[at : at + 16, :] = turned[i, pl.ds(7 - k, BX, stride=8), :] - turned[i, pl.ds(k, BX, stride=8), :]
    for i in range(3):
        own[i].wait()
        rows[16 * i : 16 * i + 16, 0:BY] = members[i]
    folded = fold(rows, wide)
    for i in range(GY):
        copied[i] = folded
    sent = started([(copied, block)], 9)
    for copy in ends:
        copy.wait()
    sent += started([(tips.at[0], xlow), (tips.at[1], xhigh)], 10)
    for copy in sent:
        copy.wait()


def sides_kernel(p, q, xlow, xhigh, ylow, yhigh):
    lower = sublanes((8, NZ)) < 4

    def row(r, pt, qt):
        ylow[r] = jnp.where(lower, pt[0:8], pltpu.roll(qt[0:8], 4, 0))
        yhigh[r] = jnp.where(lower, pltpu.roll(qt[24:32], 4, 0), pt[24:32])

    for r in range(BX):
        row(4 + r, p.at[r], q.at[r])
    for i in range(4):
        row(i, xlow.at[i], xlow.at[4 + max(i - 1, 0)])
        row(20 + i, xhigh.at[i], xhigh.at[4 + min(i, 2)])


def unfold_kernel(blocks, members, jumps, to_low, to_high):
    quarter = lanes((FOLD, 128)) // 32
    for g in range(4):
        for t in range(8):
            if g >= 2 and t < 5:
                continue
            merged = blocks[4 * t + (-g) % 4]
            for s in range(1, 4):
                merged = jnp.where(quarter == s, blocks[4 * t + (s - g) % 4], merged)
            merged = pltpu.roll(merged, (128 - 32 * g) % 128, 1)
            column = slice(128 * t, 128 * (t + 1))
            narrow = slice(128 * (t - 5), 128 * (t - 4))
            if g == 0:
                members[0:40, column] = merged
            elif g == 1:
                members[40:48, column] = merged[0:8]
                if t >= 5:
                    jumps[0:32, narrow] = merged[8:40]
            else:
                jumps[40 * g - 48 : 40 * g - 8, narrow] = merged
    for out, at in ((to_low, 0), (to_high, 12)):
        for i in range(3):
            out[4 * i : 4 * i + 4, :] = members[16 * i + at : 16 * i + at + 4, :]
        for k in range(4):
            out[12 + 4 * k : 16 + 4 * k, 0:WINDOW] = jumps[16 * k + at : 16 * k + at + 4, :]
        for k in range(3):
            out[12 + 4 * k : 16 + 4 * k, 512 : 512 + WINDOW] = jumps[64 + 16 * k + at : 68 + 16 * k + at, :]


def edge_free(shape, edge):
    return jnp.broadcast_to(edge.astype(jnp.int32), shape) == 0


def air_kernel(p, q, xlow, xhigh, ylow, yhigh, out_next, out_last, a, b, sems):
    tall = lax.axis_index("gx")
    wide = lax.axis_index("gy")
    first, last = tall == 0, tall == GX - 1
    bottom, top = wide == 0, wide == GY - 1
    layers = [slice(128 * k, 128 * (k + 1)) for k in range(4)]
    copies = []
    for k in range(4):
        copies.append(pltpu.make_async_copy(p.at[:, :, layers[k]], a.at[k, 4:20, 8:40], sems.at[k]))
        copies.append(pltpu.make_async_copy(q.at[:, :, layers[k]], b.at[k, 4:20, 8:40], sems.at[4 + k]))
    for copy in copies:
        copy.start()
    inner_low, inner_high = edge_free((BY, 128), first), edge_free((BY, 128), last)
    tile_low, tile_high = edge_free((8, 128), bottom), edge_free((8, 128), top)
    for k in range(4):
        for i in range(4):
            a[k, i, 8:40] = jnp.where(inner_low, xlow[i, :, layers[k]], 0.0)
            a[k, 20 + i, 8:40] = jnp.where(inner_high, xhigh[i, :, layers[k]], 0.0)
        for i in range(3):
            b[k, 1 + i, 8:40] = jnp.where(inner_low, xlow[4 + i, :, layers[k]], 0.0)
            b[k, 20 + i, 8:40] = jnp.where(inner_high, xhigh[4 + i, :, layers[k]], 0.0)
        for r in range(XE):
            lo, hi = ylow[r, :, layers[k]], yhigh[r, :, layers[k]]
            if r < 4 or r >= 20:
                free = (inner_low if r < 4 else inner_high)[0:8]
                lo = jnp.where(free, lo, 0.0)
                hi = jnp.where(free, hi, 0.0)
            lo = jnp.where(tile_low, lo, 0.0)
            hi = jnp.where(tile_high, hi, 0.0)
            a[k, r, 0:8] = lo
            a[k, r, 40:48] = hi
            b[k, r, 0:8] = pltpu.roll(lo, 4, 0)
            b[k, r, 40:48] = pltpu.roll(hi, 4, 0)
    for copy in copies:
        copy.wait()

    lane = lanes((8, 128))

    def advance(now, old, r, tile):
        at = 8 * tile
        c = [now[k, r, at : at + 8] for k in range(4)]
        up = [pltpu.roll(x, 1, 1) for x in c]
        down = [pltpu.roll(x, 127, 1) for x in c]
        for k in range(4):
            left = jnp.where(lane == 0, up[k - 1] if k else 0.0, up[k])
            right = jnp.where(lane == 127, down[k + 1] if k < 3 else 0.0, down[k])
            if tile > 0:
                before = now[k, r, at - 1 : at + 7]
            else:
                before = pltpu.roll(c[k], 1, 0)
            if tile < 5:
                after = now[k, r, at + 1 : at + 9]
            else:
                after = pltpu.roll(c[k], 7, 0)
            ring = (left + right) + (before + after) + (now[k, r - 1, at : at + 8] + now[k, r + 1, at : at + 8])
            new = (2.0 - 6.0 * COURANT) * c[k] - old[k, r, at : at + 8] + COURANT * ring
            if tile == 0:
                new = jnp.where(tile_low, new, 0.0)
            if tile == 5:
                new = jnp.where(tile_high, new, 0.0)
            old[k, r, at : at + 8] = new

    def results(x, out, at):
        return [pltpu.make_async_copy(x.at[k, 4:20, 8:40], out.at[:, :, layers[k]], sems.at[at + k]) for k in range(4)]

    for t in range(4):
        now, old = (a, b) if t % 2 == 0 else (b, a)

        def row(r):
            for tile in range(6) if t < 3 else range(1, 5):
                advance(now, old, r, tile)

        if t < 3:

            @pl.when(jnp.logical_not(first))
            def _():
                for r in range(t + 1, 4):
                    row(r)

        def body(i, carry):
            for r in range(8):
                row(4 + 8 * i + r)
            return carry

        lax.fori_loop(0, 2, body, 0)
        if t < 3:

            @pl.when(jnp.logical_not(last))
            def _():
                for r in range(20, XE - 1 - t):
                    row(r)

        if t == 2:
            sent = results(b, out_last, 8)
            for copy in sent:
                copy.start()
    sent = sent + results(a, out_next, 12)
    for copy in sent[4:]:
        copy.start()
    for copy in sent:
        copy.wait()


def split(x):
    high = x.astype(jnp.bfloat16)
    low = (x - high.astype(jnp.float32)).astype(jnp.bfloat16)
    return jnp.concatenate([high, low], axis=0)


def to_columns(x, chooser):
    n = x.shape[0]
    both = lax.dot_general(split(x), chooser, (((1,), (0,)), ((), ())), preferred_element_type=jnp.float32)
    return both[0:n] + both[n : 2 * n]


def to_rows(x, chooser):
    n = x.shape[0]
    both = lax.dot_general(split(x), chooser, (((1,), (1,)), ((), ())), preferred_element_type=jnp.float32)
    return both[0:n] + both[n : 2 * n]


def chooser_of(air_row):
    rows = lax.broadcasted_iota(jnp.int32, (WINDOW, COLS), 0) + ROW0
    return jnp.where(rows == air_row[...], 1.0, 0.0).astype(jnp.bfloat16)


def beside(field):
    n = field.shape[1]
    lane = lanes(field.shape)
    left = jnp.where(lane == 0, 0.0, pltpu.roll(field, 1, 1))
    right = jnp.where(lane == n - 1, 0.0, pltpu.roll(field, n - 1, 1))
    return left + right + pltpu.roll(field, 1, 0) + pltpu.roll(field, field.shape[0] - 1, 0)


def curve(field):
    return beside(field) - 4.0 * field


def inside(shape):
    tall = lax.axis_index("gx")
    row = sublanes(shape)
    low = jnp.where(tall == 0, 4, 0)
    high = jnp.where(tall == GX - 1, 20, 24)
    return (row >= low) & (row < high)


def membrane_kernel(
    members, jumps, hlow, hhigh, air_row, sums, start, mono1, mono2, force2, force3, source0, source1, parts, slab, listed, sems
):
    tall = lax.axis_index("gx")
    loaded = pltpu.make_async_copy(air_row, listed, sems.at[0])
    loaded.start()
    for i in range(3):
        at = XE * i
        parts[at : at + 4] = jnp.where(edge_free((4, COLS), tall == 0), hlow[4 * i : 4 * i + 4, :], 0.0)
        parts[at + 4 : at + 20] = members[16 * i : 16 * i + 16]
        parts[at + 20 : at + 24] = jnp.where(edge_free((4, COLS), tall == GX - 1), hhigh[4 * i : 4 * i + 4, :], 0.0)
    for i in range(7):
        at, row = XE * i, 12 + 4 * (i % 4)
        narrow = slice(512 * (i // 4), 512 * (i // 4) + WINDOW)
        slab[at : at + 4] = jnp.where(edge_free((4, WINDOW), tall == 0), hlow[row : row + 4, narrow], 0.0)
        slab[at + 4 : at + 20] = jumps[16 * i : 16 * i + 16]
        slab[at + 20 : at + 24] = jnp.where(edge_free((4, WINDOW), tall == GX - 1), hhigh[row : row + 4, narrow], 0.0)
    within = inside((XE, WINDOW))

    def spread(x):
        return jnp.where(within, beside(x), 0.0)

    older = [slab[96 + XE * k : 96 + XE * (k + 1)] for k in range(3)] + [None]
    newer = [slab[XE * k : XE * (k + 1)] for k in range(4)]
    free = [newer[0]]
    for t in range(3):
        step = []
        for k in range(3 - t):
            own = 2.0 - (7.0 if k == 0 else 6.0) * COURANT
            ring = spread(newer[k]) + newer[k + 1]
            if k:
                ring = ring + newer[k - 1]
            step.append(own * newer[k] - older[k] + COURANT * ring)
        older, newer = newer, step
        free.append(newer[0])
    loaded.wait()
    chooser = chooser_of(listed)
    u0, w0, m0 = parts[0:24], parts[24:48], parts[48:72]
    start[0:24] = u0
    start[24:48] = m0
    free = to_columns(jnp.concatenate(free, axis=0), chooser)
    force3[...] = free[72:96]
    drive, stiff = FORCE * m0, SPEED * m0
    row = sublanes((XE, COLS))
    mine = (row >= HALO) & (row < HALO + BX)
    totals = []

    def gram(fields, curves):
        for i in range(len(fields)):
            for j in range(i, len(fields)):
                product = fields[i] * curves[j]
                part = product[:, 0:128]
                for k in range(1, COLS // 128):
                    part = part + product[:, 128 * k : 128 * (k + 1)]
                totals.append(jnp.sum(part, axis=0, keepdims=True))

    def masked(curves):
        return [jnp.where(mine, -c, 0.0) for c in curves]

    c0 = curve(u0)
    gram([u0], masked([c0]))
    a0 = [drive * free[0:24], stiff * c0]
    u1 = [2.0 * u0 - w0 + a0[0], a0[1]]
    mono1[0:24] = u1[0]
    mono1[24:48] = u1[1]
    c1 = [curve(x) for x in u1]
    gram(u1, masked(c1))
    s0 = to_rows(jnp.concatenate(a0, axis=0), chooser)
    source0[...] = s0
    f1 = to_columns(-s0, chooser)
    a1 = [drive * (free[24:48] + f1[0:24]), drive * f1[24:48], stiff * c1[0], stiff * c1[1]]
    u2 = [2.0 * u1[0] - u0 + a1[0], 2.0 * u1[1] + a1[1], a1[2], a1[3]]
    for i in range(4):
        mono2[24 * i : 24 * (i + 1)] = u2[i]
    c2 = [curve(x) for x in u2]
    gram(u2, masked(c2))
    s1 = to_rows(jnp.concatenate(a1, axis=0), chooser)
    source1[...] = s1
    jump2 = []
    for i in range(4):
        half = SOURCE * s1[24 * i : 24 * (i + 1)]
        if i < 2:
            g1 = SOURCE * s0[24 * i : 24 * (i + 1)]
            half = half + (2.0 - 7.0 * COURANT) * g1 + COURANT * spread(g1)
        jump2.append(-2.0 * half)
    f2 = to_columns(jnp.concatenate(jump2, axis=0), chooser)
    f2 = [f2[24 * i : 24 * (i + 1)] for i in range(4)]
    f2[0] = f2[0] + free[48:72]
    for i in range(4):
        force2[24 * i : 24 * (i + 1)] = f2[i]
    u3 = [2.0 * u2[i] + drive * f2[i] for i in range(4)] + [stiff * c for c in c2]
    u3[0] = u3[0] - u1[0]
    u3[1] = u3[1] - u1[1]
    gram(u3, masked([curve(x) for x in u3]))

    count = len(totals)
    stack = jnp.concatenate(totals + [jnp.zeros((56 - count, 128), jnp.float32)], axis=0)
    column = jnp.sum(stack, axis=1, keepdims=True)
    diagonal = jnp.where(sublanes((56, 128)) == lanes((56, 128)), column, 0.0)
    sums[...] = jnp.sum(diagonal, axis=0, keepdims=True)


def quadratic(sums, at, monos):
    total = 0.0
    for i in range(len(monos)):
        for j in range(i, len(monos)):
            term = monos[i] * (sums(at) * monos[j])
            total = total + (term if i == j else 2.0 * term)
            at += 1
    return total


def finish_kernel(
    share0, share1, share2, share3, air_row, start, mono1, mono2, force2, force3, source0, source1, next_in, last_in,
    out_next, out_last, out_u, out_w, plane_next, plane_last, fields, wide_rows, turned, listed, sems,
):
    wide = lax.axis_index("gy")
    reached = (wide >= FIRST) & (wide <= LAST)
    loaded = pltpu.make_async_copy(air_row, listed, sems.at[4])
    loaded.start()
    loads = [
        pltpu.make_async_copy(next_in.at[:, :, MID - 128 : MID + 128], plane_next, sems.at[0]),
        pltpu.make_async_copy(last_in.at[:, :, MID - 128 : MID + 128], plane_last, sems.at[1]),
    ]

    @pl.when(reached)
    def _():
        for copy in loads:
            copy.start()

    def tension(energy):
        return 1.0 + BERGER * energy / NODES

    def sums(at):
        return (share0[0, at] + share1[0, at]) + (share2[0, at] + share3[0, at])

    t0 = tension(sums(0))
    t1 = tension(quadratic(sums, 1, [1.0, t0]))
    four = [1.0, t0, t1, t0 * t1]
    t2 = tension(quadratic(sums, 4, four))
    t3 = tension(quadratic(sums, 14, four + [t2 * x for x in four]))

    def mixed(ref, factors):
        total = ref[0:24]
        for i in range(1, len(factors)):
            total = total + factors[i] * ref[24 * i : 24 * (i + 1)]
        return total

    loaded.wait()
    chooser = chooser_of(listed)
    m0 = start[24:48]
    drive, stiff = FORCE * m0, SPEED * m0
    u1 = mixed(mono1, four[:2])
    u2 = mixed(mono2, four)
    a2 = stiff * (t2 * curve(u2)) + drive * mixed(force2, four)
    u3 = 2.0 * u2 - u1 + a2
    s0 = mixed(source0, four[:2])
    s1 = mixed(source1, four)
    s2 = to_rows(a2, chooser)
    within = inside((XE, WINDOW))

    def spread(x):
        return jnp.where(within, beside(x), 0.0)

    g1 = SOURCE * s0
    g2 = [SOURCE * s1 + (2.0 - 7.0 * COURANT) * g1 + COURANT * spread(g1), COURANT * g1]
    g3 = [
        SOURCE * s2 + (2.0 - 7.0 * COURANT) * g2[0] - g1 + COURANT * (spread(g2[0]) + g2[1]),
        (2.0 - 6.0 * COURANT) * g2[1] + COURANT * (spread(g2[1]) + g2[0]),
        COURANT * g2[1],
    ]
    f3 = to_columns(-2.0 * g3[0], chooser)
    a3 = stiff * (t3 * curve(u3)) + drive * (f3 + force3[...])
    u4 = 2.0 * u3 - u2 + a3

    tile = pl.ds(pl.multiple_of(128 * (wide // 4), 128), 128)
    back = lax.rem(128 - 32 * lax.rem(wide, 4), 128)
    fields[0:24] = u4
    fields[24:48] = u3
    out_u[...] = pltpu.roll(fields[4:20, tile], back, 1)[:, 0:BY]
    out_w[...] = pltpu.roll(fields[28:44, tile], back, 1)[:, 0:BY]

    @pl.when(reached)
    def _():
        s3 = to_rows(a3, chooser)
        g4 = [
            SOURCE * s3 + (2.0 - 7.0 * COURANT) * g3[0] - g2[0] + COURANT * (spread(g3[0]) + g3[1]),
            (2.0 - 6.0 * COURANT) * g3[1] - g2[1] + COURANT * (spread(g3[1]) + g3[0] + g3[2]),
            (2.0 - 6.0 * COURANT) * g3[2] + COURANT * (spread(g3[2]) + g3[1]),
            COURANT * g3[2],
        ]
        tile = pl.ds(pl.multiple_of(128 * (wide // 4 - ROW0 // 128), 128), 128)
        for copy in loads:
            copy.wait()
        for gains, plane in ((g4, plane_next), (g3 + [None], plane_last)):
            for k in range(4):
                if gains[k] is None:
                    turned[pl.ds(k, BX, stride=8), :] = jnp.zeros((BX, 128), jnp.float32)
                    turned[pl.ds(7 - k, BX, stride=8), :] = jnp.zeros((BX, 128), jnp.float32)
                    continue
                wide_rows[...] = gains[k]
                part = pltpu.roll(wide_rows[4:20, tile], back, 1)
                turned[pl.ds(k, BX, stride=8), :] = part
                turned[pl.ds(7 - k, BX, stride=8), :] = -part
            across = jnp.transpose(turned[...])[0:BY]
            lane = lanes((BY, 128))
            for x in range(BX):
                above = jnp.where(lane < 4, pltpu.roll(across, (128 - 8 * x) % 128, 1), 0.0)
                below = jnp.where(lane >= 124, pltpu.roll(across, (120 - 8 * x) % 128, 1), 0.0)
                plane[x, :, 0:128] = plane[x, :, 0:128] + below
                plane[x, :, 128:256] = plane[x, :, 128:256] + above
        stores = [
            pltpu.make_async_copy(plane_next, out_next.at[:, :, MID - 128 : MID + 128], sems.at[2]),
            pltpu.make_async_copy(plane_last, out_last.at[:, :, MID - 128 : MID + 128], sems.at[3]),
        ]
        for copy in stores:
            copy.start()
        for copy in stores:
            copy.wait()


def ring(count, by):
    return [(i, (i + by) % count) for i in range(count)]


def across(count, by):
    return [(i, (i + 2 * by) % count if by else i ^ 1) for i in range(count)]


def per_device(air_now, air_prev, membrane_now, membrane_prev, inv_mass, air_row):
    def sems(n):
        return pltpu.SemaphoreType.DMA((n,))

    halo_x, halo_y, stripe = f32(7, BY, NZ), f32(XE, 8, NZ), f32(28, COLS)
    to_xlow, to_xhigh, block = pl.pallas_call(
        pack_kernel,
        out_shape=(halo_x, halo_x, f32(GY, FOLD, 128)),
        in_specs=[HBM] * 5,
        out_specs=(HBM,) * 3,
        scratch_shapes=[
            VMEM((2, 7, BY, NZ), jnp.float32),
            VMEM((GY, FOLD, 128), jnp.float32),
            VMEM((2, BX, BY, 256), jnp.float32),
            VMEM((3, BX, BY), jnp.float32),
            VMEM((2, 128, 128), jnp.float32),
            VMEM((PACK, 128), jnp.float32),
            sems(12),
        ],
        compiler_params=granted(63),
        name="pack",
    )(air_now, air_prev, membrane_now, membrane_prev, inv_mass)
    blocks = lax.all_to_all(block, "gy", 0, 0)
    xlow = lax.ppermute(to_xhigh, "gx", ring(GX, 1))
    xhigh = lax.ppermute(to_xlow, "gx", ring(GX, -1))
    members, jumps, to_low, to_high = pl.pallas_call(
        unfold_kernel,
        out_shape=(f32(48, COLS), f32(112, WINDOW), stripe, stripe),
        in_specs=[WHOLE],
        out_specs=(WHOLE,) * 4,
        compiler_params=granted(3),
        name="unfold",
    )(blocks)
    hlow = lax.ppermute(to_high, "gx", ring(GX, 1))
    hhigh = lax.ppermute(to_low, "gx", ring(GX, -1))
    to_ylow, to_yhigh = pl.pallas_call(
        sides_kernel,
        out_shape=(halo_y, halo_y),
        in_specs=[WHOLE] * 4,
        out_specs=(WHOLE,) * 2,
        compiler_params=granted(8),
        name="sides",
    )(air_now, air_prev, xlow, xhigh)
    ylow = lax.ppermute(to_yhigh, "gy", ring(GY, 1))
    yhigh = lax.ppermute(to_ylow, "gy", ring(GY, -1))
    air = f32(BX, BY, NZ)
    brick = VMEM((4, XE, YE, 128), jnp.float32)
    next_free, last_free = pl.pallas_call(
        air_kernel,
        out_shape=(air, air),
        in_specs=[HBM, HBM] + [WHOLE] * 4,
        out_specs=(HBM, HBM),
        scratch_shapes=[brick, brick, sems(16)],
        compiler_params=granted(8),
        cost_estimate=pl.CostEstimate(flops=40_000_000, bytes_accessed=8_000_000, transcendentals=0),
        name="air_free",
    )(air_now, air_prev, xlow, xhigh, ylow, yhigh)
    listed = air_row.reshape(1, COLS)
    sums, *saved = pl.pallas_call(
        membrane_kernel,
        out_shape=(
            f32(1, 128), f32(48, COLS), f32(48, COLS), f32(96, COLS), f32(96, COLS), f32(24, COLS),
            f32(48, WINDOW), f32(96, WINDOW),
        ),
        in_specs=[WHOLE] * 4 + [HBM],
        out_specs=(WHOLE,) * 8,
        scratch_shapes=[
            VMEM((3 * XE, COLS), jnp.float32),
            VMEM((7 * XE, WINDOW), jnp.float32),
            VMEM((1, COLS), jnp.int32),
            sems(1),
        ],
        compiler_params=granted(10),
        name="membrane",
    )(members, jumps, hlow, hhigh, listed)
    sums = sums + lax.ppermute(sums, "gx", across(GX, 0))
    shares = [sums] + [lax.ppermute(sums, "gx", across(GX, by)) for by in (1, 2, 3)]
    return pl.pallas_call(
        finish_kernel,
        out_shape=(air, air, f32(BX, BY), f32(BX, BY)),
        in_specs=[pl.BlockSpec(memory_space=pltpu.SMEM)] * 4 + [HBM] + [WHOLE] * 7 + [HBM, HBM],
        out_specs=(HBM, HBM, WHOLE, WHOLE),
        scratch_shapes=[
            VMEM((BX, BY, 256), jnp.float32),
            VMEM((BX, BY, 256), jnp.float32),
            VMEM((48, COLS), jnp.float32),
            VMEM((XE, WINDOW), jnp.float32),
            VMEM((128, 128), jnp.float32),
            VMEM((1, COLS), jnp.int32),
            sems(5),
        ],
        input_output_aliases={12: 0, 13: 1},
        compiler_params=granted(8),
        name="finish",
    )(*shares, listed, *saved, next_free, last_free)


def solution(mesh):
    in_specs = (
        P("gx", "gy", None),
        P("gx", "gy", None),
        P("gx", "gy"),
        P("gx", "gy"),
        P("gx", "gy"),
        P(),
    )
    out_specs = (P("gx", "gy", None), P("gx", "gy", None), P("gx", "gy"), P("gx", "gy"))
    return jax.shard_map(
        per_device, mesh=mesh, in_specs=in_specs, out_specs=out_specs, check_vma=False
    )
```

```python
import functools

import jax
import jax.numpy as jnp
from jax import lax
from jax.experimental import pallas as pl
from jax.experimental.pallas import tpu as pltpu
from jax.sharding import PartitionSpec as P

COURANT = 0.32
SPEED = 0.08
BERGER = 0.4
FORCE = 0.1
SOURCE = 0.5

GX, GY = 8, 32
BX, BY, NZ = 16, 32, 512
MID = NZ // 2
COLS = GY * BY
NODES = GX * BX * COLS
HALO = 4
XE = BX + 2 * HALO
YE = BY + 16
WINDOW = 384
ROW0 = COLS - WINDOW
FIRST, LAST = 22, 30
PACK = 160
FOLD = 40

VMEM = pltpu.VMEM
WHOLE = pl.BlockSpec(memory_space=pltpu.VMEM)
ANY = pl.BlockSpec(memory_space=pl.ANY)
HBM = pl.BlockSpec(memory_space=pltpu.HBM)


def granted(mib):
    return pltpu.CompilerParams(vmem_limit_bytes=mib * 1024 * 1024)


def f32(*shape):
    return jax.ShapeDtypeStruct(shape, jnp.float32)


def lanes(shape):
    return lax.broadcasted_iota(jnp.int32, shape, len(shape) - 1)


def sublanes(shape):
    return lax.broadcasted_iota(jnp.int32, shape, len(shape) - 2)


def fold(rows, wide):
    quarter = lanes((FOLD, 128)) // 32
    folded = rows[0:FOLD, :]
    for g in range(1, 4):
        folded = jnp.where(quarter == g, pltpu.roll(rows[FOLD * g : FOLD * (g + 1), :], 32 * g, 1), folded)
    return pltpu.roll(folded, 32 * lax.rem(wide, 4), 1)


def pack_kernel(
    p, q, u, w, m, xlow, xhigh, ylow, yhigh, block,
    edges, planes, members, turned, rows, sems,
):
    wide = lax.axis_index("gy")

    def started(pairs, at):
        copies = [pltpu.make_async_copy(x, y, sems.at[at + i]) for i, (x, y) in enumerate(pairs)]
        for copy in copies:
            copy.start()
        return copies

    mids = started([(x.at[:, :, MID - 128 : MID + 128], planes.at[i]) for i, x in enumerate((p, q))], 0)
    own = started([(x, members.at[i]) for i, x in enumerate((u, w, m))], 2)
    ins = started([(x.at[:, at : at + 8], edges.at[i]) for i, (x, at) in enumerate(((p, 0), (q, 0), (p, 24), (q, 24)))], 12)
    ends = started(
        [
            (p.at[0:4], xlow.at[0:4]),
            (q.at[0:3], xlow.at[4:7]),
            (p.at[12:16], xhigh.at[0:4]),
            (q.at[13:16], xhigh.at[4:7]),
        ],
        5,
    )
    lane = lanes((BY, 128))
    for i in range(2):
        mids[i].wait()
        total = jnp.zeros((BY, 128), jnp.float32)
        for x in range(BX):
            above = pltpu.roll(planes[i, x, :, 128:256], 8 * x, 1)
            below = pltpu.roll(planes[i, x, :, 0:128], (8 * x + 8) % 128, 1)
            total = jnp.where((lane >= 8 * x) & (lane < 8 * x + 4), above, total)
            total = jnp.where((lane >= 8 * x + 4) & (lane < 8 * x + 8), below, total)
        turned[i, 0:BY, :] = total
        turned[i, BY:128, :] = jnp.zeros((128 - BY, 128), jnp.float32)
        turned[i] = jnp.transpose(turned[i])
        for k in range(4 - i):
            at = 48 + 64 * i + 16 * k
            rows[at : at + 16, :] = turned[i, pl.ds(7 - k, BX, stride=8), :] - turned[i, pl.ds(k, BX, stride=8), :]
    for i in range(3):
        own[i].wait()
        rows[16 * i : 16 * i + 16, 0:BY] = members[i]
    folded = fold(rows, wide)
    for i in range(GY):
        block[i] = folded
    lower = sublanes((8, NZ)) < 4
    for copy in ins:
        copy.wait()
    for r in range(BX):
        ylow[r] = jnp.where(lower, edges[0, r], pltpu.roll(edges[1, r], 4, 0))
        yhigh[r] = jnp.where(lower, pltpu.roll(edges[3, r], 4, 0), edges[2, r])
    for copy in ends:
        copy.wait()


def corner_kernel(xlow, xhigh, own_low, own_high, out_ylow, out_yhigh, corners, sems):
    copies = [
        pltpu.make_async_copy(own, out.at[4:20], sems.at[4 + i])
        for i, (own, out) in enumerate(((own_low, out_ylow), (own_high, out_yhigh)))
    ]
    for copy in copies:
        copy.start()
    lower = sublanes((8, NZ)) < 4
    for i in range(4):
        for at, halo, j in ((0, xlow, 4 + max(i - 1, 0)), (1, xhigh, 4 + min(i, 2))):
            corners[0, at, i] = jnp.where(lower, halo[i, 0:8], pltpu.roll(halo[j, 0:8], 4, 0))
            corners[1, at, i] = jnp.where(lower, pltpu.roll(halo[j, 24:32], 4, 0), halo[i, 24:32])
    for i, out in enumerate((out_ylow, out_yhigh)):
        for at in range(2):
            copy = pltpu.make_async_copy(corners.at[i, at], out.at[20 * at : 20 * at + 4], sems.at[2 * i + at])
            copy.start()
            copies.append(copy)
    for copy in copies:
        copy.wait()


def unfold_kernel(blocks, members, jumps, to_low, to_high):
    quarter = lanes((FOLD, 128)) // 32
    for g in range(4):
        for t in range(8):
            if g >= 2 and t < 5:
                continue
            merged = blocks[4 * t + (-g) % 4]
            for s in range(1, 4):
                merged = jnp.where(quarter == s, blocks[4 * t + (s - g) % 4], merged)
            merged = pltpu.roll(merged, (128 - 32 * g) % 128, 1)
            column = slice(128 * t, 128 * (t + 1))
            narrow = slice(128 * (t - 5), 128 * (t - 4))
            if g == 0:
                members[0:40, column] = merged
            elif g == 1:
                members[40:48, column] = merged[0:8]
                if t >= 5:
                    jumps[0:32, narrow] = merged[8:40]
            else:
                jumps[40 * g - 48 : 40 * g - 8, narrow] = merged
    for out, at in ((to_low, 0), (to_high, 12)):
        for i in range(3):
            out[4 * i : 4 * i + 4, :] = members[16 * i + at : 16 * i + at + 4, :]
        for k in range(4):
            out[12 + 4 * k : 16 + 4 * k, 0:WINDOW] = jumps[16 * k + at : 16 * k + at + 4, :]
        for k in range(3):
            out[12 + 4 * k : 16 + 4 * k, 512 : 512 + WINDOW] = jumps[64 + 16 * k + at : 68 + 16 * k + at, :]


def edge_free(shape, edge):
    return jnp.broadcast_to(edge.astype(jnp.int32), shape) == 0


def air_kernel(p, q, xlow, xhigh, ylow, yhigh, out_next, out_last, a, b, sems):
    tall = lax.axis_index("gx")
    wide = lax.axis_index("gy")
    first, last = tall == 0, tall == GX - 1
    bottom, top = wide == 0, wide == GY - 1
    layers = [slice(128 * k, 128 * (k + 1)) for k in range(4)]
    pairs = []
    for k in range(4):
        z = layers[k]
        pairs += [
            (p.at[:, :, z], a.at[k, 4:20, 8:40]),
            (q.at[:, :, z], b.at[k, 4:20, 8:40]),
            (xlow.at[0:4, :, z], a.at[k, 0:4, 8:40]),
            (xlow.at[4:7, :, z], b.at[k, 1:4, 8:40]),
            (xhigh.at[0:4, :, z], a.at[k, 20:24, 8:40]),
            (xhigh.at[4:7, :, z], b.at[k, 20:23, 8:40]),
            (ylow.at[:, :, z], a.at[k, :, 0:8]),
            (yhigh.at[:, :, z], a.at[k, :, 40:48]),
        ]
    copies = [pltpu.make_async_copy(x, y, sems.at[i]) for i, (x, y) in enumerate(pairs)]
    for copy in copies:
        copy.start()
    for copy in copies:
        copy.wait()

    def cleared(edge, ref, at):
        @pl.when(edge)
        def _():
            for k in range(4):
                ref.at[(k, *at)][...] = jnp.zeros(ref.at[(k, *at)].shape, jnp.float32)

    cleared(first, a, (slice(0, 4),))
    cleared(first, b, (slice(1, 4),))
    cleared(last, a, (slice(20, 24),))
    cleared(last, b, (slice(20, 23),))
    cleared(bottom, a, (slice(0, XE), slice(0, 8)))
    cleared(top, a, (slice(0, XE), slice(40, 48)))
    for k in range(4):
        for r in range(1, XE - 1):
            b[k, r, 0:8] = pltpu.roll(a[k, r, 0:8], 4, 0)
            b[k, r, 40:48] = pltpu.roll(a[k, r, 40:48], 4, 0)

    tile_low, tile_high = edge_free((8, 128), bottom), edge_free((8, 128), top)
    lane = lanes((8, 128))

    def advance(now, old, r, tile):
        at = 8 * tile
        c = [now[k, r, at : at + 8] for k in range(4)]
        up = [pltpu.roll(x, 1, 1) for x in c]
        down = [pltpu.roll(x, 127, 1) for x in c]
        for k in range(4):
            left = jnp.where(lane == 0, up[k - 1] if k else 0.0, up[k])
            right = jnp.where(lane == 127, down[k + 1] if k < 3 else 0.0, down[k])
            if tile > 0:
                before = now[k, r, at - 1 : at + 7]
            else:
                before = pltpu.roll(c[k], 1, 0)
            if tile < 5:
                after = now[k, r, at + 1 : at + 9]
            else:
                after = pltpu.roll(c[k], 7, 0)
            ring = (left + right) + (before + after) + (now[k, r - 1, at : at + 8] + now[k, r + 1, at : at + 8])
            new = (2.0 - 6.0 * COURANT) * c[k] - old[k, r, at : at + 8] + COURANT * ring
            if tile == 0:
                new = jnp.where(tile_low, new, 0.0)
            if tile == 5:
                new = jnp.where(tile_high, new, 0.0)
            old[k, r, at : at + 8] = new

    sent = []

    def send(x, out, rows, at):
        for k in range(4):
            target = out.at[rows, :, layers[k]]
            copy = pltpu.make_async_copy(x.at[k, rows.start + 4 : rows.stop + 4, 8:40], target, sems.at[at + k])
            copy.start()
            sent.append(copy)

    for t in range(4):
        now, old = (a, b) if t % 2 == 0 else (b, a)

        def row(r):
            for tile in range(6) if t < 3 else range(1, 5):
                advance(now, old, r, tile)

        if t < 3:

            @pl.when(jnp.logical_not(first))
            def _():
                for r in range(t + 1, 4):
                    row(r)

        for r in range(4, 20):
            row(r)
            if t == 3 and r in (11, 19):
                send(a, out_next, slice(r - 11, r - 3), 36 + 4 * (r // 19))
        if t < 3:

            @pl.when(jnp.logical_not(last))
            def _():
                for r in range(20, XE - 1 - t):
                    row(r)

        if t == 2:
            send(b, out_last, slice(0, 16), 32)
    for copy in sent:
        copy.wait()


def split(x):
    high = x.astype(jnp.bfloat16)
    low = (x - high.astype(jnp.float32)).astype(jnp.bfloat16)
    return jnp.concatenate([high, low], axis=0)


def to_columns(x, chooser):
    n = x.shape[0]
    both = lax.dot_general(split(x), chooser, (((1,), (0,)), ((), ())), preferred_element_type=jnp.float32)
    return both[0:n] + both[n : 2 * n]


def to_rows(x, chooser):
    n = x.shape[0]
    both = lax.dot_general(split(x), chooser, (((1,), (1,)), ((), ())), preferred_element_type=jnp.float32)
    return both[0:n] + both[n : 2 * n]


def chooser_of(air_row):
    rows = lax.broadcasted_iota(jnp.int32, (WINDOW, COLS), 0) + ROW0
    return jnp.where(rows == air_row[...], 1.0, 0.0).astype(jnp.bfloat16)


def beside(field):
    n = field.shape[1]
    lane = lanes(field.shape)
    left = jnp.where(lane == 0, 0.0, pltpu.roll(field, 1, 1))
    right = jnp.where(lane == n - 1, 0.0, pltpu.roll(field, n - 1, 1))
    return left + right + pltpu.roll(field, 1, 0) + pltpu.roll(field, field.shape[0] - 1, 0)


def curve(field):
    return beside(field) - 4.0 * field


def inside(shape):
    tall = lax.axis_index("gx")
    row = sublanes(shape)
    low = jnp.where(tall == 0, 4, 0)
    high = jnp.where(tall == GX - 1, 20, 24)
    return (row >= low) & (row < high)


def membrane_kernel(
    members, jumps, hlow, hhigh, air_row, sums, start, mono1, mono2, force2, force3, source0, source1, parts, slab, listed, sems
):
    tall = lax.axis_index("gx")
    loaded = pltpu.make_async_copy(air_row, listed, sems.at[0])
    loaded.start()
    for i in range(3):
        at = XE * i
        parts[at : at + 4] = jnp.where(edge_free((4, COLS), tall == 0), hlow[4 * i : 4 * i + 4, :], 0.0)
        parts[at + 4 : at + 20] = members[16 * i : 16 * i + 16]
        parts[at + 20 : at + 24] = jnp.where(edge_free((4, COLS), tall == GX - 1), hhigh[4 * i : 4 * i + 4, :], 0.0)
    for i in range(7):
        at, row = XE * i, 12 + 4 * (i % 4)
        narrow = slice(512 * (i // 4), 512 * (i // 4) + WINDOW)
        slab[at : at + 4] = jnp.where(edge_free((4, WINDOW), tall == 0), hlow[row : row + 4, narrow], 0.0)
        slab[at + 4 : at + 20] = jumps[16 * i : 16 * i + 16]
        slab[at + 20 : at + 24] = jnp.where(edge_free((4, WINDOW), tall == GX - 1), hhigh[row : row + 4, narrow], 0.0)
    within = inside((XE, WINDOW))

    def spread(x):
        return jnp.where(within, beside(x), 0.0)

    older = [slab[96 + XE * k : 96 + XE * (k + 1)] for k in range(3)] + [None]
    newer = [slab[XE * k : XE * (k + 1)] for k in range(4)]
    free = [newer[0]]
    for t in range(3):
        step = []
        for k in range(3 - t):
            own = 2.0 - (7.0 if k == 0 else 6.0) * COURANT
            ring = spread(newer[k]) + newer[k + 1]
            if k:
                ring = ring + newer[k - 1]
            step.append(own * newer[k] - older[k] + COURANT * ring)
        older, newer = newer, step
        free.append(newer[0])
    loaded.wait()
    chooser = chooser_of(listed)
    u0, w0, m0 = parts[0:24], parts[24:48], parts[48:72]
    start[0:24] = u0
    start[24:48] = m0
    free = to_columns(jnp.concatenate(free, axis=0), chooser)
    force3[...] = free[72:96]
    drive, stiff = FORCE * m0, SPEED * m0
    row = sublanes((XE, COLS))
    mine = (row >= HALO) & (row < HALO + BX)
    totals = []

    def gram(fields, curves):
        for i in range(len(fields)):
            for j in range(i, len(fields)):
                product = fields[i] * curves[j]
                part = product[:, 0:128]
                for k in range(1, COLS // 128):
                    part = part + product[:, 128 * k : 128 * (k + 1)]
                totals.append(jnp.sum(part, axis=0, keepdims=True))

    def masked(curves):
        return [jnp.where(mine, -c, 0.0) for c in curves]

    c0 = curve(u0)
    gram([u0], masked([c0]))
    a0 = [drive * free[0:24], stiff * c0]
    u1 = [2.0 * u0 - w0 + a0[0], a0[1]]
    mono1[0:24] = u1[0]
    mono1[24:48] = u1[1]
    c1 = [curve(x) for x in u1]
    gram(u1, masked(c1))
    s0 = to_rows(jnp.concatenate(a0, axis=0), chooser)
    source0[...] = s0
    f1 = to_columns(-s0, chooser)
    a1 = [drive * (free[24:48] + f1[0:24]), drive * f1[24:48], stiff * c1[0], stiff * c1[1]]
    u2 = [2.0 * u1[0] - u0 + a1[0], 2.0 * u1[1] + a1[1], a1[2], a1[3]]
    for i in range(4):
        mono2[24 * i : 24 * (i + 1)] = u2[i]
    c2 = [curve(x) for x in u2]
    gram(u2, masked(c2))
    s1 = to_rows(jnp.concatenate(a1, axis=0), chooser)
    source1[...] = s1
    jump2 = []
    for i in range(4):
        half = SOURCE * s1[24 * i : 24 * (i + 1)]
        if i < 2:
            g1 = SOURCE * s0[24 * i : 24 * (i + 1)]
            half = half + (2.0 - 7.0 * COURANT) * g1 + COURANT * spread(g1)
        jump2.append(-2.0 * half)
    f2 = to_columns(jnp.concatenate(jump2, axis=0), chooser)
    f2 = [f2[24 * i : 24 * (i + 1)] for i in range(4)]
    f2[0] = f2[0] + free[48:72]
    for i in range(4):
        force2[24 * i : 24 * (i + 1)] = f2[i]
    u3 = [2.0 * u2[i] + drive * f2[i] for i in range(4)] + [stiff * c for c in c2]
    u3[0] = u3[0] - u1[0]
    u3[1] = u3[1] - u1[1]
    gram(u3, masked([curve(x) for x in u3]))

    count = len(totals)
    stack = jnp.concatenate(totals + [jnp.zeros((56 - count, 128), jnp.float32)], axis=0)
    column = jnp.sum(stack, axis=1, keepdims=True)
    diagonal = jnp.where(sublanes((56, 128)) == lanes((56, 128)), column, 0.0)
    sums[...] = jnp.sum(diagonal, axis=0, keepdims=True)


def quadratic(sums, at, monos):
    total = 0.0
    for i in range(len(monos)):
        for j in range(i, len(monos)):
            term = monos[i] * (sums(at) * monos[j])
            total = total + (term if i == j else 2.0 * term)
            at += 1
    return total


def finish_kernel(
    share0, share1, share2, share3, air_row, start, mono1, mono2, force2, force3, source0, source1, next_in, last_in,
    out_next, out_last, out_u, out_w, plane_next, plane_last, fields, wide_rows, turned, listed, sems,
):
    wide = lax.axis_index("gy")
    reached = (wide >= FIRST) & (wide <= LAST)
    loaded = pltpu.make_async_copy(air_row, listed, sems.at[4])
    loaded.start()
    loads = [
        pltpu.make_async_copy(next_in.at[:, :, MID - 128 : MID + 128], plane_next, sems.at[0]),
        pltpu.make_async_copy(last_in.at[:, :, MID - 128 : MID + 128], plane_last, sems.at[1]),
    ]

    @pl.when(reached)
    def _():
        for copy in loads:
            copy.start()

    def tension(energy):
        return 1.0 + BERGER * energy / NODES

    def sums(at):
        return (share0[0, at] + share1[0, at]) + (share2[0, at] + share3[0, at])

    t0 = tension(sums(0))
    t1 = tension(quadratic(sums, 1, [1.0, t0]))
    four = [1.0, t0, t1, t0 * t1]
    t2 = tension(quadratic(sums, 4, four))
    t3 = tension(quadratic(sums, 14, four + [t2 * x for x in four]))

    def mixed(ref, factors):
        total = ref[0:24]
        for i in range(1, len(factors)):
            total = total + factors[i] * ref[24 * i : 24 * (i + 1)]
        return total

    loaded.wait()
    chooser = chooser_of(listed)
    m0 = start[24:48]
    drive, stiff = FORCE * m0, SPEED * m0
    u1 = mixed(mono1, four[:2])
    u2 = mixed(mono2, four)
    a2 = stiff * (t2 * curve(u2)) + drive * mixed(force2, four)
    u3 = 2.0 * u2 - u1 + a2
    s0 = mixed(source0, four[:2])
    s1 = mixed(source1, four)
    s2 = to_rows(a2, chooser)
    within = inside((XE, WINDOW))

    def spread(x):
        return jnp.where(within, beside(x), 0.0)

    g1 = SOURCE * s0
    g2 = [SOURCE * s1 + (2.0 - 7.0 * COURANT) * g1 + COURANT * spread(g1), COURANT * g1]
    g3 = [
        SOURCE * s2 + (2.0 - 7.0 * COURANT) * g2[0] - g1 + COURANT * (spread(g2[0]) + g2[1]),
        (2.0 - 6.0 * COURANT) * g2[1] + COURANT * (spread(g2[1]) + g2[0]),
        COURANT * g2[1],
    ]
    f3 = to_columns(-2.0 * g3[0], chooser)
    a3 = stiff * (t3 * curve(u3)) + drive * (f3 + force3[...])
    u4 = 2.0 * u3 - u2 + a3

    tile = pl.ds(pl.multiple_of(128 * (wide // 4), 128), 128)
    back = lax.rem(128 - 32 * lax.rem(wide, 4), 128)
    fields[0:24] = u4
    fields[24:48] = u3
    out_u[...] = pltpu.roll(fields[4:20, tile], back, 1)[:, 0:BY]
    out_w[...] = pltpu.roll(fields[28:44, tile], back, 1)[:, 0:BY]

    @pl.when(reached)
    def _():
        s3 = to_rows(a3, chooser)
        g4 = [
            SOURCE * s3 + (2.0 - 7.0 * COURANT) * g3[0] - g2[0] + COURANT * (spread(g3[0]) + g3[1]),
            (2.0 - 6.0 * COURANT) * g3[1] - g2[1] + COURANT * (spread(g3[1]) + g3[0] + g3[2]),
            (2.0 - 6.0 * COURANT) * g3[2] + COURANT * (spread(g3[2]) + g3[1]),
            COURANT * g3[2],
        ]
        tile = pl.ds(pl.multiple_of(128 * (wide // 4 - ROW0 // 128), 128), 128)
        for copy in loads:
            copy.wait()
        for gains, plane in ((g4, plane_next), (g3 + [None], plane_last)):
            for k in range(4):
                if gains[k] is None:
                    turned[pl.ds(k, BX, stride=8), :] = jnp.zeros((BX, 128), jnp.float32)
                    turned[pl.ds(7 - k, BX, stride=8), :] = jnp.zeros((BX, 128), jnp.float32)
                    continue
                wide_rows[...] = gains[k]
                part = pltpu.roll(wide_rows[4:20, tile], back, 1)
                turned[pl.ds(k, BX, stride=8), :] = part
                turned[pl.ds(7 - k, BX, stride=8), :] = -part
            across = jnp.transpose(turned[...])[0:BY]
            lane = lanes((BY, 128))
            for x in range(BX):
                above = jnp.where(lane < 4, pltpu.roll(across, (128 - 8 * x) % 128, 1), 0.0)
                below = jnp.where(lane >= 124, pltpu.roll(across, (120 - 8 * x) % 128, 1), 0.0)
                plane[x, :, 0:128] = plane[x, :, 0:128] + below
                plane[x, :, 128:256] = plane[x, :, 128:256] + above
        stores = [
            pltpu.make_async_copy(plane_next, out_next.at[:, :, MID - 128 : MID + 128], sems.at[2]),
            pltpu.make_async_copy(plane_last, out_last.at[:, :, MID - 128 : MID + 128], sems.at[3]),
        ]
        for copy in stores:
            copy.start()
        for copy in stores:
            copy.wait()


def ring(count, by):
    return [(i, (i + by) % count) for i in range(count)]


def across(count, by):
    return [(i, (i + 2 * by) % count if by else i ^ 1) for i in range(count)]


def per_device(air_now, air_prev, membrane_now, membrane_prev, inv_mass, air_row):
    def sems(n):
        return pltpu.SemaphoreType.DMA((n,))

    halo_x, halo_y, own_y, stripe = f32(7, BY, NZ), f32(XE, 8, NZ), f32(BX, 8, NZ), f32(28, COLS)
    listed = air_row.reshape(1, COLS)
    air_now, air_prev, membrane_now, membrane_prev, inv_mass, listed = (
        pltpu.with_memory_space_constraint(x, pltpu.HBM)
        for x in (air_now, air_prev, membrane_now, membrane_prev, inv_mass, listed)
    )
    to_xlow, to_xhigh, to_ylow, to_yhigh, block = pl.pallas_call(
        pack_kernel,
        out_shape=(halo_x, halo_x, own_y, own_y, f32(GY, FOLD, 128)),
        in_specs=[HBM] * 5,
        out_specs=(WHOLE,) * 5,
        scratch_shapes=[
            VMEM((4, BX, 8, NZ), jnp.float32),
            VMEM((2, BX, BY, 256), jnp.float32),
            VMEM((3, BX, BY), jnp.float32),
            VMEM((2, 128, 128), jnp.float32),
            VMEM((PACK, 128), jnp.float32),
            sems(16),
        ],
        compiler_params=granted(8),
        name="pack",
    )(air_now, air_prev, membrane_now, membrane_prev, inv_mass)
    blocks = lax.all_to_all(block, "gy", 0, 0)
    xlow = lax.ppermute(to_xhigh, "gx", ring(GX, 1))
    xhigh = lax.ppermute(to_xlow, "gx", ring(GX, -1))
    members, jumps, to_low, to_high = pl.pallas_call(
        unfold_kernel,
        out_shape=(f32(48, COLS), f32(112, WINDOW), stripe, stripe),
        in_specs=[WHOLE],
        out_specs=(WHOLE,) * 4,
        compiler_params=granted(3),
        name="unfold",
    )(blocks)
    hlow = lax.ppermute(to_high, "gx", ring(GX, 1))
    hhigh = lax.ppermute(to_low, "gx", ring(GX, -1))
    to_ylow, to_yhigh = pl.pallas_call(
        corner_kernel,
        out_shape=(halo_y, halo_y),
        in_specs=[WHOLE] * 2 + [ANY] * 2,
        out_specs=(HBM,) * 2,
        scratch_shapes=[VMEM((2, 2, 4, 8, NZ), jnp.float32), sems(6)],
        compiler_params=granted(3),
        name="corners",
    )(xlow, xhigh, to_ylow, to_yhigh)
    ylow = lax.ppermute(to_yhigh, "gy", ring(GY, 1))
    yhigh = lax.ppermute(to_ylow, "gy", ring(GY, -1))
    air = f32(BX, BY, NZ)
    brick = VMEM((4, XE, YE, 128), jnp.float32)
    next_free, last_free = pl.pallas_call(
        air_kernel,
        out_shape=(air, air),
        in_specs=[HBM] * 2 + [ANY] * 4,
        out_specs=(HBM, HBM),
        scratch_shapes=[brick, brick, sems(44)],
        compiler_params=granted(8),
        cost_estimate=pl.CostEstimate(flops=40_000_000, bytes_accessed=8_000_000, transcendentals=0),
        name="air_free",
    )(air_now, air_prev, xlow, xhigh, ylow, yhigh)
    sums, *saved = pl.pallas_call(
        membrane_kernel,
        out_shape=(
            f32(1, 128), f32(48, COLS), f32(48, COLS), f32(96, COLS), f32(96, COLS), f32(24, COLS),
            f32(48, WINDOW), f32(96, WINDOW),
        ),
        in_specs=[WHOLE] * 4 + [HBM],
        out_specs=(WHOLE,) * 8,
        scratch_shapes=[
            VMEM((3 * XE, COLS), jnp.float32),
            VMEM((7 * XE, WINDOW), jnp.float32),
            VMEM((1, COLS), jnp.int32),
            sems(1),
        ],
        compiler_params=granted(10),
        name="membrane",
    )(members, jumps, hlow, hhigh, listed)
    sums = sums + lax.ppermute(sums, "gx", across(GX, 0))
    shares = [sums] + [lax.ppermute(sums, "gx", across(GX, by)) for by in (1, 2, 3)]
    return pl.pallas_call(
        finish_kernel,
        out_shape=(air, air, f32(BX, BY), f32(BX, BY)),
        in_specs=[pl.BlockSpec(memory_space=pltpu.SMEM)] * 4 + [HBM] + [WHOLE] * 7 + [HBM, HBM],
        out_specs=(HBM, HBM, WHOLE, WHOLE),
        scratch_shapes=[
            VMEM((BX, BY, 256), jnp.float32),
            VMEM((BX, BY, 256), jnp.float32),
            VMEM((48, COLS), jnp.float32),
            VMEM((XE, WINDOW), jnp.float32),
            VMEM((128, 128), jnp.float32),
            VMEM((1, COLS), jnp.int32),
            sems(5),
        ],
        input_output_aliases={12: 0, 13: 1},
        compiler_params=granted(8),
        name="finish",
    )(*shares, listed, *saved, next_free, last_free)


def solution(mesh):
    in_specs = (
        P("gx", "gy", None),
        P("gx", "gy", None),
        P("gx", "gy"),
        P("gx", "gy"),
        P("gx", "gy"),
        P(),
    )
    out_specs = (P("gx", "gy", None), P("gx", "gy", None), P("gx", "gy"), P("gx", "gy"))
    return jax.shard_map(
        per_device, mesh=mesh, in_specs=in_specs, out_specs=out_specs, check_vma=False
    )
```

```python
import functools

import jax
import jax.numpy as jnp
from jax import lax
from jax.experimental import pallas as pl
from jax.experimental.pallas import tpu as pltpu
from jax.sharding import PartitionSpec as P

COURANT = 0.32
SPEED = 0.08
BERGER = 0.4
FORCE = 0.1
SOURCE = 0.5

GX, GY = 8, 32
BX, BY, NZ = 16, 32, 512
MID = NZ // 2
COLS = GY * BY
NODES = GX * BX * COLS
HALO = 4
XE = BX + 2 * HALO
YE = BY + 16
WINDOW = 384
ROW0 = COLS - WINDOW
FIRST, LAST = 22, 30
PACK = 160
FOLD = 40

VMEM = pltpu.VMEM
WHOLE = pl.BlockSpec(memory_space=pltpu.VMEM)
ANY = pl.BlockSpec(memory_space=pl.ANY)
HBM = pl.BlockSpec(memory_space=pltpu.HBM)


def granted(mib):
    return pltpu.CompilerParams(vmem_limit_bytes=mib * 1024 * 1024)


def f32(*shape):
    return jax.ShapeDtypeStruct(shape, jnp.float32)


def lanes(shape):
    return lax.broadcasted_iota(jnp.int32, shape, len(shape) - 1)


def sublanes(shape):
    return lax.broadcasted_iota(jnp.int32, shape, len(shape) - 2)


def fold(rows, wide):
    quarter = lanes((FOLD, 128)) // 32
    folded = rows[0:FOLD, :]
    for g in range(1, 4):
        folded = jnp.where(quarter == g, pltpu.roll(rows[FOLD * g : FOLD * (g + 1), :], 32 * g, 1), folded)
    return pltpu.roll(folded, 32 * lax.rem(wide, 4), 1)


def started(pairs, sems):
    copies = [pltpu.make_async_copy(x, y, sems.at[i]) for i, (x, y) in enumerate(pairs)]
    for copy in copies:
        copy.start()
    return copies


def block_kernel(p, q, u, w, m, block, planes, members, turned, rows, sems):
    wide = lax.axis_index("gy")
    middle = slice(MID - 128, MID + 128)
    pairs = [(p.at[:, :, middle], planes.at[0]), (q.at[:, :, middle], planes.at[1])]
    copies = started(pairs + [(x, members.at[i]) for i, x in enumerate((u, w, m))], sems)
    lane = lanes((BY, 128))
    for i in range(2):
        copies[i].wait()
        total = jnp.zeros((BY, 128), jnp.float32)
        for x in range(BX):
            above = pltpu.roll(planes[i, x, :, 128:256], 8 * x, 1)
            below = pltpu.roll(planes[i, x, :, 0:128], (8 * x + 8) % 128, 1)
            total = jnp.where((lane >= 8 * x) & (lane < 8 * x + 4), above, total)
            total = jnp.where((lane >= 8 * x + 4) & (lane < 8 * x + 8), below, total)
        turned[i, 0:BY, :] = total
        turned[i, BY:128, :] = jnp.zeros((128 - BY, 128), jnp.float32)
        turned[i] = jnp.transpose(turned[i])
        for k in range(4 - i):
            at = 48 + 64 * i + 16 * k
            rows[at : at + 16, :] = turned[i, pl.ds(7 - k, BX, stride=8), :] - turned[i, pl.ds(k, BX, stride=8), :]
    for i in range(3):
        copies[2 + i].wait()
        rows[16 * i : 16 * i + 16, 0:BY] = members[i]
    folded = fold(rows, wide)
    for i in range(GY):
        block[i] = folded


def pack_kernel(p, q, after, xlow, xhigh, ylow, yhigh, edges, sems):
    pairs = [(x.at[:, at : at + 8], edges.at[i]) for i, (x, at) in enumerate(((p, 0), (q, 0), (p, 24), (q, 24)))]
    pairs += [
        (p.at[0:4], xlow.at[0:4]),
        (q.at[0:3], xlow.at[4:7]),
        (p.at[12:16], xhigh.at[0:4]),
        (q.at[13:16], xhigh.at[4:7]),
    ]
    copies = started(pairs, sems)
    lower = sublanes((8, NZ)) < 4
    for copy in copies[0:4]:
        copy.wait()
    for r in range(BX):
        ylow[r] = jnp.where(lower, edges[0, r], pltpu.roll(edges[1, r], 4, 0))
        yhigh[r] = jnp.where(lower, pltpu.roll(edges[3, r], 4, 0), edges[2, r])
    for copy in copies[4:]:
        copy.wait()


def corner_kernel(xlow, xhigh, own_low, own_high, out_ylow, out_yhigh, corners, sems):
    copies = [
        pltpu.make_async_copy(own, out.at[4:20], sems.at[4 + i])
        for i, (own, out) in enumerate(((own_low, out_ylow), (own_high, out_yhigh)))
    ]
    for copy in copies:
        copy.start()
    lower = sublanes((8, NZ)) < 4
    for i in range(4):
        for at, halo, j in ((0, xlow, 4 + max(i - 1, 0)), (1, xhigh, 4 + min(i, 2))):
            corners[0, at, i] = jnp.where(lower, halo[i, 0:8], pltpu.roll(halo[j, 0:8], 4, 0))
            corners[1, at, i] = jnp.where(lower, pltpu.roll(halo[j, 24:32], 4, 0), halo[i, 24:32])
    for i, out in enumerate((out_ylow, out_yhigh)):
        for at in range(2):
            copy = pltpu.make_async_copy(corners.at[i, at], out.at[20 * at : 20 * at + 4], sems.at[2 * i + at])
            copy.start()
            copies.append(copy)
    for copy in copies:
        copy.wait()


def unfold_kernel(blocks, members, jumps, to_low, to_high):
    quarter = lanes((FOLD, 128)) // 32
    for g in range(4):
        for t in range(8):
            if g >= 2 and t < 5:
                continue
            merged = blocks[4 * t + (-g) % 4]
            for s in range(1, 4):
                merged = jnp.where(quarter == s, blocks[4 * t + (s - g) % 4], merged)
            merged = pltpu.roll(merged, (128 - 32 * g) % 128, 1)
            column = slice(128 * t, 128 * (t + 1))
            narrow = slice(128 * (t - 5), 128 * (t - 4))
            if g == 0:
                members[0:40, column] = merged
            elif g == 1:
                members[40:48, column] = merged[0:8]
                if t >= 5:
                    jumps[0:32, narrow] = merged[8:40]
            else:
                jumps[40 * g - 48 : 40 * g - 8, narrow] = merged
    for out, at in ((to_low, 0), (to_high, 12)):
        for i in range(3):
            out[4 * i : 4 * i + 4, :] = members[16 * i + at : 16 * i + at + 4, :]
        for k in range(4):
            out[12 + 4 * k : 16 + 4 * k, 0:WINDOW] = jumps[16 * k + at : 16 * k + at + 4, :]
        for k in range(3):
            out[12 + 4 * k : 16 + 4 * k, 512 : 512 + WINDOW] = jumps[64 + 16 * k + at : 68 + 16 * k + at, :]


def edge_free(shape, edge):
    return jnp.broadcast_to(edge.astype(jnp.int32), shape) == 0


def air_kernel(p, q, xlow, xhigh, ylow, yhigh, out_next, out_last, a, b, sems):
    tall = lax.axis_index("gx")
    wide = lax.axis_index("gy")
    first, last = tall == 0, tall == GX - 1
    bottom, top = wide == 0, wide == GY - 1
    layers = [slice(128 * k, 128 * (k + 1)) for k in range(4)]
    pairs = []
    for k in range(4):
        z = layers[k]
        pairs += [
            (p.at[:, :, z], a.at[k, 4:20, 8:40]),
            (q.at[:, :, z], b.at[k, 4:20, 8:40]),
            (xlow.at[0:4, :, z], a.at[k, 0:4, 8:40]),
            (xlow.at[4:7, :, z], b.at[k, 1:4, 8:40]),
            (xhigh.at[0:4, :, z], a.at[k, 20:24, 8:40]),
            (xhigh.at[4:7, :, z], b.at[k, 20:23, 8:40]),
            (ylow.at[:, :, z], a.at[k, :, 0:8]),
            (yhigh.at[:, :, z], a.at[k, :, 40:48]),
        ]
    copies = [pltpu.make_async_copy(x, y, sems.at[i]) for i, (x, y) in enumerate(pairs)]
    for copy in copies:
        copy.start()
    for copy in copies:
        copy.wait()

    def cleared(edge, ref, at):
        @pl.when(edge)
        def _():
            for k in range(4):
                ref.at[(k, *at)][...] = jnp.zeros(ref.at[(k, *at)].shape, jnp.float32)

    cleared(first, a, (slice(0, 4),))
    cleared(first, b, (slice(1, 4),))
    cleared(last, a, (slice(20, 24),))
    cleared(last, b, (slice(20, 23),))
    cleared(bottom, a, (slice(0, XE), slice(0, 8)))
    cleared(top, a, (slice(0, XE), slice(40, 48)))
    for k in range(4):
        for r in range(1, XE - 1):
            b[k, r, 0:8] = pltpu.roll(a[k, r, 0:8], 4, 0)
            b[k, r, 40:48] = pltpu.roll(a[k, r, 40:48], 4, 0)

    tile_low, tile_high = edge_free((8, 128), bottom), edge_free((8, 128), top)
    lane = lanes((8, 128))

    def advance(now, old, r, tile):
        at = 8 * tile
        c = [now[k, r, at : at + 8] for k in range(4)]
        up = [pltpu.roll(x, 1, 1) for x in c]
        down = [pltpu.roll(x, 127, 1) for x in c]
        for k in range(4):
            left = jnp.where(lane == 0, up[k - 1] if k else 0.0, up[k])
            right = jnp.where(lane == 127, down[k + 1] if k < 3 else 0.0, down[k])
            if tile > 0:
                before = now[k, r, at - 1 : at + 7]
            else:
                before = pltpu.roll(c[k], 1, 0)
            if tile < 5:
                after = now[k, r, at + 1 : at + 9]
            else:
                after = pltpu.roll(c[k], 7, 0)
            ring = (left + right) + (before + after) + (now[k, r - 1, at : at + 8] + now[k, r + 1, at : at + 8])
            new = (2.0 - 6.0 * COURANT) * c[k] - old[k, r, at : at + 8] + COURANT * ring
            if tile == 0:
                new = jnp.where(tile_low, new, 0.0)
            if tile == 5:
                new = jnp.where(tile_high, new, 0.0)
            old[k, r, at : at + 8] = new

    sent = []

    def send(x, out, rows, at):
        for k in range(4):
            target = out.at[rows, :, layers[k]]
            copy = pltpu.make_async_copy(x.at[k, rows.start + 4 : rows.stop + 4, 8:40], target, sems.at[at + k])
            copy.start()
            sent.append(copy)

    for t in range(4):
        now, old = (a, b) if t % 2 == 0 else (b, a)

        def row(r):
            for tile in range(6) if t < 3 else range(1, 5):
                advance(now, old, r, tile)

        if t < 3:

            @pl.when(jnp.logical_not(first))
            def _():
                for r in range(t + 1, 4):
                    row(r)

        for r in range(4, 20):
            row(r)
            if t == 3 and r in (11, 19):
                send(a, out_next, slice(r - 11, r - 3), 36 + 4 * (r // 19))
        if t < 3:

            @pl.when(jnp.logical_not(last))
            def _():
                for r in range(20, XE - 1 - t):
                    row(r)

        if t == 2:
            send(b, out_last, slice(0, 16), 32)
    for copy in sent:
        copy.wait()


def split(x):
    high = x.astype(jnp.bfloat16)
    low = (x - high.astype(jnp.float32)).astype(jnp.bfloat16)
    return jnp.concatenate([high, low], axis=0)


def to_columns(x, chooser):
    n = x.shape[0]
    both = lax.dot_general(split(x), chooser, (((1,), (0,)), ((), ())), preferred_element_type=jnp.float32)
    return both[0:n] + both[n : 2 * n]


def to_rows(x, chooser):
    n = x.shape[0]
    both = lax.dot_general(split(x), chooser, (((1,), (1,)), ((), ())), preferred_element_type=jnp.float32)
    return both[0:n] + both[n : 2 * n]


def chooser_of(air_row):
    rows = lax.broadcasted_iota(jnp.int32, (WINDOW, COLS), 0) + ROW0
    return jnp.where(rows == air_row[...], 1.0, 0.0).astype(jnp.bfloat16)


def beside(field):
    n = field.shape[1]
    lane = lanes(field.shape)
    left = jnp.where(lane == 0, 0.0, pltpu.roll(field, 1, 1))
    right = jnp.where(lane == n - 1, 0.0, pltpu.roll(field, n - 1, 1))
    return left + right + pltpu.roll(field, 1, 0) + pltpu.roll(field, field.shape[0] - 1, 0)


def curve(field):
    return beside(field) - 4.0 * field


def inside(shape):
    tall = lax.axis_index("gx")
    row = sublanes(shape)
    low = jnp.where(tall == 0, 4, 0)
    high = jnp.where(tall == GX - 1, 20, 24)
    return (row >= low) & (row < high)


def membrane_kernel(
    members, jumps, hlow, hhigh, air_row, sums, start, mono1, mono2, force2, force3, source0, source1, parts, slab
):
    tall = lax.axis_index("gx")
    for i in range(3):
        at = XE * i
        parts[at : at + 4] = jnp.where(edge_free((4, COLS), tall == 0), hlow[4 * i : 4 * i + 4, :], 0.0)
        parts[at + 4 : at + 20] = members[16 * i : 16 * i + 16]
        parts[at + 20 : at + 24] = jnp.where(edge_free((4, COLS), tall == GX - 1), hhigh[4 * i : 4 * i + 4, :], 0.0)
    for i in range(7):
        at, row = XE * i, 12 + 4 * (i % 4)
        narrow = slice(512 * (i // 4), 512 * (i // 4) + WINDOW)
        slab[at : at + 4] = jnp.where(edge_free((4, WINDOW), tall == 0), hlow[row : row + 4, narrow], 0.0)
        slab[at + 4 : at + 20] = jumps[16 * i : 16 * i + 16]
        slab[at + 20 : at + 24] = jnp.where(edge_free((4, WINDOW), tall == GX - 1), hhigh[row : row + 4, narrow], 0.0)
    within = inside((XE, WINDOW))

    def spread(x):
        return jnp.where(within, beside(x), 0.0)

    older = [slab[96 + XE * k : 96 + XE * (k + 1)] for k in range(3)] + [None]
    newer = [slab[XE * k : XE * (k + 1)] for k in range(4)]
    free = [newer[0]]
    for t in range(3):
        step = []
        for k in range(3 - t):
            own = 2.0 - (7.0 if k == 0 else 6.0) * COURANT
            ring = spread(newer[k]) + newer[k + 1]
            if k:
                ring = ring + newer[k - 1]
            step.append(own * newer[k] - older[k] + COURANT * ring)
        older, newer = newer, step
        free.append(newer[0])
    chooser = chooser_of(air_row)
    u0, w0, m0 = parts[0:24], parts[24:48], parts[48:72]
    start[0:24] = u0
    start[24:48] = m0
    free = to_columns(jnp.concatenate(free, axis=0), chooser)
    force3[...] = free[72:96]
    drive, stiff = FORCE * m0, SPEED * m0
    row = sublanes((XE, COLS))
    mine = (row >= HALO) & (row < HALO + BX)
    totals = []

    def gram(fields, curves):
        for i in range(len(fields)):
            for j in range(i, len(fields)):
                product = fields[i] * curves[j]
                part = product[:, 0:128]
                for k in range(1, COLS // 128):
                    part = part + product[:, 128 * k : 128 * (k + 1)]
                totals.append(jnp.sum(part, axis=0, keepdims=True))

    def masked(curves):
        return [jnp.where(mine, -c, 0.0) for c in curves]

    c0 = curve(u0)
    gram([u0], masked([c0]))
    a0 = [drive * free[0:24], stiff * c0]
    u1 = [2.0 * u0 - w0 + a0[0], a0[1]]
    mono1[0:24] = u1[0]
    mono1[24:48] = u1[1]
    c1 = [curve(x) for x in u1]
    gram(u1, masked(c1))
    s0 = to_rows(jnp.concatenate(a0, axis=0), chooser)
    source0[...] = s0
    f1 = to_columns(-s0, chooser)
    a1 = [drive * (free[24:48] + f1[0:24]), drive * f1[24:48], stiff * c1[0], stiff * c1[1]]
    u2 = [2.0 * u1[0] - u0 + a1[0], 2.0 * u1[1] + a1[1], a1[2], a1[3]]
    for i in range(4):
        mono2[24 * i : 24 * (i + 1)] = u2[i]
    c2 = [curve(x) for x in u2]
    gram(u2, masked(c2))
    s1 = to_rows(jnp.concatenate(a1, axis=0), chooser)
    source1[...] = s1
    jump2 = []
    for i in range(4):
        half = SOURCE * s1[24 * i : 24 * (i + 1)]
        if i < 2:
            g1 = SOURCE * s0[24 * i : 24 * (i + 1)]
            half = half + (2.0 - 7.0 * COURANT) * g1 + COURANT * spread(g1)
        jump2.append(-2.0 * half)
    f2 = to_columns(jnp.concatenate(jump2, axis=0), chooser)
    f2 = [f2[24 * i : 24 * (i + 1)] for i in range(4)]
    f2[0] = f2[0] + free[48:72]
    for i in range(4):
        force2[24 * i : 24 * (i + 1)] = f2[i]
    u3 = [2.0 * u2[i] + drive * f2[i] for i in range(4)] + [stiff * c for c in c2]
    u3[0] = u3[0] - u1[0]
    u3[1] = u3[1] - u1[1]
    gram(u3, masked([curve(x) for x in u3]))

    count = len(totals)
    stack = jnp.concatenate(totals + [jnp.zeros((56 - count, 128), jnp.float32)], axis=0)
    column = jnp.sum(stack, axis=1, keepdims=True)
    diagonal = jnp.where(sublanes((56, 128)) == lanes((56, 128)), column, 0.0)
    sums[...] = jnp.sum(diagonal, axis=0, keepdims=True)


def quadratic(sums, at, monos):
    total = 0.0
    for i in range(len(monos)):
        for j in range(i, len(monos)):
            term = monos[i] * (sums(at) * monos[j])
            total = total + (term if i == j else 2.0 * term)
            at += 1
    return total


def finish_kernel(
    share0, share1, share2, share3, air_row, start, mono1, mono2, force2, force3, source0, source1, next_in, last_in,
    out_next, out_last, out_u, out_w, plane_next, plane_last, fields, wide_rows, turned, sems,
):
    wide = lax.axis_index("gy")
    reached = (wide >= FIRST) & (wide <= LAST)
    loads = [
        pltpu.make_async_copy(next_in.at[:, :, MID - 128 : MID + 128], plane_next, sems.at[0]),
        pltpu.make_async_copy(last_in.at[:, :, MID - 128 : MID + 128], plane_last, sems.at[1]),
    ]

    @pl.when(reached)
    def _():
        for copy in loads:
            copy.start()

    def tension(energy):
        return 1.0 + BERGER * energy / NODES

    def sums(at):
        return (share0[0, at] + share1[0, at]) + (share2[0, at] + share3[0, at])

    t0 = tension(sums(0))
    t1 = tension(quadratic(sums, 1, [1.0, t0]))
    four = [1.0, t0, t1, t0 * t1]
    t2 = tension(quadratic(sums, 4, four))
    t3 = tension(quadratic(sums, 14, four + [t2 * x for x in four]))

    def mixed(ref, factors):
        total = ref[0:24]
        for i in range(1, len(factors)):
            total = total + factors[i] * ref[24 * i : 24 * (i + 1)]
        return total

    chooser = chooser_of(air_row)
    m0 = start[24:48]
    drive, stiff = FORCE * m0, SPEED * m0
    u1 = mixed(mono1, four[:2])
    u2 = mixed(mono2, four)
    a2 = stiff * (t2 * curve(u2)) + drive * mixed(force2, four)
    u3 = 2.0 * u2 - u1 + a2
    s0 = mixed(source0, four[:2])
    s1 = mixed(source1, four)
    s2 = to_rows(a2, chooser)
    within = inside((XE, WINDOW))

    def spread(x):
        return jnp.where(within, beside(x), 0.0)

    g1 = SOURCE * s0
    g2 = [SOURCE * s1 + (2.0 - 7.0 * COURANT) * g1 + COURANT * spread(g1), COURANT * g1]
    g3 = [
        SOURCE * s2 + (2.0 - 7.0 * COURANT) * g2[0] - g1 + COURANT * (spread(g2[0]) + g2[1]),
        (2.0 - 6.0 * COURANT) * g2[1] + COURANT * (spread(g2[1]) + g2[0]),
        COURANT * g2[1],
    ]
    f3 = to_columns(-2.0 * g3[0], chooser)
    a3 = stiff * (t3 * curve(u3)) + drive * (f3 + force3[...])
    u4 = 2.0 * u3 - u2 + a3

    tile = pl.ds(pl.multiple_of(128 * (wide // 4), 128), 128)
    back = lax.rem(128 - 32 * lax.rem(wide, 4), 128)
    fields[0:24] = u4
    fields[24:48] = u3
    out_u[...] = pltpu.roll(fields[4:20, tile], back, 1)[:, 0:BY]
    out_w[...] = pltpu.roll(fields[28:44, tile], back, 1)[:, 0:BY]

    @pl.when(reached)
    def _():
        s3 = to_rows(a3, chooser)
        g4 = [
            SOURCE * s3 + (2.0 - 7.0 * COURANT) * g3[0] - g2[0] + COURANT * (spread(g3[0]) + g3[1]),
            (2.0 - 6.0 * COURANT) * g3[1] - g2[1] + COURANT * (spread(g3[1]) + g3[0] + g3[2]),
            (2.0 - 6.0 * COURANT) * g3[2] + COURANT * (spread(g3[2]) + g3[1]),
            COURANT * g3[2],
        ]
        tile = pl.ds(pl.multiple_of(128 * (wide // 4 - ROW0 // 128), 128), 128)
        for copy in loads:
            copy.wait()
        for gains, plane in ((g4, plane_next), (g3 + [None], plane_last)):
            for k in range(4):
                if gains[k] is None:
                    turned[pl.ds(k, BX, stride=8), :] = jnp.zeros((BX, 128), jnp.float32)
                    turned[pl.ds(7 - k, BX, stride=8), :] = jnp.zeros((BX, 128), jnp.float32)
                    continue
                wide_rows[...] = gains[k]
                part = pltpu.roll(wide_rows[4:20, tile], back, 1)
                turned[pl.ds(k, BX, stride=8), :] = part
                turned[pl.ds(7 - k, BX, stride=8), :] = -part
            across = jnp.transpose(turned[...])[0:BY]
            lane = lanes((BY, 128))
            for x in range(BX):
                above = jnp.where(lane < 4, pltpu.roll(across, (128 - 8 * x) % 128, 1), 0.0)
                below = jnp.where(lane >= 124, pltpu.roll(across, (120 - 8 * x) % 128, 1), 0.0)
                plane[x, :, 0:128] = plane[x, :, 0:128] + below
                plane[x, :, 128:256] = plane[x, :, 128:256] + above
        stores = [
            pltpu.make_async_copy(plane_next, out_next.at[:, :, MID - 128 : MID + 128], sems.at[2]),
            pltpu.make_async_copy(plane_last, out_last.at[:, :, MID - 128 : MID + 128], sems.at[3]),
        ]
        for copy in stores:
            copy.start()
        for copy in stores:
            copy.wait()


def ring(count, by):
    return [(i, (i + by) % count) for i in range(count)]


def across(count, by):
    return [(i, (i + 2 * by) % count if by else i ^ 1) for i in range(count)]


def per_device(air_now, air_prev, membrane_now, membrane_prev, inv_mass, air_row):
    def sems(n):
        return pltpu.SemaphoreType.DMA((n,))

    halo_x, halo_y, own_y, stripe = f32(7, BY, NZ), f32(XE, 8, NZ), f32(BX, 8, NZ), f32(28, COLS)
    listed = air_row.reshape(1, COLS)
    air_now, air_prev, membrane_now, membrane_prev, inv_mass = (
        pltpu.with_memory_space_constraint(x, pltpu.HBM)
        for x in (air_now, air_prev, membrane_now, membrane_prev, inv_mass)
    )
    block = pl.pallas_call(
        block_kernel,
        out_shape=f32(GY, FOLD, 128),
        in_specs=[HBM] * 5,
        out_specs=WHOLE,
        scratch_shapes=[
            VMEM((2, BX, BY, 256), jnp.float32),
            VMEM((3, BX, BY), jnp.float32),
            VMEM((2, 128, 128), jnp.float32),
            VMEM((PACK, 128), jnp.float32),
            sems(5),
        ],
        compiler_params=granted(6),
        name="block",
    )(air_now, air_prev, membrane_now, membrane_prev, inv_mass)
    to_xlow, to_xhigh, to_ylow, to_yhigh = pl.pallas_call(
        pack_kernel,
        out_shape=(halo_x, halo_x, own_y, own_y),
        in_specs=[HBM] * 2 + [ANY],
        out_specs=(WHOLE,) * 4,
        scratch_shapes=[VMEM((4, BX, 8, NZ), jnp.float32), sems(8)],
        compiler_params=granted(4),
        name="pack",
    )(air_now, air_prev, block)
    blocks = lax.all_to_all(block, "gy", 0, 0)
    xlow = lax.ppermute(to_xhigh, "gx", ring(GX, 1))
    xhigh = lax.ppermute(to_xlow, "gx", ring(GX, -1))
    members, jumps, to_low, to_high = pl.pallas_call(
        unfold_kernel,
        out_shape=(f32(48, COLS), f32(112, WINDOW), stripe, stripe),
        in_specs=[WHOLE],
        out_specs=(WHOLE,) * 4,
        compiler_params=granted(3),
        name="unfold",
    )(blocks)
    hlow = lax.ppermute(to_high, "gx", ring(GX, 1))
    hhigh = lax.ppermute(to_low, "gx", ring(GX, -1))
    to_ylow, to_yhigh = pl.pallas_call(
        corner_kernel,
        out_shape=(halo_y, halo_y),
        in_specs=[WHOLE] * 2 + [ANY] * 2,
        out_specs=(HBM,) * 2,
        scratch_shapes=[VMEM((2, 2, 4, 8, NZ), jnp.float32), sems(6)],
        compiler_params=granted(3),
        name="corners",
    )(xlow, xhigh, to_ylow, to_yhigh)
    ylow = lax.ppermute(to_yhigh, "gy", ring(GY, 1))
    yhigh = lax.ppermute(to_ylow, "gy", ring(GY, -1))
    air = f32(BX, BY, NZ)
    brick = VMEM((4, XE, YE, 128), jnp.float32)
    next_free, last_free = pl.pallas_call(
        air_kernel,
        out_shape=(air, air),
        in_specs=[HBM] * 2 + [ANY] * 4,
        out_specs=(HBM, HBM),
        scratch_shapes=[brick, brick, sems(44)],
        compiler_params=granted(8),
        cost_estimate=pl.CostEstimate(flops=40_000_000, bytes_accessed=8_000_000, transcendentals=0),
        name="air_free",
    )(air_now, air_prev, xlow, xhigh, ylow, yhigh)
    sums, *saved = pl.pallas_call(
        membrane_kernel,
        out_shape=(
            f32(1, 128), f32(48, COLS), f32(48, COLS), f32(96, COLS), f32(96, COLS), f32(24, COLS),
            f32(48, WINDOW), f32(96, WINDOW),
        ),
        in_specs=[WHOLE] * 5,
        out_specs=(WHOLE,) * 8,
        scratch_shapes=[
            VMEM((3 * XE, COLS), jnp.float32),
            VMEM((7 * XE, WINDOW), jnp.float32),
        ],
        compiler_params=granted(10),
        name="membrane",
    )(members, jumps, hlow, hhigh, listed)
    sums = sums + lax.ppermute(sums, "gx", across(GX, 0))
    shares = [sums] + [lax.ppermute(sums, "gx", across(GX, by)) for by in (1, 2, 3)]
    return pl.pallas_call(
        finish_kernel,
        out_shape=(air, air, f32(BX, BY), f32(BX, BY)),
        in_specs=[pl.BlockSpec(memory_space=pltpu.SMEM)] * 4 + [WHOLE] * 8 + [HBM, HBM],
        out_specs=(HBM, HBM, WHOLE, WHOLE),
        scratch_shapes=[
            VMEM((BX, BY, 256), jnp.float32),
            VMEM((BX, BY, 256), jnp.float32),
            VMEM((48, COLS), jnp.float32),
            VMEM((XE, WINDOW), jnp.float32),
            VMEM((128, 128), jnp.float32),
            sems(4),
        ],
        input_output_aliases={12: 0, 13: 1},
        compiler_params=granted(8),
        name="finish",
    )(*shares, listed, *saved, next_free, last_free)


def solution(mesh):
    in_specs = (
        P("gx", "gy", None),
        P("gx", "gy", None),
        P("gx", "gy"),
        P("gx", "gy"),
        P("gx", "gy"),
        P(),
    )
    out_specs = (P("gx", "gy", None), P("gx", "gy", None), P("gx", "gy"), P("gx", "gy"))
    return jax.shard_map(
        per_device, mesh=mesh, in_specs=in_specs, out_specs=out_specs, check_vma=False
    )
```

```python
import functools

import jax
import jax.numpy as jnp
from jax import lax
from jax.experimental import pallas as pl
from jax.experimental.pallas import tpu as pltpu
from jax.sharding import PartitionSpec as P

COURANT = 0.32
SPEED = 0.08
BERGER = 0.4
FORCE = 0.1
SOURCE = 0.5

GX, GY = 8, 32
BX, BY, NZ = 16, 32, 512
MID = NZ // 2
COLS = GY * BY
NODES = GX * BX * COLS
HALO = 4
XE = BX + 2 * HALO
YE = BY + 16
WINDOW = 384
ROW0 = COLS - WINDOW
FIRST, LAST = 22, 30
PACK = 160
FOLD = 40
STRIPE_ROWS = (4, 3, 3, 3, 3, 3, 3, 2, 2, 2)

VMEM = pltpu.VMEM
WHOLE = pl.BlockSpec(memory_space=pltpu.VMEM)
ANY = pl.BlockSpec(memory_space=pl.ANY)
HBM = pl.BlockSpec(memory_space=pltpu.HBM)


def granted(mib):
    return pltpu.CompilerParams(vmem_limit_bytes=mib * 1024 * 1024)


def f32(*shape):
    return jax.ShapeDtypeStruct(shape, jnp.float32)


def lanes(shape):
    return lax.broadcasted_iota(jnp.int32, shape, len(shape) - 1)


def sublanes(shape):
    return lax.broadcasted_iota(jnp.int32, shape, len(shape) - 2)


def fold(rows, wide):
    quarter = lanes((FOLD, 128)) // 32
    folded = rows[0:FOLD, :]
    for g in range(1, 4):
        folded = jnp.where(quarter == g, pltpu.roll(rows[FOLD * g : FOLD * (g + 1), :], 32 * g, 1), folded)
    return pltpu.roll(folded, 32 * lax.rem(wide, 4), 1)


def started(pairs, sems):
    copies = [pltpu.make_async_copy(x, y, sems.at[i]) for i, (x, y) in enumerate(pairs)]
    for copy in copies:
        copy.start()
    return copies


def block_kernel(p, q, u, w, m, block, planes, members, turned, rows, sems):
    wide = lax.axis_index("gy")
    middle = slice(MID - 128, MID + 128)
    pairs = [(p.at[:, :, middle], planes.at[0]), (q.at[:, :, middle], planes.at[1])]
    copies = started(pairs + [(x, members.at[i]) for i, x in enumerate((u, w, m))], sems)
    lane = lanes((BY, 128))
    for i in range(2):
        copies[i].wait()
        total = jnp.zeros((BY, 128), jnp.float32)
        for x in range(BX):
            above = pltpu.roll(planes[i, x, :, 128:256], 8 * x, 1)
            below = pltpu.roll(planes[i, x, :, 0:128], (8 * x + 8) % 128, 1)
            total = jnp.where((lane >= 8 * x) & (lane < 8 * x + 4), above, total)
            total = jnp.where((lane >= 8 * x + 4) & (lane < 8 * x + 8), below, total)
        turned[i, 0:BY, :] = total
        turned[i, BY:128, :] = jnp.zeros((128 - BY, 128), jnp.float32)
        turned[i] = jnp.transpose(turned[i])
        for k in range(4 - i):
            at = 48 + 64 * i + 16 * k
            rows[at : at + 16, :] = turned[i, pl.ds(7 - k, BX, stride=8), :] - turned[i, pl.ds(k, BX, stride=8), :]
    for i in range(3):
        copies[2 + i].wait()
        rows[16 * i : 16 * i + 16, 0:BY] = members[i]
    folded = fold(rows, wide)
    for i in range(GY):
        block[i] = folded


def pack_kernel(p, q, after, xlow, xhigh, ylow, yhigh, edges, sems):
    pairs = [(x.at[:, at : at + 8], edges.at[i]) for i, (x, at) in enumerate(((p, 0), (q, 0), (p, 24), (q, 24)))]
    pairs += [
        (p.at[0:4], xlow.at[0:4]),
        (q.at[0:3], xlow.at[4:7]),
        (p.at[12:16], xhigh.at[0:4]),
        (q.at[13:16], xhigh.at[4:7]),
    ]
    copies = started(pairs, sems)
    lower = sublanes((8, NZ)) < 4
    for copy in copies[0:4]:
        copy.wait()
    for r in range(BX):
        ylow[r] = jnp.where(lower, edges[0, r], pltpu.roll(edges[1, r], 4, 0))
        yhigh[r] = jnp.where(lower, pltpu.roll(edges[3, r], 4, 0), edges[2, r])
    for copy in copies[4:]:
        copy.wait()


def corner_kernel(xlow, xhigh, own_low, own_high, out_ylow, out_yhigh, corners, sems):
    copies = [
        pltpu.make_async_copy(own, out.at[4:20], sems.at[4 + i])
        for i, (own, out) in enumerate(((own_low, out_ylow), (own_high, out_yhigh)))
    ]
    for copy in copies:
        copy.start()
    lower = sublanes((8, NZ)) < 4
    for i in range(4):
        for at, halo, j in ((0, xlow, 4 + max(i - 1, 0)), (1, xhigh, 4 + min(i, 2))):
            corners[0, at, i] = jnp.where(lower, halo[i, 0:8], pltpu.roll(halo[j, 0:8], 4, 0))
            corners[1, at, i] = jnp.where(lower, pltpu.roll(halo[j, 24:32], 4, 0), halo[i, 24:32])
    for i, out in enumerate((out_ylow, out_yhigh)):
        for at in range(2):
            copy = pltpu.make_async_copy(corners.at[i, at], out.at[20 * at : 20 * at + 4], sems.at[2 * i + at])
            copy.start()
            copies.append(copy)
    for copy in copies:
        copy.wait()


def stripe_slot(row):
    return 10 + (row - 10) // 2, 512 * (row % 2)


def unfold_kernel(blocks, members, jumps, to_low, to_high):
    quarter = lanes((FOLD, 128)) // 32
    for g in range(4):
        for t in range(8):
            if g >= 2 and t < 5:
                continue
            merged = blocks[4 * t + (-g) % 4]
            for s in range(1, 4):
                merged = jnp.where(quarter == s, blocks[4 * t + (s - g) % 4], merged)
            merged = pltpu.roll(merged, (128 - 32 * g) % 128, 1)
            column = slice(128 * t, 128 * (t + 1))
            narrow = slice(128 * (t - 5), 128 * (t - 4))
            if g == 0:
                members[0:40, column] = merged
            elif g == 1:
                members[40:48, column] = merged[0:8]
                if t >= 5:
                    jumps[0:32, narrow] = merged[8:40]
            else:
                jumps[40 * g - 48 : 40 * g - 8, narrow] = merged
    for out, end in ((to_low, 0), (to_high, BX)):
        for i, n in enumerate(STRIPE_ROWS):
            row, at = sum(STRIPE_ROWS[:i]), 16 * i + (end - n if end else 0)
            if i < 3:
                out[row : row + n, :] = members[at : at + n, :]
            else:
                for j in range(n):
                    slot, lane = stripe_slot(row + j)
                    out[slot : slot + 1, lane : lane + WINDOW] = jumps[at - 48 + j : at - 47 + j, :]


def edge_free(shape, edge):
    return jnp.broadcast_to(edge.astype(jnp.int32), shape) == 0


def stage_kernel(p, q, after, out_p, out_q, done, sems):
    copies = started([(p, out_p), (q, out_q)], sems)
    done[...] = jnp.zeros((8, 128), jnp.float32)
    for copy in copies:
        copy.wait()


def air_kernel(p, q, xlow, xhigh, ylow, yhigh, out_next, out_last, a, b, sems):
    tall = lax.axis_index("gx")
    wide = lax.axis_index("gy")
    first, last = tall == 0, tall == GX - 1
    bottom, top = wide == 0, wide == GY - 1
    layers = [slice(128 * k, 128 * (k + 1)) for k in range(4)]
    pairs = []
    for k in range(4):
        z = layers[k]
        pairs += [
            (p.at[:, :, z], a.at[k, 4:20, 8:40]),
            (q.at[:, :, z], b.at[k, 4:20, 8:40]),
            (xlow.at[0:4, :, z], a.at[k, 0:4, 8:40]),
            (xlow.at[4:7, :, z], b.at[k, 1:4, 8:40]),
            (xhigh.at[0:4, :, z], a.at[k, 20:24, 8:40]),
            (xhigh.at[4:7, :, z], b.at[k, 20:23, 8:40]),
            (ylow.at[:, :, z], a.at[k, :, 0:8]),
            (yhigh.at[:, :, z], a.at[k, :, 40:48]),
        ]
    copies = [pltpu.make_async_copy(x, y, sems.at[i]) for i, (x, y) in enumerate(pairs)]
    for copy in copies:
        copy.start()
    for copy in copies:
        copy.wait()

    def cleared(edge, ref, at):
        @pl.when(edge)
        def _():
            for k in range(4):
                ref.at[(k, *at)][...] = jnp.zeros(ref.at[(k, *at)].shape, jnp.float32)

    cleared(first, a, (slice(0, 4),))
    cleared(first, b, (slice(1, 4),))
    cleared(last, a, (slice(20, 24),))
    cleared(last, b, (slice(20, 23),))
    cleared(bottom, a, (slice(0, XE), slice(0, 8)))
    cleared(top, a, (slice(0, XE), slice(40, 48)))
    for k in range(4):
        for r in range(1, XE - 1):
            b[k, r, 0:8] = pltpu.roll(a[k, r, 0:8], 4, 0)
            b[k, r, 40:48] = pltpu.roll(a[k, r, 40:48], 4, 0)

    tile_low, tile_high = edge_free((8, 128), bottom), edge_free((8, 128), top)
    lane = lanes((8, 128))

    def advance(now, old, r, tile):
        at = 8 * tile
        c = [now[k, r, at : at + 8] for k in range(4)]
        up = [pltpu.roll(x, 1, 1) for x in c]
        down = [pltpu.roll(x, 127, 1) for x in c]
        for k in range(4):
            left = jnp.where(lane == 0, up[k - 1] if k else 0.0, up[k])
            right = jnp.where(lane == 127, down[k + 1] if k < 3 else 0.0, down[k])
            if tile > 0:
                before = now[k, r, at - 1 : at + 7]
            else:
                before = pltpu.roll(c[k], 1, 0)
            if tile < 5:
                after = now[k, r, at + 1 : at + 9]
            else:
                after = pltpu.roll(c[k], 7, 0)
            ring = (left + right) + (before + after) + (now[k, r - 1, at : at + 8] + now[k, r + 1, at : at + 8])
            new = (2.0 - 6.0 * COURANT) * c[k] - old[k, r, at : at + 8] + COURANT * ring
            if tile == 0:
                new = jnp.where(tile_low, new, 0.0)
            if tile == 5:
                new = jnp.where(tile_high, new, 0.0)
            old[k, r, at : at + 8] = new

    sent = []

    def send(x, out, rows, at):
        for k in range(4):
            target = out.at[rows, :, layers[k]]
            copy = pltpu.make_async_copy(x.at[k, rows.start + 4 : rows.stop + 4, 8:40], target, sems.at[at + k])
            copy.start()
            sent.append(copy)

    for t in range(4):
        now, old = (a, b) if t % 2 == 0 else (b, a)

        def row(r):
            for tile in range(6) if t < 3 else range(1, 5):
                advance(now, old, r, tile)

        if t < 3:

            @pl.when(jnp.logical_not(first))
            def _():
                for r in range(t + 1, 4):
                    row(r)

        for r in range(4, 20):
            row(r)
            if t == 3 and r in (11, 19):
                send(a, out_next, slice(r - 11, r - 3), 36 + 4 * (r // 19))
        if t < 3:

            @pl.when(jnp.logical_not(last))
            def _():
                for r in range(20, XE - 1 - t):
                    row(r)

        if t == 2:
            send(b, out_last, slice(0, 16), 32)
    for copy in sent:
        copy.wait()


def split(x):
    high = x.astype(jnp.bfloat16)
    low = (x - high.astype(jnp.float32)).astype(jnp.bfloat16)
    return jnp.concatenate([high, low], axis=0)


def to_columns(x, chooser):
    n = x.shape[0]
    both = lax.dot_general(split(x), chooser, (((1,), (0,)), ((), ())), preferred_element_type=jnp.float32)
    return both[0:n] + both[n : 2 * n]


def to_rows(x, chooser):
    n = x.shape[0]
    both = lax.dot_general(split(x), chooser, (((1,), (1,)), ((), ())), preferred_element_type=jnp.float32)
    return both[0:n] + both[n : 2 * n]


def chooser_of(air_row):
    rows = lax.broadcasted_iota(jnp.int32, (WINDOW, COLS), 0) + ROW0
    return jnp.where(rows == air_row[...], 1.0, 0.0).astype(jnp.bfloat16)


def beside(field):
    n = field.shape[1]
    lane = lanes(field.shape)
    left = jnp.where(lane == 0, 0.0, pltpu.roll(field, 1, 1))
    right = jnp.where(lane == n - 1, 0.0, pltpu.roll(field, n - 1, 1))
    return left + right + pltpu.roll(field, 1, 0) + pltpu.roll(field, field.shape[0] - 1, 0)


def curve(field):
    return beside(field) - 4.0 * field


def inside(shape):
    tall = lax.axis_index("gx")
    row = sublanes(shape)
    low = jnp.where(tall == 0, 4, 0)
    high = jnp.where(tall == GX - 1, 20, 24)
    return (row >= low) & (row < high)


def membrane_kernel(
    members, jumps, hlow, hhigh, air_row, after, sums, start, mono1, mono2, force2, force3, source0, source1, parts, slab
):
    tall = lax.axis_index("gx")
    first, last = tall == 0, tall == GX - 1
    for i, n in enumerate(STRIPE_ROWS):
        row = sum(STRIPE_ROWS[:i])
        if i < 3:
            ref, at, own, width = parts, XE * i, members[16 * i : 16 * i + 16], COLS
        else:
            ref, at, own, width = slab, XE * (i - 3), jumps[16 * (i - 3) : 16 * (i - 3) + 16], WINDOW
        ref[at + 4 : at + 20] = own
        if n < 4:
            ref[at : at + 4 - n] = jnp.zeros((4 - n, width), jnp.float32)
            ref[at + 20 + n : at + 24] = jnp.zeros((4 - n, width), jnp.float32)
        low, high = at + 4 - n, at + 20
        if i < 3:
            ref[low : low + n] = jnp.where(edge_free((n, width), first), hlow[row : row + n, :], 0.0)
            ref[high : high + n] = jnp.where(edge_free((n, width), last), hhigh[row : row + n, :], 0.0)
        else:
            for j in range(n):
                slot, lane = stripe_slot(row + j)
                here = slice(lane, lane + WINDOW)
                ref[low + j : low + j + 1] = jnp.where(edge_free((1, width), first), hlow[slot : slot + 1, here], 0.0)
                ref[high + j : high + j + 1] = jnp.where(edge_free((1, width), last), hhigh[slot : slot + 1, here], 0.0)
    within = inside((XE, WINDOW))

    def spread(x):
        return jnp.where(within, beside(x), 0.0)

    older = [slab[96 + XE * k : 96 + XE * (k + 1)] for k in range(3)] + [None]
    newer = [slab[XE * k : XE * (k + 1)] for k in range(4)]
    free = [newer[0]]
    for t in range(3):
        step = []
        for k in range(3 - t):
            own = 2.0 - (7.0 if k == 0 else 6.0) * COURANT
            ring = spread(newer[k]) + newer[k + 1]
            if k:
                ring = ring + newer[k - 1]
            step.append(own * newer[k] - older[k] + COURANT * ring)
        older, newer = newer, step
        free.append(newer[0])
    chooser = chooser_of(air_row)
    u0, w0, m0 = parts[0:24], parts[24:48], parts[48:72]
    start[0:24] = u0
    start[24:48] = m0
    free = to_columns(jnp.concatenate(free, axis=0), chooser)
    force3[...] = free[72:96]
    drive, stiff = FORCE * m0, SPEED * m0
    row = sublanes((XE, COLS))
    mine = (row >= HALO) & (row < HALO + BX)
    totals = []

    def gram(fields, curves):
        for i in range(len(fields)):
            for j in range(i, len(fields)):
                product = fields[i] * curves[j]
                part = product[:, 0:128]
                for k in range(1, COLS // 128):
                    part = part + product[:, 128 * k : 128 * (k + 1)]
                totals.append(jnp.sum(part, axis=0, keepdims=True))

    def masked(curves):
        return [jnp.where(mine, -c, 0.0) for c in curves]

    c0 = curve(u0)
    gram([u0], masked([c0]))
    a0 = [drive * free[0:24], stiff * c0]
    u1 = [2.0 * u0 - w0 + a0[0], a0[1]]
    mono1[0:24] = u1[0]
    mono1[24:48] = u1[1]
    c1 = [curve(x) for x in u1]
    gram(u1, masked(c1))
    s0 = to_rows(jnp.concatenate(a0, axis=0), chooser)
    source0[...] = s0
    f1 = to_columns(-s0, chooser)
    a1 = [drive * (free[24:48] + f1[0:24]), drive * f1[24:48], stiff * c1[0], stiff * c1[1]]
    u2 = [2.0 * u1[0] - u0 + a1[0], 2.0 * u1[1] + a1[1], a1[2], a1[3]]
    for i in range(4):
        mono2[24 * i : 24 * (i + 1)] = u2[i]
    c2 = [curve(x) for x in u2]
    gram(u2, masked(c2))
    s1 = to_rows(jnp.concatenate(a1, axis=0), chooser)
    source1[...] = s1
    jump2 = []
    for i in range(4):
        half = SOURCE * s1[24 * i : 24 * (i + 1)]
        if i < 2:
            g1 = SOURCE * s0[24 * i : 24 * (i + 1)]
            half = half + (2.0 - 7.0 * COURANT) * g1 + COURANT * spread(g1)
        jump2.append(-2.0 * half)
    f2 = to_columns(jnp.concatenate(jump2, axis=0), chooser)
    f2 = [f2[24 * i : 24 * (i + 1)] for i in range(4)]
    f2[0] = f2[0] + free[48:72]
    for i in range(4):
        force2[24 * i : 24 * (i + 1)] = f2[i]
    u3 = [2.0 * u2[i] + drive * f2[i] for i in range(4)] + [stiff * c for c in c2]
    u3[0] = u3[0] - u1[0]
    u3[1] = u3[1] - u1[1]
    gram(u3, masked([curve(x) for x in u3]))

    count = len(totals)
    stack = jnp.concatenate(totals + [jnp.zeros((56 - count, 128), jnp.float32)], axis=0)
    column = jnp.sum(stack, axis=1, keepdims=True)
    diagonal = jnp.where(sublanes((56, 128)) == lanes((56, 128)), column, 0.0)
    sums[...] = jnp.sum(diagonal, axis=0, keepdims=True)


def quadratic(sums, at, monos):
    total = 0.0
    for i in range(len(monos)):
        for j in range(i, len(monos)):
            term = monos[i] * (sums(at) * monos[j])
            total = total + (term if i == j else 2.0 * term)
            at += 1
    return total


def finish_kernel(
    share0, share1, share2, share3, air_row, start, mono1, mono2, force2, force3, source0, source1, next_in, last_in,
    out_next, out_last, out_u, out_w, plane_next, plane_last, fields, wide_rows, turned, sems,
):
    wide = lax.axis_index("gy")
    reached = (wide >= FIRST) & (wide <= LAST)
    loads = [
        pltpu.make_async_copy(next_in.at[:, :, MID - 128 : MID + 128], plane_next, sems.at[0]),
        pltpu.make_async_copy(last_in.at[:, :, MID - 128 : MID + 128], plane_last, sems.at[1]),
    ]

    @pl.when(reached)
    def _():
        for copy in loads:
            copy.start()

    def tension(energy):
        return 1.0 + BERGER * energy / NODES

    def sums(at):
        return (share0[0, at] + share1[0, at]) + (share2[0, at] + share3[0, at])

    t0 = tension(sums(0))
    t1 = tension(quadratic(sums, 1, [1.0, t0]))
    four = [1.0, t0, t1, t0 * t1]
    t2 = tension(quadratic(sums, 4, four))
    t3 = tension(quadratic(sums, 14, four + [t2 * x for x in four]))

    def mixed(ref, factors):
        total = ref[0:24]
        for i in range(1, len(factors)):
            total = total + factors[i] * ref[24 * i : 24 * (i + 1)]
        return total

    chooser = chooser_of(air_row)
    m0 = start[24:48]
    drive, stiff = FORCE * m0, SPEED * m0
    u1 = mixed(mono1, four[:2])
    u2 = mixed(mono2, four)
    a2 = stiff * (t2 * curve(u2)) + drive * mixed(force2, four)
    u3 = 2.0 * u2 - u1 + a2
    s0 = mixed(source0, four[:2])
    s1 = mixed(source1, four)
    s2 = to_rows(a2, chooser)
    within = inside((XE, WINDOW))

    def spread(x):
        return jnp.where(within, beside(x), 0.0)

    g1 = SOURCE * s0
    g2 = [SOURCE * s1 + (2.0 - 7.0 * COURANT) * g1 + COURANT * spread(g1), COURANT * g1]
    g3 = [
        SOURCE * s2 + (2.0 - 7.0 * COURANT) * g2[0] - g1 + COURANT * (spread(g2[0]) + g2[1]),
        (2.0 - 6.0 * COURANT) * g2[1] + COURANT * (spread(g2[1]) + g2[0]),
        COURANT * g2[1],
    ]
    f3 = to_columns(-2.0 * g3[0], chooser)
    a3 = stiff * (t3 * curve(u3)) + drive * (f3 + force3[...])
    u4 = 2.0 * u3 - u2 + a3

    tile = pl.ds(pl.multiple_of(128 * (wide // 4), 128), 128)
    back = lax.rem(128 - 32 * lax.rem(wide, 4), 128)
    fields[0:24] = u4
    fields[24:48] = u3
    out_u[...] = pltpu.roll(fields[4:20, tile], back, 1)[:, 0:BY]
    out_w[...] = pltpu.roll(fields[28:44, tile], back, 1)[:, 0:BY]

    @pl.when(reached)
    def _():
        s3 = to_rows(a3, chooser)
        g4 = [
            SOURCE * s3 + (2.0 - 7.0 * COURANT) * g3[0] - g2[0] + COURANT * (spread(g3[0]) + g3[1]),
            (2.0 - 6.0 * COURANT) * g3[1] - g2[1] + COURANT * (spread(g3[1]) + g3[0] + g3[2]),
            (2.0 - 6.0 * COURANT) * g3[2] + COURANT * (spread(g3[2]) + g3[1]),
            COURANT * g3[2],
        ]
        tile = pl.ds(pl.multiple_of(128 * (wide // 4 - ROW0 // 128), 128), 128)
        for copy in loads:
            copy.wait()
        for gains, plane in ((g4, plane_next), (g3 + [None], plane_last)):
            for k in range(4):
                if gains[k] is None:
                    turned[pl.ds(k, BX, stride=8), :] = jnp.zeros((BX, 128), jnp.float32)
                    turned[pl.ds(7 - k, BX, stride=8), :] = jnp.zeros((BX, 128), jnp.float32)
                    continue
                wide_rows[...] = gains[k]
                part = pltpu.roll(wide_rows[4:20, tile], back, 1)
                turned[pl.ds(k, BX, stride=8), :] = part
                turned[pl.ds(7 - k, BX, stride=8), :] = -part
            across = jnp.transpose(turned[...])[0:BY]
            lane = lanes((BY, 128))
            for x in range(BX):
                above = jnp.where(lane < 4, pltpu.roll(across, (128 - 8 * x) % 128, 1), 0.0)
                below = jnp.where(lane >= 124, pltpu.roll(across, (120 - 8 * x) % 128, 1), 0.0)
                plane[x, :, 0:128] = plane[x, :, 0:128] + below
                plane[x, :, 128:256] = plane[x, :, 128:256] + above
        stores = [
            pltpu.make_async_copy(plane_next, out_next.at[:, :, MID - 128 : MID + 128], sems.at[2]),
            pltpu.make_async_copy(plane_last, out_last.at[:, :, MID - 128 : MID + 128], sems.at[3]),
        ]
        for copy in stores:
            copy.start()
        for copy in stores:
            copy.wait()


def ring(count, by):
    return [(i, (i + by) % count) for i in range(count)]


def across(count, by):
    return [(i, (i + 2 * by) % count if by else i ^ 1) for i in range(count)]


def per_device(air_now, air_prev, membrane_now, membrane_prev, inv_mass, air_row):
    def sems(n):
        return pltpu.SemaphoreType.DMA((n,))

    halo_x, halo_y, own_y, stripe = f32(7, BY, NZ), f32(XE, 8, NZ), f32(BX, 8, NZ), f32(19, COLS)
    listed = air_row.reshape(1, COLS)
    air_now, air_prev, membrane_now, membrane_prev, inv_mass = (
        pltpu.with_memory_space_constraint(x, pltpu.HBM)
        for x in (air_now, air_prev, membrane_now, membrane_prev, inv_mass)
    )
    block = pl.pallas_call(
        block_kernel,
        out_shape=f32(GY, FOLD, 128),
        in_specs=[HBM] * 5,
        out_specs=WHOLE,
        scratch_shapes=[
            VMEM((2, BX, BY, 256), jnp.float32),
            VMEM((3, BX, BY), jnp.float32),
            VMEM((2, 128, 128), jnp.float32),
            VMEM((PACK, 128), jnp.float32),
            sems(5),
        ],
        compiler_params=granted(6),
        name="block",
    )(air_now, air_prev, membrane_now, membrane_prev, inv_mass)
    to_xlow, to_xhigh, to_ylow, to_yhigh = pl.pallas_call(
        pack_kernel,
        out_shape=(halo_x, halo_x, own_y, own_y),
        in_specs=[HBM] * 2 + [ANY],
        out_specs=(WHOLE,) * 4,
        scratch_shapes=[VMEM((4, BX, 8, NZ), jnp.float32), sems(8)],
        compiler_params=granted(4),
        name="pack",
    )(air_now, air_prev, block)
    blocks = lax.all_to_all(block, "gy", 0, 0)
    xlow = lax.ppermute(to_xhigh, "gx", ring(GX, 1))
    xhigh = lax.ppermute(to_xlow, "gx", ring(GX, -1))
    members, jumps, to_low, to_high = pl.pallas_call(
        unfold_kernel,
        out_shape=(f32(48, COLS), f32(112, WINDOW), stripe, stripe),
        in_specs=[WHOLE],
        out_specs=(WHOLE,) * 4,
        compiler_params=granted(3),
        name="unfold",
    )(blocks)
    hlow = lax.ppermute(to_high, "gx", ring(GX, 1))
    hhigh = lax.ppermute(to_low, "gx", ring(GX, -1))
    to_ylow, to_yhigh = pl.pallas_call(
        corner_kernel,
        out_shape=(halo_y, halo_y),
        in_specs=[WHOLE] * 2 + [ANY] * 2,
        out_specs=(HBM,) * 2,
        scratch_shapes=[VMEM((2, 2, 4, 8, NZ), jnp.float32), sems(6)],
        compiler_params=granted(3),
        name="corners",
    )(xlow, xhigh, to_ylow, to_yhigh)
    ylow = lax.ppermute(to_yhigh, "gy", ring(GY, 1))
    yhigh = lax.ppermute(to_ylow, "gy", ring(GY, -1))
    air = f32(BX, BY, NZ)
    *staged, done = pl.pallas_call(
        stage_kernel,
        out_shape=(air, air, f32(8, 128)),
        in_specs=[HBM] * 2 + [ANY],
        out_specs=(WHOLE,) * 3,
        scratch_shapes=[sems(2)],
        compiler_params=granted(3),
        cost_estimate=pl.CostEstimate(flops=0, bytes_accessed=8_000_000, transcendentals=0),
        name="stage",
    )(air_now, air_prev, to_low)
    brick = VMEM((4, XE, YE, 128), jnp.float32)
    next_free, last_free = pl.pallas_call(
        air_kernel,
        out_shape=(air, air),
        in_specs=[ANY] * 6,
        out_specs=(HBM, HBM),
        scratch_shapes=[brick, brick, sems(44)],
        compiler_params=granted(8),
        cost_estimate=pl.CostEstimate(flops=40_000_000, bytes_accessed=8_000_000, transcendentals=0),
        name="air_free",
    )(*staged, xlow, xhigh, ylow, yhigh)
    sums, *saved = pl.pallas_call(
        membrane_kernel,
        out_shape=(
            f32(1, 128), f32(48, COLS), f32(48, COLS), f32(96, COLS), f32(96, COLS), f32(24, COLS),
            f32(48, WINDOW), f32(96, WINDOW),
        ),
        in_specs=[WHOLE] * 5 + [ANY],
        out_specs=(WHOLE,) * 8,
        scratch_shapes=[
            VMEM((3 * XE, COLS), jnp.float32),
            VMEM((7 * XE, WINDOW), jnp.float32),
        ],
        compiler_params=granted(10),
        name="membrane",
    )(members, jumps, hlow, hhigh, listed, done)
    sums = sums + lax.ppermute(sums, "gx", across(GX, 0))
    shares = [sums] + [lax.ppermute(sums, "gx", across(GX, by)) for by in (1, 2, 3)]
    return pl.pallas_call(
        finish_kernel,
        out_shape=(air, air, f32(BX, BY), f32(BX, BY)),
        in_specs=[pl.BlockSpec(memory_space=pltpu.SMEM)] * 4 + [WHOLE] * 8 + [HBM, HBM],
        out_specs=(HBM, HBM, WHOLE, WHOLE),
        scratch_shapes=[
            VMEM((BX, BY, 256), jnp.float32),
            VMEM((BX, BY, 256), jnp.float32),
            VMEM((48, COLS), jnp.float32),
            VMEM((XE, WINDOW), jnp.float32),
            VMEM((128, 128), jnp.float32),
            sems(4),
        ],
        input_output_aliases={12: 0, 13: 1},
        compiler_params=granted(8),
        name="finish",
    )(*shares, listed, *saved, next_free, last_free)


def solution(mesh):
    in_specs = (
        P("gx", "gy", None),
        P("gx", "gy", None),
        P("gx", "gy"),
        P("gx", "gy"),
        P("gx", "gy"),
        P(),
    )
    out_specs = (P("gx", "gy", None), P("gx", "gy", None), P("gx", "gy"), P("gx", "gy"))
    return jax.shard_map(
        per_device, mesh=mesh, in_specs=in_specs, out_specs=out_specs, check_vma=False
    )
```

```python
import functools

import jax
import jax.numpy as jnp
from jax import lax
from jax.experimental import pallas as pl
from jax.experimental.pallas import tpu as pltpu
from jax.sharding import PartitionSpec as P

COURANT = 0.32
SPEED = 0.08
BERGER = 0.4
FORCE = 0.1
SOURCE = 0.5

GX, GY = 8, 32
BX, BY, NZ = 16, 32, 512
MID = NZ // 2
COLS = GY * BY
NODES = GX * BX * COLS
HALO = 4
XE = BX + 2 * HALO
YE = BY + 16
WINDOW = 384
ROW0 = COLS - WINDOW
FIRST, LAST = 22, 30
PACK = 160
FOLD = 40
STRIPE_ROWS = (4, 3, 3, 3, 3, 3, 3, 2, 2, 2)

VMEM = pltpu.VMEM
WHOLE = pl.BlockSpec(memory_space=pltpu.VMEM)
ANY = pl.BlockSpec(memory_space=pl.ANY)
HBM = pl.BlockSpec(memory_space=pltpu.HBM)


def granted(mib):
    return pltpu.CompilerParams(vmem_limit_bytes=mib * 1024 * 1024)


def f32(*shape):
    return jax.ShapeDtypeStruct(shape, jnp.float32)


def lanes(shape):
    return lax.broadcasted_iota(jnp.int32, shape, len(shape) - 1)


def sublanes(shape):
    return lax.broadcasted_iota(jnp.int32, shape, len(shape) - 2)


def fold(rows, wide):
    quarter = lanes((FOLD, 128)) // 32
    folded = rows[0:FOLD, :]
    for g in range(1, 4):
        folded = jnp.where(quarter == g, pltpu.roll(rows[FOLD * g : FOLD * (g + 1), :], 32 * g, 1), folded)
    return pltpu.roll(folded, 32 * lax.rem(wide, 4), 1)


def started(pairs, sems):
    copies = [pltpu.make_async_copy(x, y, sems.at[i]) for i, (x, y) in enumerate(pairs)]
    for copy in copies:
        copy.start()
    return copies


def block_kernel(p, q, u, w, m, block, planes, members, turned, rows, sems):
    wide = lax.axis_index("gy")
    middle = slice(MID - 128, MID + 128)
    pairs = [(p.at[:, :, middle], planes.at[0]), (q.at[:, :, middle], planes.at[1])]
    copies = started(pairs + [(x, members.at[i]) for i, x in enumerate((u, w, m))], sems)
    lane = lanes((BY, 128))
    for i in range(2):
        copies[i].wait()
        total = jnp.zeros((BY, 128), jnp.float32)
        for x in range(BX):
            above = pltpu.roll(planes[i, x, :, 128:256], 8 * x, 1)
            below = pltpu.roll(planes[i, x, :, 0:128], (8 * x + 8) % 128, 1)
            total = jnp.where((lane >= 8 * x) & (lane < 8 * x + 4), above, total)
            total = jnp.where((lane >= 8 * x + 4) & (lane < 8 * x + 8), below, total)
        turned[i, 0:BY, :] = total
        turned[i, BY:128, :] = jnp.zeros((128 - BY, 128), jnp.float32)
        turned[i] = jnp.transpose(turned[i])
        for k in range(4 - i):
            at = 48 + 64 * i + 16 * k
            rows[at : at + 16, :] = turned[i, pl.ds(7 - k, BX, stride=8), :] - turned[i, pl.ds(k, BX, stride=8), :]
    for i in range(3):
        copies[2 + i].wait()
        rows[16 * i : 16 * i + 16, 0:BY] = members[i]
    folded = fold(rows, wide)
    for i in range(GY):
        block[i] = folded


def tips_kernel(p, q, after, xlow, xhigh, sems):
    pairs = [
        (p.at[0:4], xlow.at[0:4]),
        (q.at[0:3], xlow.at[4:7]),
        (p.at[12:16], xhigh.at[0:4]),
        (q.at[13:16], xhigh.at[4:7]),
    ]
    for copy in started(pairs, sems):
        copy.wait()


def sides_kernel(p, q, after, ylow, yhigh, edges, sems):
    pairs = [(x.at[:, at : at + 8], edges.at[i]) for i, (x, at) in enumerate(((p, 0), (q, 0), (p, 24), (q, 24)))]
    for copy in started(pairs, sems):
        copy.wait()
    lower = sublanes((8, NZ)) < 4
    for r in range(BX):
        ylow[r] = jnp.where(lower, edges[0, r], pltpu.roll(edges[1, r], 4, 0))
        yhigh[r] = jnp.where(lower, pltpu.roll(edges[3, r], 4, 0), edges[2, r])


def corner_kernel(xlow, xhigh, own_low, own_high, out_ylow, out_yhigh, corners, sems):
    copies = [
        pltpu.make_async_copy(own, out.at[4:20], sems.at[4 + i])
        for i, (own, out) in enumerate(((own_low, out_ylow), (own_high, out_yhigh)))
    ]
    for copy in copies:
        copy.start()
    lower = sublanes((8, NZ)) < 4
    for i in range(4):
        for at, halo, j in ((0, xlow, 4 + max(i - 1, 0)), (1, xhigh, 4 + min(i, 2))):
            corners[0, at, i] = jnp.where(lower, halo[i, 0:8], pltpu.roll(halo[j, 0:8], 4, 0))
            corners[1, at, i] = jnp.where(lower, pltpu.roll(halo[j, 24:32], 4, 0), halo[i, 24:32])
    for i, out in enumerate((out_ylow, out_yhigh)):
        for at in range(2):
            copy = pltpu.make_async_copy(corners.at[i, at], out.at[20 * at : 20 * at + 4], sems.at[2 * i + at])
            copy.start()
            copies.append(copy)
    for copy in copies:
        copy.wait()


def stripe_slot(row):
    return 10 + (row - 10) // 2, 512 * (row % 2)


def unfold_kernel(blocks, members, jumps, to_low, to_high):
    quarter = lanes((FOLD, 128)) // 32
    for g in range(4):
        for t in range(8):
            if g >= 2 and t < 5:
                continue
            merged = blocks[4 * t + (-g) % 4]
            for s in range(1, 4):
                merged = jnp.where(quarter == s, blocks[4 * t + (s - g) % 4], merged)
            merged = pltpu.roll(merged, (128 - 32 * g) % 128, 1)
            column = slice(128 * t, 128 * (t + 1))
            narrow = slice(128 * (t - 5), 128 * (t - 4))
            if g == 0:
                members[0:40, column] = merged
            elif g == 1:
                members[40:48, column] = merged[0:8]
                if t >= 5:
                    jumps[0:32, narrow] = merged[8:40]
            else:
                jumps[40 * g - 48 : 40 * g - 8, narrow] = merged
    for out, end in ((to_low, 0), (to_high, BX)):
        for i, n in enumerate(STRIPE_ROWS):
            row, at = sum(STRIPE_ROWS[:i]), 16 * i + (end - n if end else 0)
            if i < 3:
                out[row : row + n, :] = members[at : at + n, :]
            else:
                for j in range(n):
                    slot, lane = stripe_slot(row + j)
                    out[slot : slot + 1, lane : lane + WINDOW] = jumps[at - 48 + j : at - 47 + j, :]


def edge_free(shape, edge):
    return jnp.broadcast_to(edge.astype(jnp.int32), shape) == 0


def stage_kernel(p, q, after, out_p, out_q, done, sems):
    copies = started([(p, out_p), (q, out_q)], sems)
    done[...] = jnp.zeros((8, 128), jnp.float32)
    for copy in copies:
        copy.wait()


def air_kernel(p, q, xlow, xhigh, ylow, yhigh, out_next, out_last, a, b, sems):
    tall = lax.axis_index("gx")
    wide = lax.axis_index("gy")
    first, last = tall == 0, tall == GX - 1
    bottom, top = wide == 0, wide == GY - 1
    layers = [slice(128 * k, 128 * (k + 1)) for k in range(4)]
    pairs = []
    for k in range(4):
        z = layers[k]
        pairs += [
            (p.at[:, :, z], a.at[k, 4:20, 8:40]),
            (q.at[:, :, z], b.at[k, 4:20, 8:40]),
            (xlow.at[0:4, :, z], a.at[k, 0:4, 8:40]),
            (xlow.at[4:7, :, z], b.at[k, 1:4, 8:40]),
            (xhigh.at[0:4, :, z], a.at[k, 20:24, 8:40]),
            (xhigh.at[4:7, :, z], b.at[k, 20:23, 8:40]),
            (ylow.at[:, :, z], a.at[k, :, 0:8]),
            (yhigh.at[:, :, z], a.at[k, :, 40:48]),
        ]
    copies = [pltpu.make_async_copy(x, y, sems.at[i]) for i, (x, y) in enumerate(pairs)]
    for copy in copies:
        copy.start()
    for copy in copies:
        copy.wait()

    def cleared(edge, ref, at):
        @pl.when(edge)
        def _():
            for k in range(4):
                ref.at[(k, *at)][...] = jnp.zeros(ref.at[(k, *at)].shape, jnp.float32)

    cleared(first, a, (slice(0, 4),))
    cleared(first, b, (slice(1, 4),))
    cleared(last, a, (slice(20, 24),))
    cleared(last, b, (slice(20, 23),))
    cleared(bottom, a, (slice(0, XE), slice(0, 8)))
    cleared(top, a, (slice(0, XE), slice(40, 48)))
    for k in range(4):
        for r in range(1, XE - 1):
            b[k, r, 0:8] = pltpu.roll(a[k, r, 0:8], 4, 0)
            b[k, r, 40:48] = pltpu.roll(a[k, r, 40:48], 4, 0)

    tile_low, tile_high = edge_free((8, 128), bottom), edge_free((8, 128), top)
    lane = lanes((8, 128))

    def advance(now, old, r, tile):
        at = 8 * tile
        c = [now[k, r, at : at + 8] for k in range(4)]
        up = [pltpu.roll(x, 1, 1) for x in c]
        down = [pltpu.roll(x, 127, 1) for x in c]
        for k in range(4):
            left = jnp.where(lane == 0, up[k - 1] if k else 0.0, up[k])
            right = jnp.where(lane == 127, down[k + 1] if k < 3 else 0.0, down[k])
            if tile > 0:
                before = now[k, r, at - 1 : at + 7]
            else:
                before = pltpu.roll(c[k], 1, 0)
            if tile < 5:
                after = now[k, r, at + 1 : at + 9]
            else:
                after = pltpu.roll(c[k], 7, 0)
            ring = (left + right) + (before + after) + (now[k, r - 1, at : at + 8] + now[k, r + 1, at : at + 8])
            new = (2.0 - 6.0 * COURANT) * c[k] - old[k, r, at : at + 8] + COURANT * ring
            if tile == 0:
                new = jnp.where(tile_low, new, 0.0)
            if tile == 5:
                new = jnp.where(tile_high, new, 0.0)
            old[k, r, at : at + 8] = new

    sent = []

    def send(x, out, rows, at):
        for k in range(4):
            target = out.at[rows, :, layers[k]]
            copy = pltpu.make_async_copy(x.at[k, rows.start + 4 : rows.stop + 4, 8:40], target, sems.at[at + k])
            copy.start()
            sent.append(copy)

    for t in range(4):
        now, old = (a, b) if t % 2 == 0 else (b, a)

        def row(r):
            for tile in range(6) if t < 3 else range(1, 5):
                advance(now, old, r, tile)

        if t < 3:

            @pl.when(jnp.logical_not(first))
            def _():
                for r in range(t + 1, 4):
                    row(r)

        for r in range(4, 20):
            row(r)
            if t == 3 and r in (11, 19):
                send(a, out_next, slice(r - 11, r - 3), 36 + 4 * (r // 19))
        if t < 3:

            @pl.when(jnp.logical_not(last))
            def _():
                for r in range(20, XE - 1 - t):
                    row(r)

        if t == 2:
            send(b, out_last, slice(0, 16), 32)
    for copy in sent:
        copy.wait()


def split(x):
    high = x.astype(jnp.bfloat16)
    low = (x - high.astype(jnp.float32)).astype(jnp.bfloat16)
    return jnp.concatenate([high, low], axis=0)


def to_columns(x, chooser):
    n = x.shape[0]
    both = lax.dot_general(split(x), chooser, (((1,), (0,)), ((), ())), preferred_element_type=jnp.float32)
    return both[0:n] + both[n : 2 * n]


def to_rows(x, chooser):
    n = x.shape[0]
    both = lax.dot_general(split(x), chooser, (((1,), (1,)), ((), ())), preferred_element_type=jnp.float32)
    return both[0:n] + both[n : 2 * n]


def chooser_of(air_row):
    rows = lax.broadcasted_iota(jnp.int32, (WINDOW, COLS), 0) + ROW0
    return jnp.where(rows == air_row[...], 1.0, 0.0).astype(jnp.bfloat16)


def beside(field):
    n = field.shape[1]
    lane = lanes(field.shape)
    left = jnp.where(lane == 0, 0.0, pltpu.roll(field, 1, 1))
    right = jnp.where(lane == n - 1, 0.0, pltpu.roll(field, n - 1, 1))
    return left + right + pltpu.roll(field, 1, 0) + pltpu.roll(field, field.shape[0] - 1, 0)


def curve(field):
    return beside(field) - 4.0 * field


def inside(shape):
    tall = lax.axis_index("gx")
    row = sublanes(shape)
    low = jnp.where(tall == 0, 4, 0)
    high = jnp.where(tall == GX - 1, 20, 24)
    return (row >= low) & (row < high)


def membrane_kernel(
    members, jumps, hlow, hhigh, air_row, after, sums, start, mono1, mono2, force2, force3, source0, source1, parts, slab
):
    tall = lax.axis_index("gx")
    first, last = tall == 0, tall == GX - 1
    for i, n in enumerate(STRIPE_ROWS):
        row = sum(STRIPE_ROWS[:i])
        if i < 3:
            ref, at, own, width = parts, XE * i, members[16 * i : 16 * i + 16], COLS
        else:
            ref, at, own, width = slab, XE * (i - 3), jumps[16 * (i - 3) : 16 * (i - 3) + 16], WINDOW
        ref[at + 4 : at + 20] = own
        if n < 4:
            ref[at : at + 4 - n] = jnp.zeros((4 - n, width), jnp.float32)
            ref[at + 20 + n : at + 24] = jnp.zeros((4 - n, width), jnp.float32)
        low, high = at + 4 - n, at + 20
        if i < 3:
            ref[low : low + n] = jnp.where(edge_free((n, width), first), hlow[row : row + n, :], 0.0)
            ref[high : high + n] = jnp.where(edge_free((n, width), last), hhigh[row : row + n, :], 0.0)
        else:
            for j in range(n):
                slot, lane = stripe_slot(row + j)
                here = slice(lane, lane + WINDOW)
                ref[low + j : low + j + 1] = jnp.where(edge_free((1, width), first), hlow[slot : slot + 1, here], 0.0)
                ref[high + j : high + j + 1] = jnp.where(edge_free((1, width), last), hhigh[slot : slot + 1, here], 0.0)
    within = inside((XE, WINDOW))

    def spread(x):
        return jnp.where(within, beside(x), 0.0)

    older = [slab[96 + XE * k : 96 + XE * (k + 1)] for k in range(3)] + [None]
    newer = [slab[XE * k : XE * (k + 1)] for k in range(4)]
    free = [newer[0]]
    for t in range(3):
        step = []
        for k in range(3 - t):
            own = 2.0 - (7.0 if k == 0 else 6.0) * COURANT
            ring = spread(newer[k]) + newer[k + 1]
            if k:
                ring = ring + newer[k - 1]
            step.append(own * newer[k] - older[k] + COURANT * ring)
        older, newer = newer, step
        free.append(newer[0])
    chooser = chooser_of(air_row)
    u0, w0, m0 = parts[0:24], parts[24:48], parts[48:72]
    start[0:24] = u0
    start[24:48] = m0
    free = to_columns(jnp.concatenate(free, axis=0), chooser)
    force3[...] = free[72:96]
    drive, stiff = FORCE * m0, SPEED * m0
    row = sublanes((XE, COLS))
    mine = (row >= HALO) & (row < HALO + BX)
    totals = []

    def gram(fields, curves):
        for i in range(len(fields)):
            for j in range(i, len(fields)):
                product = fields[i] * curves[j]
                part = product[:, 0:128]
                for k in range(1, COLS // 128):
                    part = part + product[:, 128 * k : 128 * (k + 1)]
                totals.append(jnp.sum(part, axis=0, keepdims=True))

    def masked(curves):
        return [jnp.where(mine, -c, 0.0) for c in curves]

    c0 = curve(u0)
    gram([u0], masked([c0]))
    a0 = [drive * free[0:24], stiff * c0]
    u1 = [2.0 * u0 - w0 + a0[0], a0[1]]
    mono1[0:24] = u1[0]
    mono1[24:48] = u1[1]
    c1 = [curve(x) for x in u1]
    gram(u1, masked(c1))
    s0 = to_rows(jnp.concatenate(a0, axis=0), chooser)
    source0[...] = s0
    f1 = to_columns(-s0, chooser)
    a1 = [drive * (free[24:48] + f1[0:24]), drive * f1[24:48], stiff * c1[0], stiff * c1[1]]
    u2 = [2.0 * u1[0] - u0 + a1[0], 2.0 * u1[1] + a1[1], a1[2], a1[3]]
    for i in range(4):
        mono2[24 * i : 24 * (i + 1)] = u2[i]
    c2 = [curve(x) for x in u2]
    gram(u2, masked(c2))
    s1 = to_rows(jnp.concatenate(a1, axis=0), chooser)
    source1[...] = s1
    jump2 = []
    for i in range(4):
        half = SOURCE * s1[24 * i : 24 * (i + 1)]
        if i < 2:
            g1 = SOURCE * s0[24 * i : 24 * (i + 1)]
            half = half + (2.0 - 7.0 * COURANT) * g1 + COURANT * spread(g1)
        jump2.append(-2.0 * half)
    f2 = to_columns(jnp.concatenate(jump2, axis=0), chooser)
    f2 = [f2[24 * i : 24 * (i + 1)] for i in range(4)]
    f2[0] = f2[0] + free[48:72]
    for i in range(4):
        force2[24 * i : 24 * (i + 1)] = f2[i]
    u3 = [2.0 * u2[i] + drive * f2[i] for i in range(4)] + [stiff * c for c in c2]
    u3[0] = u3[0] - u1[0]
    u3[1] = u3[1] - u1[1]
    gram(u3, masked([curve(x) for x in u3]))

    count = len(totals)
    stack = jnp.concatenate(totals + [jnp.zeros((56 - count, 128), jnp.float32)], axis=0)
    column = jnp.sum(stack, axis=1, keepdims=True)
    diagonal = jnp.where(sublanes((56, 128)) == lanes((56, 128)), column, 0.0)
    sums[...] = jnp.sum(diagonal, axis=0, keepdims=True)


def quadratic(sums, at, monos):
    total = 0.0
    for i in range(len(monos)):
        for j in range(i, len(monos)):
            term = monos[i] * (sums(at) * monos[j])
            total = total + (term if i == j else 2.0 * term)
            at += 1
    return total


def finish_kernel(
    share0, share1, share2, share3, air_row, start, mono1, mono2, force2, force3, source0, source1, next_in, last_in,
    out_next, out_last, out_u, out_w, plane_next, plane_last, fields, wide_rows, turned, sems,
):
    wide = lax.axis_index("gy")
    reached = (wide >= FIRST) & (wide <= LAST)
    loads = [
        pltpu.make_async_copy(next_in.at[:, :, MID - 128 : MID + 128], plane_next, sems.at[0]),
        pltpu.make_async_copy(last_in.at[:, :, MID - 128 : MID + 128], plane_last, sems.at[1]),
    ]

    @pl.when(reached)
    def _():
        for copy in loads:
            copy.start()

    def tension(energy):
        return 1.0 + BERGER * energy / NODES

    def sums(at):
        return (share0[0, at] + share1[0, at]) + (share2[0, at] + share3[0, at])

    t0 = tension(sums(0))
    t1 = tension(quadratic(sums, 1, [1.0, t0]))
    four = [1.0, t0, t1, t0 * t1]
    t2 = tension(quadratic(sums, 4, four))
    t3 = tension(quadratic(sums, 14, four + [t2 * x for x in four]))

    def mixed(ref, factors):
        total = ref[0:24]
        for i in range(1, len(factors)):
            total = total + factors[i] * ref[24 * i : 24 * (i + 1)]
        return total

    chooser = chooser_of(air_row)
    m0 = start[24:48]
    drive, stiff = FORCE * m0, SPEED * m0
    u1 = mixed(mono1, four[:2])
    u2 = mixed(mono2, four)
    a2 = stiff * (t2 * curve(u2)) + drive * mixed(force2, four)
    u3 = 2.0 * u2 - u1 + a2
    s0 = mixed(source0, four[:2])
    s1 = mixed(source1, four)
    s2 = to_rows(a2, chooser)
    within = inside((XE, WINDOW))

    def spread(x):
        return jnp.where(within, beside(x), 0.0)

    g1 = SOURCE * s0
    g2 = [SOURCE * s1 + (2.0 - 7.0 * COURANT) * g1 + COURANT * spread(g1), COURANT * g1]
    g3 = [
        SOURCE * s2 + (2.0 - 7.0 * COURANT) * g2[0] - g1 + COURANT * (spread(g2[0]) + g2[1]),
        (2.0 - 6.0 * COURANT) * g2[1] + COURANT * (spread(g2[1]) + g2[0]),
        COURANT * g2[1],
    ]
    f3 = to_columns(-2.0 * g3[0], chooser)
    a3 = stiff * (t3 * curve(u3)) + drive * (f3 + force3[...])
    u4 = 2.0 * u3 - u2 + a3

    tile = pl.ds(pl.multiple_of(128 * (wide // 4), 128), 128)
    back = lax.rem(128 - 32 * lax.rem(wide, 4), 128)
    fields[0:24] = u4
    fields[24:48] = u3
    out_u[...] = pltpu.roll(fields[4:20, tile], back, 1)[:, 0:BY]
    out_w[...] = pltpu.roll(fields[28:44, tile], back, 1)[:, 0:BY]

    @pl.when(reached)
    def _():
        s3 = to_rows(a3, chooser)
        g4 = [
            SOURCE * s3 + (2.0 - 7.0 * COURANT) * g3[0] - g2[0] + COURANT * (spread(g3[0]) + g3[1]),
            (2.0 - 6.0 * COURANT) * g3[1] - g2[1] + COURANT * (spread(g3[1]) + g3[0] + g3[2]),
            (2.0 - 6.0 * COURANT) * g3[2] + COURANT * (spread(g3[2]) + g3[1]),
            COURANT * g3[2],
        ]
        tile = pl.ds(pl.multiple_of(128 * (wide // 4 - ROW0 // 128), 128), 128)
        for copy in loads:
            copy.wait()
        for gains, plane in ((g4, plane_next), (g3 + [None], plane_last)):
            for k in range(4):
                if gains[k] is None:
                    turned[pl.ds(k, BX, stride=8), :] = jnp.zeros((BX, 128), jnp.float32)
                    turned[pl.ds(7 - k, BX, stride=8), :] = jnp.zeros((BX, 128), jnp.float32)
                    continue
                wide_rows[...] = gains[k]
                part = pltpu.roll(wide_rows[4:20, tile], back, 1)
                turned[pl.ds(k, BX, stride=8), :] = part
                turned[pl.ds(7 - k, BX, stride=8), :] = -part
            across = jnp.transpose(turned[...])[0:BY]
            lane = lanes((BY, 128))
            for x in range(BX):
                above = jnp.where(lane < 4, pltpu.roll(across, (128 - 8 * x) % 128, 1), 0.0)
                below = jnp.where(lane >= 124, pltpu.roll(across, (120 - 8 * x) % 128, 1), 0.0)
                plane[x, :, 0:128] = plane[x, :, 0:128] + below
                plane[x, :, 128:256] = plane[x, :, 128:256] + above
        stores = [
            pltpu.make_async_copy(plane_next, out_next.at[:, :, MID - 128 : MID + 128], sems.at[2]),
            pltpu.make_async_copy(plane_last, out_last.at[:, :, MID - 128 : MID + 128], sems.at[3]),
        ]
        for copy in stores:
            copy.start()
        for copy in stores:
            copy.wait()


def ring(count, by):
    return [(i, (i + by) % count) for i in range(count)]


def across(count, by):
    return [(i, (i + 2 * by) % count if by else i ^ 1) for i in range(count)]


def per_device(air_now, air_prev, membrane_now, membrane_prev, inv_mass, air_row):
    def sems(n):
        return pltpu.SemaphoreType.DMA((n,))

    halo_x, halo_y, own_y, stripe = f32(7, BY, NZ), f32(XE, 8, NZ), f32(BX, 8, NZ), f32(19, COLS)
    listed = air_row.reshape(1, COLS)
    air_now, air_prev, membrane_now, membrane_prev, inv_mass = (
        pltpu.with_memory_space_constraint(x, pltpu.HBM)
        for x in (air_now, air_prev, membrane_now, membrane_prev, inv_mass)
    )
    block = pl.pallas_call(
        block_kernel,
        out_shape=f32(GY, FOLD, 128),
        in_specs=[HBM] * 5,
        out_specs=WHOLE,
        scratch_shapes=[
            VMEM((2, BX, BY, 256), jnp.float32),
            VMEM((3, BX, BY), jnp.float32),
            VMEM((2, 128, 128), jnp.float32),
            VMEM((PACK, 128), jnp.float32),
            sems(5),
        ],
        compiler_params=granted(6),
        name="block",
    )(air_now, air_prev, membrane_now, membrane_prev, inv_mass)
    to_xlow, to_xhigh = pl.pallas_call(
        tips_kernel,
        out_shape=(halo_x, halo_x),
        in_specs=[HBM] * 2 + [ANY],
        out_specs=(WHOLE,) * 2,
        scratch_shapes=[sems(4)],
        compiler_params=granted(3),
        name="tips",
    )(air_now, air_prev, block)
    to_ylow, to_yhigh = pl.pallas_call(
        sides_kernel,
        out_shape=(own_y, own_y),
        in_specs=[HBM] * 2 + [ANY],
        out_specs=(WHOLE,) * 2,
        scratch_shapes=[VMEM((4, BX, 8, NZ), jnp.float32), sems(4)],
        compiler_params=granted(3),
        cost_estimate=pl.CostEstimate(flops=0, bytes_accessed=8_000_000, transcendentals=0),
        name="sides",
    )(air_now, air_prev, to_xlow)
    blocks = lax.all_to_all(block, "gy", 0, 0)
    xlow = lax.ppermute(to_xhigh, "gx", ring(GX, 1))
    xhigh = lax.ppermute(to_xlow, "gx", ring(GX, -1))
    members, jumps, to_low, to_high = pl.pallas_call(
        unfold_kernel,
        out_shape=(f32(48, COLS), f32(112, WINDOW), stripe, stripe),
        in_specs=[WHOLE],
        out_specs=(WHOLE,) * 4,
        compiler_params=granted(3),
        name="unfold",
    )(blocks)
    hlow = lax.ppermute(to_high, "gx", ring(GX, 1))
    hhigh = lax.ppermute(to_low, "gx", ring(GX, -1))
    to_ylow, to_yhigh = pl.pallas_call(
        corner_kernel,
        out_shape=(halo_y, halo_y),
        in_specs=[WHOLE] * 2 + [ANY] * 2,
        out_specs=(HBM,) * 2,
        scratch_shapes=[VMEM((2, 2, 4, 8, NZ), jnp.float32), sems(6)],
        compiler_params=granted(3),
        name="corners",
    )(xlow, xhigh, to_ylow, to_yhigh)
    ylow = lax.ppermute(to_yhigh, "gy", ring(GY, 1))
    yhigh = lax.ppermute(to_ylow, "gy", ring(GY, -1))
    air = f32(BX, BY, NZ)
    *staged, done = pl.pallas_call(
        stage_kernel,
        out_shape=(air, air, f32(8, 128)),
        in_specs=[HBM] * 2 + [ANY],
        out_specs=(WHOLE,) * 3,
        scratch_shapes=[sems(2)],
        compiler_params=granted(3),
        cost_estimate=pl.CostEstimate(flops=0, bytes_accessed=8_000_000, transcendentals=0),
        name="stage",
    )(air_now, air_prev, to_low)
    brick = VMEM((4, XE, YE, 128), jnp.float32)
    next_free, last_free = pl.pallas_call(
        air_kernel,
        out_shape=(air, air),
        in_specs=[ANY] * 6,
        out_specs=(HBM, HBM),
        scratch_shapes=[brick, brick, sems(44)],
        compiler_params=granted(8),
        cost_estimate=pl.CostEstimate(flops=40_000_000, bytes_accessed=8_000_000, transcendentals=0),
        name="air_free",
    )(*staged, xlow, xhigh, ylow, yhigh)
    sums, *saved = pl.pallas_call(
        membrane_kernel,
        out_shape=(
            f32(1, 128), f32(48, COLS), f32(48, COLS), f32(96, COLS), f32(96, COLS), f32(24, COLS),
            f32(48, WINDOW), f32(96, WINDOW),
        ),
        in_specs=[WHOLE] * 5 + [ANY],
        out_specs=(WHOLE,) * 8,
        scratch_shapes=[
            VMEM((3 * XE, COLS), jnp.float32),
            VMEM((7 * XE, WINDOW), jnp.float32),
        ],
        compiler_params=granted(10),
        name="membrane",
    )(members, jumps, hlow, hhigh, listed, done)
    sums = sums + lax.ppermute(sums, "gx", across(GX, 0))
    shares = [sums] + [lax.ppermute(sums, "gx", across(GX, by)) for by in (1, 2, 3)]
    return pl.pallas_call(
        finish_kernel,
        out_shape=(air, air, f32(BX, BY), f32(BX, BY)),
        in_specs=[pl.BlockSpec(memory_space=pltpu.SMEM)] * 4 + [WHOLE] * 8 + [HBM, HBM],
        out_specs=(HBM, HBM, WHOLE, WHOLE),
        scratch_shapes=[
            VMEM((BX, BY, 256), jnp.float32),
            VMEM((BX, BY, 256), jnp.float32),
            VMEM((48, COLS), jnp.float32),
            VMEM((XE, WINDOW), jnp.float32),
            VMEM((128, 128), jnp.float32),
            sems(4),
        ],
        input_output_aliases={12: 0, 13: 1},
        compiler_params=granted(8),
        name="finish",
    )(*shares, listed, *saved, next_free, last_free)


def solution(mesh):
    in_specs = (
        P("gx", "gy", None),
        P("gx", "gy", None),
        P("gx", "gy"),
        P("gx", "gy"),
        P("gx", "gy"),
        P(),
    )
    out_specs = (P("gx", "gy", None), P("gx", "gy", None), P("gx", "gy"), P("gx", "gy"))
    return jax.shard_map(
        per_device, mesh=mesh, in_specs=in_specs, out_specs=out_specs, check_vma=False
    )
```
